32 devices in a mesh: section: 4 (over y, x), expert: 8 (over z, core).
Axes of the slice: x: 2, y: 2, z: 4, core: 2. Of those that a mesh axis runs over, the one named last changes fastest.
Arguments:
- embedded: bfloat16 [4, 128, 7168], P('section', 'expert'), may hold values from -6 to 6
- norm_gain: float32 [4, 7168], P('section'), may hold values from 0.1 to 1.9
- gate_proj: bfloat16 [4, 7168, 2048], P('section', None, 'expert'), may hold values from -0.0625 to 0.0625
- up_proj: bfloat16 [4, 7168, 2048], P('section', None, 'expert'), may hold values from -0.0625 to 0.0625
- down_proj: bfloat16 [4, 2048, 7168], P('section', 'expert'), may hold values from -0.125 to 0.125
- expert_ids: int32 [4, 4, 128, 8], P('section', None, 'expert'), may hold values from 0 to 255, all different within a row; in each aligned block of 16 rows (0 to 15, 16 to 31, ..., all dimensions but the last counted through in order) at most 2 rows name the same one
- route_gates: float32 [4, 4, 128, 8], P('section', None, 'expert'), may hold values from 0.2 to 2.5
Outputs:
- processed: bfloat16 [4, 128, 7168], P('section', 'expert')
The draws below stay inside these ranges and needn't reach their ends.
Inputs may be any that keep to these rules, and one draw needn't show every extreme that they name: `expert_ids`: each row names 8 different experts; within one layer and micro-batch no expert is named by more than 2 tokens of an aligned block of 16 tokens.
All inputs are finite; a program needn't handle non-finite values.
Results may differ from the reference program's by a relative error of at most 0.0085.
Values may be sent and summed in bfloat16 or wider, within the bound.
No kernel may reach another device: no remote copies, remote signals or barrier semaphores. Data moves between devices by JAX's collectives and lax.ppermute only.
A program may use at most 128 MiB of HBM per device.

```python
import math
import jax
import jax.numpy as jnp
import numpy as np
from jax import lax

D = 7168
ROUTED = 256
TOP = 8
HID_DEV = 256
CAP = 2
TOK_MB = 16
HIDDEN_SIZE = 2048
EXPERTS = 1
LAYERS = 4
MICRO = 4
TOKENS = 128
N_SECTION = 4
N_EXPERT = 8


def block_levels(rng, shape, shards, least, top_value):
    def one(position, shards_of):
        heights = jax.random.uniform(jax.random.fold_in(jax.random.fold_in(rng, 6), position), (shards_of,), jnp.float32, least / len(shards), top_value / len(shards))
        return jnp.repeat(jnp.exp(heights), shape[position] // shards_of).reshape((-1,) + (1,) * (len(shape) - position - 1))

    loudness = one(*shards[0])
    for cut in shards[1:]:
        loudness = loudness * one(*cut)
    return loudness


def shared_out(key, own, number, rows, amount, top, limit, skew):
    sequence = jax.random.permutation(key, amount)
    packed, common = load_shares(amount, rows * top, limit, skew, True), load_shares(amount, rows * top, limit, skew, False)
    places = jnp.arange(amount)

    def named(tallies, rotation):
        used = int((tallies > 0).sum())
        fixed = max(1, used // 4)
        moved = fixed + (places - fixed + rotation * (used - fixed)) % max(1, amount - fixed)
        return jnp.zeros((amount,), jnp.int32).at[sequence[jnp.where(places < fixed, places, moved)]].set(jnp.asarray(tallies, jnp.int32))

    tallies = jnp.where(number % 4 == 0, named(packed, number // 4), named(common, number - number // 4 - 1))
    mixed = jax.random.permutation(jax.random.fold_in(own, 3), amount)
    donor, receiver = mixed[0:amount // 2 * 2:2], mixed[1:amount // 2 * 2:2]
    slack = jnp.minimum(tallies[donor] - 1, limit - tallies[receiver]) // 2
    slack = jnp.where((donor == sequence[0]) | (receiver == sequence[0]) | (tallies[receiver] == 0), 0, jnp.maximum(slack, 0))
    moved = jax.random.randint(jax.random.fold_in(own, 4), (amount // 2,), 0, 1 << 20) % (slack + 1)
    tallies = tallies.at[donor].add(-moved).at[receiver].add(moved)
    members = jnp.searchsorted(jnp.cumsum(tallies), jnp.arange(rows * top), side="right").astype(jnp.int32)
    table = members.reshape(top, rows).T
    table = table[jax.random.permutation(jax.random.fold_in(own, 1), rows)]
    rotation = jax.random.randint(jax.random.fold_in(own, 2), (rows, 1), 0, top)
    return jnp.take_along_axis(table, (jnp.arange(top)[None, :] + rotation) % top, axis=1)


def load_shares(count, total, reach, skew, full):
    portions = [(1 << 20) // math.isqrt(standing ** skew) + 1 for standing in range(1, count + 1)]
    largest = reach if full else min(reach, max(-(-total // count), total * portions[0] // sum(portions)))
    least = 1 if total - largest >= count - 1 else 0
    given, spare = [largest] + [least] * (count - 1), total - largest - least * (count - 1)
    while spare > 0:
        movable = [i for i in range(1, count) if given[i] < largest] or [i for i in range(1, count) if given[i] < reach]
        pool, budget = sum([portions[i] for i in movable]), spare
        for i in movable:
            more = min(reach - given[i], max(1, budget * portions[i] // pool), spare)
            given[i] = given[i] + more
            spare = spare - more
    return np.array(given)


def normal_values(stream_key, dims, width, most, pieces=(), kind=jnp.bfloat16):
    entries = jax.random.normal(stream_key, dims, jnp.float32) * width
    if len(pieces) > 0:
        entries = block_levels(stream_key, dims, pieces, -0.22, 0.18) * entries
    return jnp.clip(entries, min=-most, max=most).astype(kind)


def setup_inputs(seed: int = 0) -> dict:
    key_list = jax.random.split(jax.random.key(seed), 8)
    embedded = normal_values(key_list[0], (MICRO, TOKENS, D), 1.0, 6.0, ((0, 4), (1, 8)))
    norm_gain = jnp.clip(1.0 + 0.18 * jax.random.normal(key_list[1], (LAYERS, D), jnp.float32), 0.1, 1.9)
    gate_proj = normal_values(key_list[2], (LAYERS, D, EXPERTS * HIDDEN_SIZE), D ** -0.5, 0.0625, ((0, 4), (2, 8)))
    up_proj = normal_values(key_list[3], (LAYERS, D, EXPERTS * HIDDEN_SIZE), D ** -0.5, 0.0625, ((0, 4), (2, 8)))
    down_proj = normal_values(key_list[4], (LAYERS, EXPERTS * HIDDEN_SIZE, D), HIDDEN_SIZE ** -0.5, 0.125, ((0, 4), (1, 8)))
    expert_ids_keys = jax.random.split(jax.random.fold_in(key_list[5], 1), LAYERS * MICRO * TOKENS // TOK_MB)
    expert_ids_turns = jax.random.permutation(jax.random.fold_in(key_list[5], 3), LAYERS * MICRO * TOKENS // TOK_MB)
    expert_ids = jax.vmap(lambda own, number: shared_out(jax.random.fold_in(key_list[5], 2), own, number, TOK_MB, ROUTED, TOP, CAP, 2))(expert_ids_keys, expert_ids_turns).reshape((LAYERS, MICRO, TOKENS, TOP))
    route_gates = jnp.clip(0.2 + 2.3 * jax.random.uniform(key_list[6], (LAYERS, MICRO, TOKENS, TOP), jnp.float32) ** block_levels(key_list[6], (LAYERS, MICRO, TOKENS, TOP), ((0, 4), (2, 8)), -0.2, 0.2), 0.2, 2.5)
    return {"embedded": embedded, "norm_gain": norm_gain, "gate_proj": gate_proj, "up_proj": up_proj, "down_proj": down_proj, "expert_ids": expert_ids, "route_gates": route_gates}


eps_norm = 1e-06

def slot_table(chosen, num_experts):
    expert_range = jnp.arange(num_experts, dtype=jnp.int32)
    matched = (chosen[..., None] == expert_range).astype(jnp.int32)
    hit_table = lax.optimization_barrier(jnp.sum(matched, axis=-2, dtype=jnp.int32))
    earlier = jnp.cumsum(hit_table, axis=-2, dtype=jnp.int32) - hit_table
    slot_index = lax.optimization_barrier(jnp.sum(matched * earlier[..., None, :], axis=-1, dtype=jnp.int32))
    inside = chosen < num_experts
    return (slot_index, inside)

def place_mask(chosen, slot_index, inside, num_experts):
    flat_index = chosen * CAP + slot_index
    target = jnp.arange(num_experts * CAP, dtype=jnp.int32)
    return (flat_index[..., None] == target) & inside[..., None]

def layer_apply(rows, gain_row, gate_mat, up_mat, down_mat, chosen, weights_k):
    group_size = min(8, N_EXPERT)
    num_experts = N_EXPERT // group_size
    width_hidden = group_size * HID_DEV
    rows_float = rows.astype(jnp.float32)
    scale = lax.rsqrt(lax.optimization_barrier(jnp.mean(rows_float * rows_float, axis=-1, keepdims=True)) + eps_norm)
    normed = (rows_float * scale * gain_row.astype(jnp.float32)).astype(jnp.bfloat16)
    blocks = chosen.reshape(N_EXPERT, TOK_MB, TOP)
    slot_index, inside = slot_table(blocks, num_experts)
    placed = place_mask(blocks, slot_index, inside, num_experts)
    mask_any = jnp.any(placed, axis=2).astype(jnp.float32)
    normed_blocks = normed.reshape(N_EXPERT, TOK_MB, D).astype(jnp.float32)
    dispatched = jnp.einsum('ntq,ntd->nqd', mask_any, normed_blocks, precision=lax.Precision.HIGHEST).astype(jnp.bfloat16)
    dispatched = dispatched.reshape(N_EXPERT, num_experts, CAP, D)
    outputs_list = []
    for expert_pos in range(num_experts):
        rows_in = dispatched[:, expert_pos].reshape(N_EXPERT * CAP, D)
        col_start = expert_pos * width_hidden
        gate_val = jnp.dot(rows_in, gate_mat[:, col_start:col_start + width_hidden], preferred_element_type=jnp.float32)
        up_val = jnp.dot(rows_in, up_mat[:, col_start:col_start + width_hidden], preferred_element_type=jnp.float32)
        hidden = (jax.nn.silu(gate_val) * up_val).astype(jnp.bfloat16)
        hidden_parts = hidden.reshape(N_EXPERT * CAP, group_size, HID_DEV).astype(jnp.float32)
        down_parts = down_mat[col_start:col_start + width_hidden].reshape(group_size, HID_DEV, D).astype(jnp.float32)
        partial_value = jnp.einsum('rgi,gid->grd', hidden_parts, down_parts, precision=lax.Precision.HIGHEST).astype(jnp.bfloat16)
        partial_value = lax.optimization_barrier(partial_value)
        summed = lax.optimization_barrier(jnp.sum(partial_value.astype(jnp.float32), axis=0))
        outputs_list.append(summed.reshape(N_EXPERT, CAP, D))
    expert_out = jnp.stack(outputs_list, axis=1).reshape(N_EXPERT, num_experts * CAP, D)
    gates_blocks = weights_k.reshape(N_EXPERT, TOK_MB, TOP)
    weight_table = lax.optimization_barrier(jnp.sum(jnp.where(placed, gates_blocks[..., None], 0.0), axis=2))
    routed_sum = jnp.einsum('ntq,nqd->ntd', weight_table, expert_out, precision=lax.Precision.HIGHEST)
    return (rows_float + routed_sum.reshape(N_EXPERT * TOK_MB, D)).astype(jnp.bfloat16)

def reference(embedded, norm_gain, gate_proj, up_proj, down_proj, expert_ids, route_gates):
    finished = []
    for micro_pos in range(N_SECTION):
        rows = embedded[micro_pos]
        for layer_pos in range(N_SECTION):
            rows = layer_apply(rows, norm_gain[layer_pos], gate_proj[layer_pos], up_proj[layer_pos], down_proj[layer_pos], expert_ids[layer_pos, micro_pos], route_gates[layer_pos, micro_pos])
        finished.append(rows)
    return jnp.stack(finished)
```

```python
import jax
import jax.numpy as jnp
from jax import lax
from jax.sharding import PartitionSpec as P

CAP = 2

eps_norm = 1e-06


def slot_weights(chosen, gates, num_experts):
    expert_range = jnp.arange(num_experts, dtype=jnp.int32)
    matched = (chosen[..., None] == expert_range).astype(jnp.int32)
    hit_table = jnp.sum(matched, axis=-2, dtype=jnp.int32)
    tokens = chosen.shape[-2]
    before = jnp.arange(tokens)[:, None] > jnp.arange(tokens)[None, :]
    earlier = jnp.sum(
        jnp.where(before[:, :, None], hit_table[..., None, :, :], 0), axis=-2, dtype=jnp.int32
    )
    weight = jnp.sum(jnp.where(matched > 0, gates[..., None], 0.0), axis=-2)
    slots = jnp.arange(CAP, dtype=jnp.int32)
    table = jnp.where(earlier[..., None] == slots, weight[..., None], 0.0)
    return table.reshape(table.shape[:-2] + (num_experts * CAP,))


def swap(array, axis, by):
    devices = lax.axis_size(axis)
    return lax.ppermute(array, axis, [(i, i ^ by) for i in range(devices)])


def section_exchange(parts):
    return [parts[0]] + [swap(parts[k], "section", k) for k in range(1, len(parts))]


def dispatch(rows):
    experts, count, width = rows.shape
    n_dev = lax.axis_size("expert")
    if n_dev == 8:
        own = rows[0]
        near = jnp.stack([own] + [swap(own, "expert", 2 * k) for k in range(1, 4)])
        return jnp.concatenate([near, swap(near, "expert", 1)])
    send = jnp.repeat(rows, n_dev // experts, axis=0)
    return lax.all_to_all(send, "expert", split_axis=0, concat_axis=0, tiled=True)


def collect(partial, experts):
    n_dev, count, width = partial.shape
    if n_dev == 8:
        other = swap(partial[4:], "expert", 1)
        both = (partial[:4].astype(jnp.float32) + other.astype(jnp.float32)).astype(jnp.bfloat16)
        got = [both[0]] + [swap(both[k], "expert", 2 * k) for k in range(1, 4)]
        return sum(g.astype(jnp.float32) for g in got)[None]
    back = lax.all_to_all(partial, "expert", split_axis=0, concat_axis=0, tiled=True)
    back = back.reshape(experts, n_dev // experts, count, width)
    return jnp.sum(back.astype(jnp.float32), axis=1)


def expert_block(rows_in, gate_mat, up_mat, down_mat):
    gate_val = jnp.dot(rows_in, gate_mat, preferred_element_type=jnp.float32)
    up_val = jnp.dot(rows_in, up_mat, preferred_element_type=jnp.float32)
    hidden = (jax.nn.silu(gate_val) * up_val).astype(jnp.bfloat16)
    return jnp.dot(hidden, down_mat, preferred_element_type=jnp.float32).astype(jnp.bfloat16)


def layer_round(sent, gain_row, gate_mat, up_mat, down_mat, num_experts):
    width = sent[0].shape[-1]
    here = jnp.stack(section_exchange(sent))
    rows_float = here.astype(jnp.float32)
    scale = lax.rsqrt(jnp.mean(rows_float * rows_float, axis=-1, keepdims=True) + eps_norm)
    normed = (rows_float * scale * gain_row).astype(jnp.bfloat16)
    micros = here.shape[0]
    normed = normed.reshape(micros, num_experts, CAP, width).transpose(1, 0, 2, 3)
    received = dispatch(normed.reshape(num_experts, micros * CAP, width))
    n_dev = received.shape[0]
    partial = expert_block(received.reshape(-1, width), gate_mat, up_mat, down_mat)
    total = collect(partial.reshape(n_dev, micros * CAP, width), num_experts)
    total = total.astype(jnp.bfloat16).reshape(num_experts, micros, CAP, width)
    total = total.transpose(1, 0, 2, 3).reshape(micros, num_experts * CAP, width)
    return section_exchange([total[k] for k in range(micros)])


def shards(embedded, norm_gain, gate_proj, up_proj, down_proj, expert_ids, route_gates):
    n_section = lax.axis_size("section")
    n_dev = lax.axis_size("expert")
    num_experts = n_dev // min(8, n_dev)
    me = lax.axis_index("section")
    base = embedded[0]
    own = slot_weights(expert_ids[0], route_gates[0], num_experts)

    def pick(stacked, index):
        return lax.dynamic_index_in_dim(stacked, index, 0, keepdims=False)

    tables = section_exchange([pick(own, me ^ k) for k in range(n_section)])
    tables = jnp.stack(tables)
    ordered = jnp.stack([pick(tables, me ^ l) for l in range(n_section)])
    chosen = ordered > 0
    picks = jnp.sum(jnp.any(chosen, axis=-1).astype(jnp.int32), axis=0)
    depth = lax.pmax(jnp.max(picks), ("section", "expert"))
    masks = chosen.astype(jnp.bfloat16)

    def take(mask, rows):
        return lax.dot_general(
            mask, rows, (((0,), (0,)), ((), ())), preferred_element_type=jnp.float32
        ).astype(jnp.bfloat16)

    def advance(rows, layer, update):
        routed = jnp.dot(
            ordered[layer],
            update.astype(jnp.float32),
            precision=lax.Precision.HIGHEST,
            preferred_element_type=jnp.float32,
        )
        return (rows.astype(jnp.float32) + routed).astype(jnp.bfloat16)

    def one_round(inputs):
        sent = [pick(inputs, me ^ k) for k in range(n_section)]
        got = jnp.stack(
            layer_round(sent, norm_gain[0], gate_proj[0], up_proj[0], down_proj[0], num_experts)
        )
        return jnp.stack([pick(got, me ^ l) for l in range(n_section)])

    def body(state):
        count, updates = state
        rows, inputs = base, []
        for layer in range(n_section):
            inputs.append(take(masks[layer], rows))
            if layer < n_section - 1:
                rows = advance(rows, layer, updates[layer])
        return count + 1, one_round(jnp.stack(inputs))

    first = jnp.stack([take(masks[layer], base) for layer in range(n_section)])
    updates = one_round(first)
    _, updates = lax.while_loop(lambda s: s[0] < depth, body, (jnp.int32(1), updates))
    rows = base
    for layer in range(n_section):
        rows = advance(rows, layer, updates[layer])
    return rows[None]


def solution(mesh):
    placed = (
        P("section", "expert", None),
        P("section", None),
        P("section", None, "expert"),
        P("section", None, "expert"),
        P("section", "expert", None),
        P("section", None, "expert", None),
        P("section", None, "expert", None),
    )
    return jax.shard_map(
        shards, mesh=mesh, in_specs=placed, out_specs=P("section", "expert", None), check_vma=False
    )
```

```python
import functools

import jax
import jax.numpy as jnp
from jax import lax
from jax.experimental import pallas as pl
from jax.experimental.pallas import tpu as pltpu
from jax.sharding import PartitionSpec as P

CAP = 2

eps_norm = 1e-06


def slot_weights(chosen, gates, num_experts):
    expert_range = jnp.arange(num_experts, dtype=jnp.int32)
    matched = (chosen[..., None] == expert_range).astype(jnp.int32)
    hit_table = jnp.sum(matched, axis=-2, dtype=jnp.int32)
    tokens = chosen.shape[-2]
    before = jnp.arange(tokens)[:, None] > jnp.arange(tokens)[None, :]
    earlier = jnp.sum(
        jnp.where(before[:, :, None], hit_table[..., None, :, :], 0), axis=-2, dtype=jnp.int32
    )
    weight = jnp.sum(jnp.where(matched > 0, gates[..., None], 0.0), axis=-2)
    slots = jnp.arange(CAP, dtype=jnp.int32)
    table = jnp.where(earlier[..., None] == slots, weight[..., None], 0.0)
    return table.reshape(table.shape[:-2] + (num_experts * CAP,))


def swap(array, axis, by):
    devices = lax.axis_size(axis)
    return lax.ppermute(array, axis, [(i, i ^ by) for i in range(devices)])


def section_exchange(parts):
    return [parts[0]] + [swap(parts[k], "section", k) for k in range(1, len(parts))]


def dispatch(rows):
    experts, count, width = rows.shape
    n_dev = lax.axis_size("expert")
    send = jnp.repeat(rows, n_dev // experts, axis=0)
    return lax.all_to_all(send, "expert", split_axis=0, concat_axis=0, tiled=True)


def collect(partial, experts):
    n_dev, count, width = partial.shape
    back = lax.all_to_all(partial, "expert", split_axis=0, concat_axis=0, tiled=True)
    back = back.reshape(experts, n_dev // experts, count, width)
    return jnp.sum(back.astype(jnp.float32), axis=1)


def expert_block(rows_in, gate_mat, up_mat, down_mat):
    gate_val = jnp.dot(rows_in, gate_mat, preferred_element_type=jnp.float32)
    up_val = jnp.dot(rows_in, up_mat, preferred_element_type=jnp.float32)
    hidden = (jax.nn.silu(gate_val) * up_val).astype(jnp.bfloat16)
    return jnp.dot(hidden, down_mat, preferred_element_type=jnp.float32).astype(jnp.bfloat16)


def layer_round(sent, gain_row, gate_mat, up_mat, down_mat, num_experts):
    width = sent[0].shape[-1]
    here = jnp.stack(section_exchange(sent))
    rows_float = here.astype(jnp.float32)
    scale = lax.rsqrt(jnp.mean(rows_float * rows_float, axis=-1, keepdims=True) + eps_norm)
    normed = (rows_float * scale * gain_row).astype(jnp.bfloat16)
    micros = here.shape[0]
    normed = normed.reshape(micros, num_experts, CAP, width).transpose(1, 0, 2, 3)
    received = dispatch(normed.reshape(num_experts, micros * CAP, width))
    n_dev = received.shape[0]
    partial = expert_block(received.reshape(-1, width), gate_mat, up_mat, down_mat)
    total = collect(partial.reshape(n_dev, micros * CAP, width), num_experts)
    total = total.astype(jnp.bfloat16).reshape(num_experts, micros, CAP, width)
    total = total.transpose(1, 0, 2, 3).reshape(micros, num_experts * CAP, width)
    return section_exchange([total[k] for k in range(micros)])


def shards_general(embedded, norm_gain, gate_proj, up_proj, down_proj, expert_ids, route_gates):
    n_section = lax.axis_size("section")
    n_dev = lax.axis_size("expert")
    num_experts = n_dev // min(8, n_dev)
    me = lax.axis_index("section")
    base = embedded[0]
    own = slot_weights(expert_ids[0], route_gates[0], num_experts)

    def pick(stacked, index):
        return lax.dynamic_index_in_dim(stacked, index, 0, keepdims=False)

    tables = section_exchange([pick(own, me ^ k) for k in range(n_section)])
    tables = jnp.stack(tables)
    ordered = jnp.stack([pick(tables, me ^ l) for l in range(n_section)])
    chosen = ordered > 0
    picks = jnp.sum(jnp.any(chosen, axis=-1).astype(jnp.int32), axis=0)
    depth = lax.pmax(jnp.max(picks), ("section", "expert"))
    masks = chosen.astype(jnp.bfloat16)

    def take(mask, rows):
        return lax.dot_general(
            mask, rows, (((0,), (0,)), ((), ())), preferred_element_type=jnp.float32
        ).astype(jnp.bfloat16)

    def advance(rows, layer, update):
        routed = jnp.dot(
            ordered[layer],
            update.astype(jnp.float32),
            precision=lax.Precision.HIGHEST,
            preferred_element_type=jnp.float32,
        )
        return (rows.astype(jnp.float32) + routed).astype(jnp.bfloat16)

    def one_round(inputs):
        sent = [pick(inputs, me ^ k) for k in range(n_section)]
        got = jnp.stack(
            layer_round(sent, norm_gain[0], gate_proj[0], up_proj[0], down_proj[0], num_experts)
        )
        return jnp.stack([pick(got, me ^ l) for l in range(n_section)])

    def body(state):
        count, updates = state
        rows, inputs = base, []
        for layer in range(n_section):
            inputs.append(take(masks[layer], rows))
            if layer < n_section - 1:
                rows = advance(rows, layer, updates[layer])
        return count + 1, one_round(jnp.stack(inputs))

    first = jnp.stack([take(masks[layer], base) for layer in range(n_section)])
    updates = one_round(first)
    _, updates = lax.while_loop(lambda s: s[0] < depth, body, (jnp.int32(1), updates))
    rows = base
    for layer in range(n_section):
        rows = advance(rows, layer, updates[layer])
    return rows[None]


LANES = 128
BF16 = jnp.bfloat16
F32 = jnp.float32


def prepare_first(width, picks, x0, x1, x2, x3, gain, rows_out, normed_out):
    messages = (x0, x1, x2, x3)
    rows = sum(
        jnp.dot(picks[j], messages[j][:, :width], preferred_element_type=F32) for j in range(4)
    )
    rows_out[...] = rows.astype(BF16)
    mean = jnp.mean(rows * rows, axis=-1, keepdims=True)
    normed_out[:, :width] = (rows * lax.rsqrt(mean + eps_norm) * gain[...]).astype(BF16)
    lane = lax.broadcasted_iota(jnp.int32, (x0.shape[0], LANES), 1)
    slots = 4 * CAP
    count = sum(jnp.where(m[:, width:].astype(F32) > 0, 1.0, 0.0) for m in messages)
    count = jnp.where(lane < slots, count, 0.0)
    pair = jnp.where(lane % CAP == 0, count + pltpu.roll(count, LANES - 1, 1), 0.0)
    deepest = jnp.max(jnp.max(pair, axis=1, keepdims=True), axis=0, keepdims=True)
    normed_out[:, width:] = jnp.broadcast_to(deepest, (rows.shape[0], LANES)).astype(BF16)


def prepare_next(place, coef, base, updates, gain, normed_out):
    rows = base[...].astype(F32)
    count = rows.shape[0]
    for layer in range(coef.shape[0]):
        step = updates[place[0] ^ layer].astype(F32)
        change = (
            coef[layer, 0] * step
            + coef[layer, 1] * pltpu.roll(step, count - 1, 0)
            + coef[layer, 2] * pltpu.roll(step, 1, 0)
        )
        rows = (rows + change).astype(BF16).astype(F32)
    mean = jnp.mean(rows * rows, axis=-1, keepdims=True)
    normed_out[...] = (rows * lax.rsqrt(mean + eps_norm) * gain[...]).astype(BF16)


def finish(place, weights, base, updates, out):
    rows = base[0].astype(F32)
    for layer in range(weights.shape[0]):
        step = updates[place[0] ^ layer].astype(F32)
        change = sum(weights[layer, q] * step[q : q + 1] for q in range(step.shape[0]))
        rows = (rows + change).astype(BF16).astype(F32)
    out[0] = rows.astype(BF16)


CHUNKS = 7


def expert_kernel(near, far, gate, up, down, near_out, far_out, rows, gates, ups, downs, sems):
    half, width = near_out.shape
    part = width // CHUNKS
    copies = []
    for c in range(CHUNKS):
        span = pl.ds(c * part, part)
        copies.append(pltpu.make_async_copy(gate.at[0, span], gates.at[span], sems.at[0, c]))
        copies.append(pltpu.make_async_copy(up.at[0, span], ups.at[span], sems.at[1, c]))
    for c in range(CHUNKS):
        span = pl.ds(c * part, part)
        copies.append(
            pltpu.make_async_copy(down.at[0, :, span], downs.at[:, span], sems.at[2, c])
        )
    for copy in copies:
        copy.start()
    rows[:half] = near[:, :width]
    rows[half:] = far[:, :width]
    gate_val = up_val = 0.0
    for c in range(CHUNKS):
        span = pl.ds(c * part, part)
        piece = rows[:, span]
        copies[2 * c].wait()
        gate_val += jnp.dot(piece, gates[span], preferred_element_type=F32)
        copies[2 * c + 1].wait()
        up_val += jnp.dot(piece, ups[span], preferred_element_type=F32)
    hidden = (gate_val * jax.nn.sigmoid(gate_val) * up_val).astype(BF16)
    for c in range(CHUNKS):
        span = pl.ds(c * part, part)
        copies[2 * CHUNKS + c].wait()
        value = jnp.dot(hidden, downs[:, span], preferred_element_type=F32).astype(BF16)
        near_out[:, span] = value[:half]
        far_out[:, span] = value[half:]


VMEM = pl.BlockSpec(memory_space=pltpu.VMEM)
SMEM = pl.BlockSpec(memory_space=pltpu.SMEM)
HBM = pl.BlockSpec(memory_space=pl.ANY)


def expert_call(near, far, gate, up, down):
    half = near.shape[0]
    _, width, hidden = gate.shape
    out = jax.ShapeDtypeStruct((half, width), BF16)
    return pl.pallas_call(
        expert_kernel,
        out_shape=(out, out),
        in_specs=[VMEM, VMEM, HBM, HBM, HBM],
        out_specs=(VMEM, VMEM),
        scratch_shapes=[
            pltpu.VMEM((2 * half, width), BF16),
            pltpu.VMEM((width, hidden), BF16),
            pltpu.VMEM((width, hidden), BF16),
            pltpu.VMEM((hidden, width), BF16),
            pltpu.SemaphoreType.DMA((3, CHUNKS)),
        ],
        compiler_params=pltpu.CompilerParams(vmem_limit_bytes=32 * 2**20),
        cost_estimate=pl.CostEstimate(
            flops=12 * half * width * hidden,
            bytes_accessed=6 * width * hidden,
            transcendentals=2 * half * hidden,
        ),
        name="experts",
    )(near, far, gate, up, down)


def spread(array):
    return [array] + [swap(array, "section", j) for j in range(1, 4)]


def group_rows(normed):
    near = jnp.concatenate([normed] + [swap(normed, "expert", 2 * k) for k in range(1, 4)])
    return near, swap(near, "expert", 1)


def group_sum(near, far, count):
    other = swap(far, "expert", 1)
    both = (near.astype(F32) + other.astype(F32)).astype(BF16)
    parts = [both[k * count : (k + 1) * count] for k in range(4)]
    got = [parts[0]] + [swap(parts[k], "expert", 2 * k) for k in range(1, 4)]
    return sum(g.astype(F32) for g in got).astype(BF16)


def shards_group(embedded, norm_gain, gate_proj, up_proj, down_proj, expert_ids, route_gates):
    me = lax.axis_index("section")
    place = me.astype(jnp.int32)[None]
    tokens, width = embedded.shape[1:]
    micros = expert_ids.shape[1]
    count = micros * CAP
    own = slot_weights(expert_ids[0], route_gates[0], 1)
    flat = own.transpose(1, 0, 2).reshape(tokens, count)
    high = lax.reduce_precision(flat, 8, 7)
    middle = lax.reduce_precision(flat - high, 8, 7)
    parts = jnp.concatenate([high, middle, flat - high - middle], axis=1).astype(BF16)
    parts = jnp.pad(parts, ((0, 0), (0, LANES - 3 * count)))
    messages = spread(jnp.concatenate([embedded[0], parts], axis=1))

    chosen = (own > 0).astype(BF16)
    spot = jnp.eye(micros, dtype=BF16)
    selector = spot[:, :, None, None] * chosen.transpose(0, 2, 1)[:, None]
    selector = selector.reshape(micros, count, tokens)
    picks = jnp.stack(
        [lax.dynamic_index_in_dim(selector, me ^ j, 0, keepdims=False) for j in range(4)]
    )
    rows, normed = pl.pallas_call(
        functools.partial(prepare_first, width),
        out_shape=(
            jax.ShapeDtypeStruct((count, width), BF16),
            jax.ShapeDtypeStruct((count, width + LANES), BF16),
        ),
        in_specs=[VMEM] * 6,
        out_specs=(VMEM, VMEM),
        compiler_params=pltpu.CompilerParams(vmem_limit_bytes=32 * 2**20),
        name="prepare_first",
    )(picks, *messages, norm_gain)

    def rest(normed):
        near, far = group_rows(normed)
        near_part, far_part = expert_call(near, far, gate_proj, up_proj, down_proj)
        update = group_sum(near_part, far_part, count)
        return near, far, jnp.stack(spread(update))

    near, far, updates = rest(normed)
    depth = jnp.maximum(jnp.max(near[:, width:]), jnp.max(far[:, width:])).astype(jnp.int32)

    tables = jnp.stack([m[:, width : width + 3 * count] for m in messages]).astype(F32)
    tables = tables.reshape(4, tokens, 3, micros, CAP)
    tables = (tables[:, :, 0] + tables[:, :, 1] + tables[:, :, 2]).transpose(0, 2, 1, 3)
    tables = jnp.stack(
        [lax.dynamic_index_in_dim(tables, me ^ l, 0, keepdims=False) for l in range(4)]
    )
    cross = jnp.sum(
        (own > 0).astype(F32)[None, :, :, :, None] * tables[:, :, :, None, :], axis=2
    )
    cross = jnp.where(jnp.arange(4)[:, None, None, None] < me, cross, 0.0)[:3]
    same = jnp.stack([cross[:, :, 0, 0], cross[:, :, 1, 1]], axis=-1)
    nothing = jnp.zeros_like(same[..., 0])
    after = jnp.stack([cross[:, :, 0, 1], nothing], axis=-1)
    before = jnp.stack([nothing, cross[:, :, 1, 0]], axis=-1)
    coef = jnp.stack([same, after, before], axis=1).reshape(3, 3, count, 1)

    def body(state):
        done, updates = state
        normed = pl.pallas_call(
            prepare_next,
            out_shape=jax.ShapeDtypeStruct((count, width), BF16),
            in_specs=[SMEM] + [VMEM] * 4,
            out_specs=VMEM,
            compiler_params=pltpu.CompilerParams(vmem_limit_bytes=32 * 2**20),
            name="prepare_next",
        )(place, coef, rows, updates, norm_gain)
        return done + 1, rest(normed)[2]

    _, updates = lax.while_loop(lambda s: s[0] < depth, body, (jnp.int32(1), updates))
    mine = lax.dynamic_index_in_dim(tables, me, 1, keepdims=False)
    weights = (
        (jnp.arange(micros) == me).astype(F32)[None, :, None, None]
        * mine.transpose(0, 2, 1)[:, None]
    ).reshape(4, count, tokens, 1)
    return pl.pallas_call(
        finish,
        out_shape=jax.ShapeDtypeStruct(embedded.shape, BF16),
        in_specs=[SMEM] + [VMEM] * 3,
        out_specs=VMEM,
        compiler_params=pltpu.CompilerParams(vmem_limit_bytes=32 * 2**20),
        name="finish",
    )(place, weights, embedded, updates)


def solution(mesh):
    placed = (
        P("section", "expert", None),
        P("section", None),
        P("section", None, "expert"),
        P("section", None, "expert"),
        P("section", "expert", None),
        P("section", None, "expert", None),
        P("section", None, "expert", None),
    )
    fits = mesh.shape["expert"] == 8 and mesh.shape["section"] == 4
    return jax.shard_map(
        shards_group if fits else shards_general, mesh=mesh, in_specs=placed, out_specs=P("section", "expert", None), check_vma=False
    )
```

```python
import jax
import jax.numpy as jnp
from jax import lax
from jax.experimental import pallas as pl
from jax.experimental.pallas import tpu as pltpu
from jax.sharding import PartitionSpec as P

CAP = 2

eps_norm = 1e-06


def slot_weights(chosen, gates, num_experts):
    expert_range = jnp.arange(num_experts, dtype=jnp.int32)
    matched = (chosen[..., None] == expert_range).astype(jnp.int32)
    hit_table = jnp.sum(matched, axis=-2, dtype=jnp.int32)
    tokens = chosen.shape[-2]
    before = jnp.arange(tokens)[:, None] > jnp.arange(tokens)[None, :]
    earlier = jnp.sum(
        jnp.where(before[:, :, None], hit_table[..., None, :, :], 0), axis=-2, dtype=jnp.int32
    )
    weight = jnp.sum(jnp.where(matched > 0, gates[..., None], 0.0), axis=-2)
    slots = jnp.arange(CAP, dtype=jnp.int32)
    table = jnp.where(earlier[..., None] == slots, weight[..., None], 0.0)
    return table.reshape(table.shape[:-2] + (num_experts * CAP,))


def swap(array, axis, by):
    devices = lax.axis_size(axis)
    return lax.ppermute(array, axis, [(i, i ^ by) for i in range(devices)])


def section_exchange(parts):
    return [parts[0]] + [swap(parts[k], "section", k) for k in range(1, len(parts))]


def dispatch(rows):
    experts, count, width = rows.shape
    n_dev = lax.axis_size("expert")
    send = jnp.repeat(rows, n_dev // experts, axis=0)
    return lax.all_to_all(send, "expert", split_axis=0, concat_axis=0, tiled=True)


def collect(partial, experts):
    n_dev, count, width = partial.shape
    back = lax.all_to_all(partial, "expert", split_axis=0, concat_axis=0, tiled=True)
    back = back.reshape(experts, n_dev // experts, count, width)
    return jnp.sum(back.astype(jnp.float32), axis=1)


def expert_block(rows_in, gate_mat, up_mat, down_mat):
    gate_val = jnp.dot(rows_in, gate_mat, preferred_element_type=jnp.float32)
    up_val = jnp.dot(rows_in, up_mat, preferred_element_type=jnp.float32)
    hidden = (jax.nn.silu(gate_val) * up_val).astype(jnp.bfloat16)
    return jnp.dot(hidden, down_mat, preferred_element_type=jnp.float32).astype(jnp.bfloat16)


def layer_round(sent, gain_row, gate_mat, up_mat, down_mat, num_experts):
    width = sent[0].shape[-1]
    here = jnp.stack(section_exchange(sent))
    rows_float = here.astype(jnp.float32)
    scale = lax.rsqrt(jnp.mean(rows_float * rows_float, axis=-1, keepdims=True) + eps_norm)
    normed = (rows_float * scale * gain_row).astype(jnp.bfloat16)
    micros = here.shape[0]
    normed = normed.reshape(micros, num_experts, CAP, width).transpose(1, 0, 2, 3)
    received = dispatch(normed.reshape(num_experts, micros * CAP, width))
    n_dev = received.shape[0]
    partial = expert_block(received.reshape(-1, width), gate_mat, up_mat, down_mat)
    total = collect(partial.reshape(n_dev, micros * CAP, width), num_experts)
    total = total.astype(jnp.bfloat16).reshape(num_experts, micros, CAP, width)
    total = total.transpose(1, 0, 2, 3).reshape(micros, num_experts * CAP, width)
    return section_exchange([total[k] for k in range(micros)])


def shards_general(embedded, norm_gain, gate_proj, up_proj, down_proj, expert_ids, route_gates):
    n_section = lax.axis_size("section")
    n_dev = lax.axis_size("expert")
    num_experts = n_dev // min(8, n_dev)
    me = lax.axis_index("section")
    base = embedded[0]
    own = slot_weights(expert_ids[0], route_gates[0], num_experts)

    def pick(stacked, index):
        return lax.dynamic_index_in_dim(stacked, index, 0, keepdims=False)

    tables = section_exchange([pick(own, me ^ k) for k in range(n_section)])
    tables = jnp.stack(tables)
    ordered = jnp.stack([pick(tables, me ^ l) for l in range(n_section)])
    chosen = ordered > 0
    picks = jnp.sum(jnp.any(chosen, axis=-1).astype(jnp.int32), axis=0)
    depth = lax.pmax(jnp.max(picks), ("section", "expert"))
    masks = chosen.astype(jnp.bfloat16)

    def take(mask, rows):
        return lax.dot_general(
            mask, rows, (((0,), (0,)), ((), ())), preferred_element_type=jnp.float32
        ).astype(jnp.bfloat16)

    def advance(rows, layer, update):
        routed = jnp.dot(
            ordered[layer],
            update.astype(jnp.float32),
            precision=lax.Precision.HIGHEST,
            preferred_element_type=jnp.float32,
        )
        return (rows.astype(jnp.float32) + routed).astype(jnp.bfloat16)

    def one_round(inputs):
        sent = [pick(inputs, me ^ k) for k in range(n_section)]
        got = jnp.stack(
            layer_round(sent, norm_gain[0], gate_proj[0], up_proj[0], down_proj[0], num_experts)
        )
        return jnp.stack([pick(got, me ^ l) for l in range(n_section)])

    def body(state):
        count, updates = state
        rows, inputs = base, []
        for layer in range(n_section):
            inputs.append(take(masks[layer], rows))
            if layer < n_section - 1:
                rows = advance(rows, layer, updates[layer])
        return count + 1, one_round(jnp.stack(inputs))

    first = jnp.stack([take(masks[layer], base) for layer in range(n_section)])
    updates = one_round(first)
    _, updates = lax.while_loop(lambda s: s[0] < depth, body, (jnp.int32(1), updates))
    rows = base
    for layer in range(n_section):
        rows = advance(rows, layer, updates[layer])
    return rows[None]


LANES = 128
SECTIONS = 4
PACK = 4
BF16 = jnp.bfloat16
F32 = jnp.float32


def normalise(rows, gain):
    mean = jnp.mean(rows * rows, axis=-1, keepdims=True)
    return (rows * lax.rsqrt(mean + eps_norm) * gain).astype(BF16)


def before(values):
    total = values
    for by in (1, 2, 4):
        total = total + pltpu.roll(total, by, 1)
    return total - values


def prepare_first(place, picks, x0, x1, x2, x3, gain, rows_out, normed_out, group_out, rank_out):
    messages = (x0, x1, x2, x3)
    slots, width = rows_out.shape
    rows = sum(
        jnp.dot(picks[j], messages[j][:, :width], preferred_element_type=F32)
        for j in range(SECTIONS)
    )
    rows_out[...] = rows[:slots].astype(BF16)
    normed_out[:, :width] = normalise(rows[slots : slots + PACK], gain[...])

    lane = lax.broadcasted_iota(jnp.int32, (x0.shape[0], LANES), 1)
    hits = [
        jnp.where((lane < slots) & (m[:, width:].astype(F32) > 0), 1.0, 0.0) for m in messages
    ]
    pairs = [
        h + jnp.where(lane % CAP == 0, pltpu.roll(h, LANES - 1, 1), pltpu.roll(h, 1, 1))
        for h in hits
    ]
    largest = [jnp.zeros((1, 1), F32) for _ in range(SECTIONS)]
    for j in range(SECTIONS):
        mine = place[0] ^ j
        level = jnp.zeros_like(hits[0])
        for other in range(SECTIONS):
            if other != j:
                level += pairs[other] * jnp.where((place[0] ^ other) < mine, 1.0, 0.0)
        filled = jnp.sum(hits[j], axis=0, keepdims=True)
        level = jnp.sum(hits[j] * level, axis=0, keepdims=True)
        order = before(filled)
        late = jnp.where((level == 0) & (order >= PACK), filled, 0.0)
        group = jnp.where(filled > 0, jnp.where(level > 0, level, late - 1.0), -2.0)
        rank = order
        for g in range(SECTIONS):
            member = jnp.where(group == g, 1.0, 0.0)
            rank = jnp.where(group == g, before(member), rank)
            size = jnp.sum(member, axis=1, keepdims=True)
            largest[g] = jnp.maximum(largest[g], size)
        group_out[pl.ds(j, 1)] = group
        rank_out[pl.ds(j, 1)] = rank
    sizes = jnp.zeros((PACK, LANES), F32)
    spot = lax.broadcasted_iota(jnp.int32, (PACK, LANES), 1)
    for g in range(SECTIONS):
        sizes = jnp.where(spot == g, largest[g], sizes)
    normed_out[:, width:] = sizes.astype(BF16)


STRIP = 1024


def arrived(turn, code, blocks, linear, updates, held):
    for j, update in enumerate(updates):
        held[pl.ds(j * PACK, PACK)] = update[...].astype(F32)
    spot = lax.broadcasted_iota(jnp.int32, blocks.shape[1:], 1)
    match = code[...] == turn * PACK + spot % PACK
    coefs = []
    for part in range(3):
        chosen = jnp.where(match, blocks[part].astype(F32), 0.0).astype(BF16)
        coefs.append(jnp.dot(linear[...], chosen, preferred_element_type=F32).astype(BF16))
    return coefs


def absorb(turn, code, line, blocks, linear, x, y, u0, u1, u2, u3, gain, x_out, y_out, normed_out, held, kept):
    coefs = arrived(turn[0] - 1, code, blocks, linear, (u0, u1, u2, u3), held)
    tokens, width = x.shape
    slots = y.shape[0]
    for start in range(0, width, STRIP):
        span = pl.ds(start, STRIP)
        piece = held[:, span].astype(BF16)
        change = sum(jnp.dot(c, piece, preferred_element_type=F32) for c in coefs)
        x_out[:, span] = (x[:, span].astype(F32) + change[:tokens]).astype(BF16)
        rows = (y[:, span].astype(F32) + change[tokens : tokens + slots]).astype(BF16)
        y_out[:, span] = rows
        kept[:, span] = rows
    spot = lax.broadcasted_iota(jnp.int32, (2 * PACK, slots), 0)
    pick = jnp.where(line[...] == turn[0] * PACK + spot, 1.0, 0.0)
    pick = jnp.where(spot < PACK, pick, 0.0).astype(BF16)
    packed = jnp.dot(pick, kept[...], preferred_element_type=F32)
    normed_out[...] = normalise(packed[:PACK], gain[...])


def finish(turn, code, blocks, linear, x, u0, u1, u2, u3, out, held):
    coefs = arrived(turn[0] - 1, code, blocks, linear, (u0, u1, u2, u3), held)
    tokens, width = x.shape
    for start in range(0, width, STRIP):
        span = pl.ds(start, STRIP)
        piece = held[:, span].astype(BF16)
        change = sum(jnp.dot(c, piece, preferred_element_type=F32) for c in coefs)
        out[0, :, span] = (x[:, span].astype(F32) + change[:tokens]).astype(BF16)


CHUNKS = 7


def expert_kernel(near, far, gate, up, down, near_out, far_out, rows, gates, ups, downs, sems):
    half, width = near_out.shape
    part = width // CHUNKS
    copies = []
    for c in range(CHUNKS):
        span = pl.ds(c * part, part)
        copies.append(pltpu.make_async_copy(gate.at[0, span], gates.at[span], sems.at[0, c]))
        copies.append(pltpu.make_async_copy(up.at[0, span], ups.at[span], sems.at[1, c]))
    for c in range(CHUNKS):
        span = pl.ds(c * part, part)
        copies.append(
            pltpu.make_async_copy(down.at[0, :, span], downs.at[:, span], sems.at[2, c])
        )
    for copy in copies:
        copy.start()
    rows[:half] = near[:, :width]
    rows[half:] = far[:, :width]
    gate_val = up_val = 0.0
    for c in range(CHUNKS):
        span = pl.ds(c * part, part)
        piece = rows[:, span]
        copies[2 * c].wait()
        gate_val += jnp.dot(piece, gates[span], preferred_element_type=F32)
        copies[2 * c + 1].wait()
        up_val += jnp.dot(piece, ups[span], preferred_element_type=F32)
    hidden = (gate_val * jax.nn.sigmoid(gate_val) * up_val).astype(BF16)
    for c in range(CHUNKS):
        span = pl.ds(c * part, part)
        copies[2 * CHUNKS + c].wait()
        value = jnp.dot(hidden, downs[:, span], preferred_element_type=F32).astype(BF16)
        near_out[:, span] = value[:half]
        far_out[:, span] = value[half:]


VMEM = pl.BlockSpec(memory_space=pltpu.VMEM)
SMEM = pl.BlockSpec(memory_space=pltpu.SMEM)
HBM = pl.BlockSpec(memory_space=pl.ANY)


def expert_call(near, far, gate, up, down):
    half = near.shape[0]
    _, width, hidden = gate.shape
    out = jax.ShapeDtypeStruct((half, width), BF16)
    return pl.pallas_call(
        expert_kernel,
        out_shape=(out, out),
        in_specs=[VMEM, VMEM, HBM, HBM, HBM],
        out_specs=(VMEM, VMEM),
        scratch_shapes=[
            pltpu.VMEM((2 * half, width), BF16),
            pltpu.VMEM((width, hidden), BF16),
            pltpu.VMEM((width, hidden), BF16),
            pltpu.VMEM((hidden, width), BF16),
            pltpu.SemaphoreType.DMA((3, CHUNKS)),
        ],
        compiler_params=pltpu.CompilerParams(vmem_limit_bytes=32 * 2**20),
        cost_estimate=pl.CostEstimate(
            flops=12 * half * width * hidden,
            bytes_accessed=6 * width * hidden,
            transcendentals=2 * half * hidden,
        ),
        name="experts",
    )(near, far, gate, up, down)


def spread(array):
    return [array] + [swap(array, "section", j) for j in range(1, 4)]


def group_rows(normed):
    near = jnp.concatenate([normed] + [swap(normed, "expert", 2 * k) for k in range(1, 4)])
    return near, swap(near, "expert", 1)


def group_sum(near, far, count):
    other = swap(far, "expert", 1)
    both = (near.astype(F32) + other.astype(F32)).astype(BF16)
    parts = [both[k * count : (k + 1) * count] for k in range(4)]
    got = [parts[0]] + [swap(parts[k], "expert", 2 * k) for k in range(1, 4)]
    return sum(g.astype(F32) for g in got).astype(BF16)


PARAMS = pltpu.CompilerParams(vmem_limit_bytes=32 * 2**20)


def shards_group(embedded, norm_gain, gate_proj, up_proj, down_proj, expert_ids, route_gates):
    me = lax.axis_index("section")
    place = me.astype(jnp.int32)[None]
    tokens, width = embedded.shape[1:]
    micros = expert_ids.shape[1]
    slots = micros * CAP
    own = slot_weights(expert_ids[0], route_gates[0], 1)
    flat = own.transpose(1, 0, 2).reshape(tokens, slots)
    high = lax.reduce_precision(flat, 8, 7)
    middle = lax.reduce_precision(flat - high, 8, 7)
    parts = jnp.concatenate([high, middle, flat - high - middle], axis=1).astype(BF16)
    parts = jnp.pad(parts, ((0, 0), (0, LANES - 3 * slots)))
    messages = spread(jnp.concatenate([embedded[0], parts], axis=1))

    hit = (flat > 0).astype(F32)
    filled = jnp.max(hit, axis=0)
    earlier = jnp.sum(jnp.where(jnp.arange(slots)[:, None] < jnp.arange(slots), filled[:, None], 0), 0)
    to_row = jnp.concatenate(
        [jnp.eye(slots), (earlier == jnp.arange(2 * PACK)[:, None]).astype(F32)], axis=0
    )
    to_row = jnp.where(jnp.arange(slots + 2 * PACK)[:, None] < slots + PACK, to_row, 0.0)
    of_micro = jnp.arange(slots) // CAP == (me ^ jnp.arange(SECTIONS))[:, None]
    picks = jnp.sum(
        jnp.where(of_micro[:, None, None, :], to_row[:, None, :] * hit, 0.0), axis=-1
    ).astype(BF16)
    rows, normed, group, rank = pl.pallas_call(
        prepare_first,
        out_shape=(
            jax.ShapeDtypeStruct((slots, width), BF16),
            jax.ShapeDtypeStruct((PACK, width + LANES), BF16),
            jax.ShapeDtypeStruct((SECTIONS, LANES), F32),
            jax.ShapeDtypeStruct((SECTIONS, LANES), F32),
        ),
        in_specs=[SMEM] + [VMEM] * 6,
        out_specs=(VMEM,) * 4,
        compiler_params=PARAMS,
        name="prepare_first",
    )(place, picks, *messages, norm_gain)

    def rest(normed):
        near, far = group_rows(normed)
        near_part, far_part = expert_call(near, far, gate_proj, up_proj, down_proj)
        return near, far, tuple(spread(group_sum(near_part, far_part, PACK)))

    near, far, updates = rest(normed)
    sizes = jnp.maximum(jnp.max(near[:, width:], axis=0), jnp.max(far[:, width:], axis=0))
    steps = (sizes[:SECTIONS].astype(jnp.int32) + PACK - 1) // PACK
    starts = [jnp.int32(1)]
    for g in range(SECTIONS):
        starts.append(starts[-1] + steps[g])
    group, rank = group[:, :slots], rank[:, :slots].astype(jnp.int32)
    code = jnp.where(group < -1, -1, rank)
    for g in range(SECTIONS):
        code = jnp.where(group == g, starts[g] * PACK + rank, code)
    code_column = jnp.broadcast_to(code[:, None], (SECTIONS, 3, slots)).reshape(-1, 1)
    code_line = code[:1]
    tables = jnp.concatenate([m[:, width : width + 3 * slots] for m in messages], axis=1)
    inner = lax.dot_general(
        hit.astype(BF16), tables, (((0,), (0,)), ((), ())), preferred_element_type=F32
    )
    column = jnp.arange(SECTIONS * 3 * slots)
    column_micro = column % slots // CAP
    inner = jnp.where(jnp.arange(slots)[:, None] // CAP == column_micro, inner, 0.0)
    inner = jnp.where((me ^ (column // (3 * slots))) < me, inner, 0.0)
    outer = jnp.where(column_micro == me, tables.astype(F32), 0.0)
    linear = jnp.concatenate([outer, inner, jnp.zeros((8, column.size), F32)], axis=0).astype(BF16)
    block = column[:, None] // (3 * slots) == jnp.arange(SECTIONS * PACK) // PACK
    part = column // slots % 3
    blocks = (block & (part[:, None] == jnp.arange(3)[:, None, None])).astype(BF16)
    held = pltpu.VMEM((SECTIONS * PACK, width), F32)

    def body(state):
        turn, x, y, updates = state
        x, y, normed = pl.pallas_call(
            absorb,
            out_shape=(
                jax.ShapeDtypeStruct((tokens, width), BF16),
                jax.ShapeDtypeStruct((slots, width), BF16),
                jax.ShapeDtypeStruct((PACK, width), BF16),
            ),
            in_specs=[SMEM] + [VMEM] * 11,
            out_specs=(VMEM,) * 3,
            scratch_shapes=[held, pltpu.VMEM((slots, width), BF16)],
            compiler_params=PARAMS,
            name="absorb",
        )(turn[None], code_column, code_line, blocks, linear, x, y, *updates, norm_gain)
        return turn + 1, x, y, rest(normed)[2]

    turn, x, _, updates = lax.while_loop(
        lambda s: s[0] < starts[-1], body, (jnp.int32(1), embedded[0], rows, updates)
    )
    return pl.pallas_call(
        finish,
        out_shape=jax.ShapeDtypeStruct(embedded.shape, BF16),
        in_specs=[SMEM] + [VMEM] * 8,
        out_specs=VMEM,
        scratch_shapes=[held],
        compiler_params=PARAMS,
        name="finish",
    )(turn[None], code_column, blocks, linear, x, *updates)


def solution(mesh):
    placed = (
        P("section", "expert", None),
        P("section", None),
        P("section", None, "expert"),
        P("section", None, "expert"),
        P("section", "expert", None),
        P("section", None, "expert", None),
        P("section", None, "expert", None),
    )
    fits = mesh.shape["expert"] == 8 and mesh.shape["section"] == 4
    return jax.shard_map(
        shards_group if fits else shards_general, mesh=mesh, in_specs=placed, out_specs=P("section", "expert", None), check_vma=False
    )
```

```python
import jax
import jax.numpy as jnp
from jax import lax
from jax.experimental import pallas as pl
from jax.experimental.pallas import tpu as pltpu
from jax.sharding import PartitionSpec as P

CAP = 2

eps_norm = 1e-06


def slot_weights(chosen, gates, num_experts):
    expert_range = jnp.arange(num_experts, dtype=jnp.int32)
    matched = (chosen[..., None] == expert_range).astype(jnp.int32)
    hit_table = jnp.sum(matched, axis=-2, dtype=jnp.int32)
    tokens = chosen.shape[-2]
    before = jnp.arange(tokens)[:, None] > jnp.arange(tokens)[None, :]
    earlier = jnp.sum(
        jnp.where(before[:, :, None], hit_table[..., None, :, :], 0), axis=-2, dtype=jnp.int32
    )
    weight = jnp.sum(jnp.where(matched > 0, gates[..., None], 0.0), axis=-2)
    slots = jnp.arange(CAP, dtype=jnp.int32)
    table = jnp.where(earlier[..., None] == slots, weight[..., None], 0.0)
    return table.reshape(table.shape[:-2] + (num_experts * CAP,))


def swap(array, axis, by):
    devices = lax.axis_size(axis)
    return lax.ppermute(array, axis, [(i, i ^ by) for i in range(devices)])


def section_exchange(parts):
    return [parts[0]] + [swap(parts[k], "section", k) for k in range(1, len(parts))]


def dispatch(rows):
    experts, count, width = rows.shape
    n_dev = lax.axis_size("expert")
    send = jnp.repeat(rows, n_dev // experts, axis=0)
    return lax.all_to_all(send, "expert", split_axis=0, concat_axis=0, tiled=True)


def collect(partial, experts):
    n_dev, count, width = partial.shape
    back = lax.all_to_all(partial, "expert", split_axis=0, concat_axis=0, tiled=True)
    back = back.reshape(experts, n_dev // experts, count, width)
    return jnp.sum(back.astype(jnp.float32), axis=1)


def expert_block(rows_in, gate_mat, up_mat, down_mat):
    gate_val = jnp.dot(rows_in, gate_mat, preferred_element_type=jnp.float32)
    up_val = jnp.dot(rows_in, up_mat, preferred_element_type=jnp.float32)
    hidden = (jax.nn.silu(gate_val) * up_val).astype(jnp.bfloat16)
    return jnp.dot(hidden, down_mat, preferred_element_type=jnp.float32).astype(jnp.bfloat16)


def layer_round(sent, gain_row, gate_mat, up_mat, down_mat, num_experts):
    width = sent[0].shape[-1]
    here = jnp.stack(section_exchange(sent))
    rows_float = here.astype(jnp.float32)
    scale = lax.rsqrt(jnp.mean(rows_float * rows_float, axis=-1, keepdims=True) + eps_norm)
    normed = (rows_float * scale * gain_row).astype(jnp.bfloat16)
    micros = here.shape[0]
    normed = normed.reshape(micros, num_experts, CAP, width).transpose(1, 0, 2, 3)
    received = dispatch(normed.reshape(num_experts, micros * CAP, width))
    n_dev = received.shape[0]
    partial = expert_block(received.reshape(-1, width), gate_mat, up_mat, down_mat)
    total = collect(partial.reshape(n_dev, micros * CAP, width), num_experts)
    total = total.astype(jnp.bfloat16).reshape(num_experts, micros, CAP, width)
    total = total.transpose(1, 0, 2, 3).reshape(micros, num_experts * CAP, width)
    return section_exchange([total[k] for k in range(micros)])


def shards_general(embedded, norm_gain, gate_proj, up_proj, down_proj, expert_ids, route_gates):
    n_section = lax.axis_size("section")
    n_dev = lax.axis_size("expert")
    num_experts = n_dev // min(8, n_dev)
    me = lax.axis_index("section")
    base = embedded[0]
    own = slot_weights(expert_ids[0], route_gates[0], num_experts)

    def pick(stacked, index):
        return lax.dynamic_index_in_dim(stacked, index, 0, keepdims=False)

    tables = section_exchange([pick(own, me ^ k) for k in range(n_section)])
    tables = jnp.stack(tables)
    ordered = jnp.stack([pick(tables, me ^ l) for l in range(n_section)])
    chosen = ordered > 0
    picks = jnp.sum(jnp.any(chosen, axis=-1).astype(jnp.int32), axis=0)
    depth = lax.pmax(jnp.max(picks), ("section", "expert"))
    masks = chosen.astype(jnp.bfloat16)

    def take(mask, rows):
        return lax.dot_general(
            mask, rows, (((0,), (0,)), ((), ())), preferred_element_type=jnp.float32
        ).astype(jnp.bfloat16)

    def advance(rows, layer, update):
        routed = jnp.dot(
            ordered[layer],
            update.astype(jnp.float32),
            precision=lax.Precision.HIGHEST,
            preferred_element_type=jnp.float32,
        )
        return (rows.astype(jnp.float32) + routed).astype(jnp.bfloat16)

    def one_round(inputs):
        sent = [pick(inputs, me ^ k) for k in range(n_section)]
        got = jnp.stack(
            layer_round(sent, norm_gain[0], gate_proj[0], up_proj[0], down_proj[0], num_experts)
        )
        return jnp.stack([pick(got, me ^ l) for l in range(n_section)])

    def body(state):
        count, updates = state
        rows, inputs = base, []
        for layer in range(n_section):
            inputs.append(take(masks[layer], rows))
            if layer < n_section - 1:
                rows = advance(rows, layer, updates[layer])
        return count + 1, one_round(jnp.stack(inputs))

    first = jnp.stack([take(masks[layer], base) for layer in range(n_section)])
    updates = one_round(first)
    _, updates = lax.while_loop(lambda s: s[0] < depth, body, (jnp.int32(1), updates))
    rows = base
    for layer in range(n_section):
        rows = advance(rows, layer, updates[layer])
    return rows[None]


LANES = 128
SECTIONS = 4
STRIP = 1024
PACK = 4
BF16 = jnp.bfloat16
F32 = jnp.float32


def normalise(squares, kept, gain, normed_out):
    width = kept.shape[1]
    mean = jnp.sum(squares, axis=-1, keepdims=True) * (1.0 / width)
    scale = lax.rsqrt(mean + eps_norm)
    for start in range(0, width, STRIP):
        span = pl.ds(start, STRIP)
        value = kept[:, span] * scale * gain[:, span]
        normed_out[:, span] = value[:PACK].astype(BF16)


def before(values):
    total = values
    for by in (1, 2, 4):
        total = total + pltpu.roll(total, by, 1)
    return total - values


def slot_code(value):
    return (value & (SECTIONS * CAP - 1)) // CAP


def make_message(
    gates, embedded, message, x_out, picks, hits_out, token_out, table, sem
):
    me = lax.axis_index("section")
    micros, _, tokens = gates.shape
    width = embedded.shape[2]
    slots = micros * CAP
    copies = [
        pltpu.make_async_copy(embedded.at[0], message.at[:, pl.ds(0, width)], sem.at[0]),
        pltpu.make_async_copy(embedded.at[0], x_out, sem.at[1]),
    ]
    for copy in copies:
        copy.start()
    token_out[...] = jnp.zeros(token_out.shape, F32)
    row = lax.broadcasted_iota(jnp.int32, (tokens, tokens), 0)
    column = lax.broadcasted_iota(jnp.int32, (tokens, tokens), 1)
    ahead = jnp.where(row < column, 1.0, 0.0).astype(BF16)
    table[...] = jnp.zeros(table.shape, F32)
    hits = jnp.zeros((tokens, tokens), F32)
    for m in range(micros):
        weight = jnp.sum(gates[m], axis=0, keepdims=True)
        hit = jnp.where(weight > 0, 1.0, 0.0)
        hit = jnp.broadcast_to(hit, (tokens, tokens))
        slot = jnp.dot(hit.astype(BF16), ahead, preferred_element_type=F32).astype(jnp.int32)
        spot = (hit > 0) & (row == m * CAP + slot) & (slot < CAP)
        hits = jnp.where(spot, 1.0, hits)
        for q in range(CAP):
            chosen = (hit[:1] > 0) & (slot[:1] == q)
            value = jnp.where(chosen, weight, 0.0)
            high = value.astype(BF16).astype(F32)
            middle = (value - high).astype(BF16).astype(F32)
            at = m * CAP + q
            table[pl.ds(at, 1)] = high
            table[pl.ds(at + slots, 1)] = middle
            table[pl.ds(at + 2 * slots, 1)] = value - high - middle
    contract = (((1,), (1,)), ((), ()))
    same = jnp.where(row == column, 1.0, 0.0).astype(BF16)
    parts = lax.dot_general(
        same, table[...].astype(BF16), contract, preferred_element_type=F32
    )
    hits = hits.astype(BF16)
    hits_out[...] = hits
    sums = jnp.dot(
        jnp.where(column < row, 1.0, 0.0).astype(BF16), hits, preferred_element_type=F32
    )
    order = lax.dot_general(
        jnp.ones((tokens, tokens), BF16), sums.astype(BF16), contract, preferred_element_type=F32
    ).astype(jnp.int32)
    wanted = (row == column) | ((row >= slots) & (row < slots + PACK) & (order == row - slots))
    wanted = wanted & (column < slots)
    for j in range(SECTIONS):
        mine = wanted & (slot_code(column) == (me ^ j))
        picks[j] = jnp.dot(
            jnp.where(mine, 1.0, 0.0).astype(BF16), hits, preferred_element_type=F32
        ).astype(BF16)
    for copy in copies:
        copy.wait()
    message[:, width:] = parts.astype(BF16)


def prepare_first(
    picks, own_hits, x0, x1, x2, x3, gain, token, rows_out, normed_out, group_out, rank_out,
    linear_out, kept,
):
    me = lax.axis_index("section")
    messages = (x0, x1, x2, x3)
    slots, width = rows_out.shape
    total = 0.0
    for start in range(0, width, STRIP):
        span = pl.ds(start, STRIP)
        rows = sum(
            jnp.dot(picks[j], messages[j][:, span], preferred_element_type=F32)
            for j in range(SECTIONS)
        )
        rows_out[:, span] = rows[:slots].astype(BF16)
        packed = rows[slots:]
        kept[:, span] = packed
        total += packed * packed
    normalise(total, kept, gain, normed_out)

    lane = lax.broadcasted_iota(jnp.int32, (x0.shape[0], LANES), 1)
    hits = [
        jnp.where((lane < slots) & (m[:, width:].astype(F32) > 0), 1.0, 0.0) for m in messages
    ]
    pairs = [
        h + jnp.where(lane % CAP == 0, pltpu.roll(h, LANES - 1, 1), pltpu.roll(h, 1, 1))
        for h in hits
    ]
    largest = [jnp.zeros((1, 1), F32) for _ in range(SECTIONS)]
    for j in range(SECTIONS):
        mine = me ^ j
        level = jnp.zeros_like(hits[0])
        for other in range(SECTIONS):
            if other != j:
                level += pairs[other] * jnp.where((me ^ other) < mine, 1.0, 0.0)
        filled = jnp.sum(hits[j], axis=0, keepdims=True)
        level = jnp.sum(hits[j] * level, axis=0, keepdims=True)
        order = before(filled)
        late = jnp.where((level == 0) & (order >= PACK), filled, 0.0)
        group = jnp.where(filled > 0, jnp.where(level > 0, level, late - 1.0), -2.0)
        rank = order
        for g in range(SECTIONS):
            member = jnp.where(group == g, 1.0, 0.0)
            rank = jnp.where(group == g, before(member), rank)
            size = jnp.sum(member, axis=1, keepdims=True)
            largest[g] = jnp.maximum(largest[g], size)
        group_out[pl.ds(j, 1)] = group
        rank_out[pl.ds(j, 1)] = rank
    sizes = jnp.zeros((PACK, LANES), F32)
    spot = lax.broadcasted_iota(jnp.int32, (PACK, LANES), 1)
    for g in range(SECTIONS):
        sizes = jnp.where(spot == g, largest[g], sizes)
    normed_out[:, width:] = sizes.astype(BF16)

    span = 3 * slots
    table = jnp.zeros(lane.shape, F32)
    sooner = jnp.zeros(own_hits.shape[:1] + (LANES,), F32)
    row = lax.broadcasted_iota(jnp.int32, sooner.shape, 0)
    column = lax.broadcasted_iota(jnp.int32, sooner.shape, 1)
    for j in range(SECTIONS):
        part = jnp.where(lane < span, messages[j][:, width:].astype(F32), 0.0)
        table = table + (pltpu.roll(part, j * span, 1) if j else part)
        inside = (column >= j * span) & (column < (j + 1) * span)
        sooner = jnp.where(inside, jnp.where((me ^ j) < me, 1.0, 0.0), sooner)
    inner = jnp.dot(own_hits[...], table.astype(BF16), preferred_element_type=F32)
    inner = jnp.where(row // CAP == slot_code(column), inner * sooner, 0.0)
    tokens = lane.shape[0]
    linear_out[:tokens] = jnp.where(slot_code(lane) == me, table, 0.0).astype(BF16)
    linear_out[tokens:] = inner.astype(BF16)


def schedule(near, far, group, rank, codes_out, line_out, rounds_out, turn_out):
    width = near.shape[1] - LANES
    slots = SECTIONS * CAP
    sizes = jnp.maximum(
        jnp.max(near[:, width:].astype(F32), axis=0, keepdims=True),
        jnp.max(far[:, width:].astype(F32), axis=0, keepdims=True),
    )
    lane = lax.broadcasted_iota(jnp.int32, sizes.shape, 1)
    code = jnp.where(group[...] < -1, 0.0, rank[...] + 1)
    start = jnp.ones((1, 1), F32)
    for g in range(SECTIONS):
        code = jnp.where(group[...] == g, start * PACK + rank[...] + 1, code)
        size = jnp.sum(jnp.where(lane == g, sizes, 0.0), axis=1, keepdims=True)
        start = start + jnp.floor((size + (PACK - 1)) * (1.0 / PACK))
    rounds_out[0] = jnp.max(start).astype(jnp.int32)
    turn_out[...] = jnp.zeros(turn_out.shape, F32)
    span = 3 * slots
    line = jnp.zeros(sizes.shape, F32)
    for j in range(SECTIONS):
        own = jnp.where(lane < slots, code[j : j + 1], 0.0)
        for part in range(3):
            shift = j * span + part * slots
            line = line + (pltpu.roll(own, shift, 1) if shift else own)
    line_out[...] = line
    eye = lax.broadcasted_iota(jnp.int32, (LANES, LANES), 0) == lax.broadcasted_iota(
        jnp.int32, (LANES, LANES), 1
    )
    turned = lax.dot_general(
        jnp.where(eye, 1.0, 0.0).astype(BF16),
        jnp.broadcast_to(line, (SECTIONS * PACK, LANES)).astype(BF16),
        (((1,), (1,)), ((), ())),
        preferred_element_type=F32,
    )
    row = lax.broadcasted_iota(jnp.int32, turned.shape, 0)
    column = lax.broadcasted_iota(jnp.int32, turned.shape, 1)
    for part in range(3):
        kept = jnp.zeros(turned.shape, F32)
        for j in range(SECTIONS):
            low = j * span + part * slots
            block = (row >= low) & (row < low + slots) & (column // PACK == j)
            kept = jnp.where(block, turned, kept)
        codes_out[part] = kept


def arrived(turn, codes, linear, updates, held):
    for j, update in enumerate(updates):
        held[pl.ds(j * PACK, PACK)] = update[...].astype(F32)
    spot = lax.broadcasted_iota(jnp.int32, codes.shape[1:], 1)
    wanted = turn * PACK + (1 + (spot & (PACK - 1))).astype(F32)
    coefs = []
    for part in range(3):
        chosen = jnp.where(codes[part] == wanted, 1.0, 0.0).astype(BF16)
        coefs.append(jnp.dot(linear[...], chosen, preferred_element_type=F32))
    return jnp.concatenate(coefs, axis=0).astype(BF16)


def changes(coefs, held, span):
    result = jnp.dot(coefs, held[:, span].astype(BF16), preferred_element_type=F32)
    third = coefs.shape[0] // 3
    return result[:third] + result[third : 2 * third] + result[2 * third :]


def absorb(
    turn, codes, line, linear, x, y, u0, u1, u2, u3, gain, turn_out, x_out, y_out, normed_out,
    held, kept,
):
    turn_out[...] = turn[...] + 1
    coefs = arrived(turn[:, :1], codes, linear, (u0, u1, u2, u3), held)
    tokens, width = x.shape
    slots = y.shape[0]
    for start in range(0, width, STRIP):
        span = pl.ds(start, STRIP)
        change = changes(coefs, held, span)
        x_out[:, span] = (x[:, span].astype(F32) + change[:tokens]).astype(BF16)
        y_out[:, span] = (y[:, span].astype(F32) + change[tokens : tokens + slots]).astype(BF16)
    spot = lax.broadcasted_iota(jnp.int32, (2 * PACK, slots), 0)
    wanted = (turn[:, :1] + 1) * PACK + (1 + spot).astype(F32)
    pick = jnp.where((line[:, :slots] == wanted) & (spot < PACK), 1.0, 0.0).astype(BF16)
    total = 0.0
    for start in range(0, width, STRIP):
        span = pl.ds(start, STRIP)
        packed = jnp.dot(pick, y_out[:, span], preferred_element_type=F32)
        kept[:, span] = packed
        total += packed * packed
    normalise(total, kept, gain, normed_out)


def finish(turn, codes, linear, x, u0, u1, u2, u3, out, held):
    coefs = arrived(turn[:, :1], codes, linear, (u0, u1, u2, u3), held)
    tokens, width = x.shape
    for start in range(0, width, STRIP):
        span = pl.ds(start, STRIP)
        change = changes(coefs, held, span)
        out[0, :, span] = (x[:, span].astype(F32) + change[:tokens]).astype(BF16)


def expert_kernel(near, far, gate, up, down, near_out, far_out, rows):
    half, width = near_out.shape
    rows[:half] = near[:, :width]
    rows[half:] = far[:, :width]
    gate_val = jnp.dot(rows[...], gate[0], preferred_element_type=F32)
    up_val = jnp.dot(rows[...], up[0], preferred_element_type=F32)
    hidden = (gate_val * jax.nn.sigmoid(gate_val) * up_val).astype(BF16)
    for start in range(0, width, STRIP):
        span = pl.ds(start, STRIP)
        value = jnp.dot(hidden, down[0, :, span], preferred_element_type=F32).astype(BF16)
        near_out[:, span] = value[:half]
        far_out[:, span] = value[half:]


def hold_kernel(token, gate, up, down, gate_out, up_out, down_out, token_out, sems):
    token_out[...] = token[...]
    pairs = ((gate, gate_out), (up, up_out), (down, down_out))
    copies = [pltpu.make_async_copy(a, b, sems.at[i]) for i, (a, b) in enumerate(pairs)]
    for copy in copies:
        copy.start()
    for copy in copies:
        copy.wait()


VMEM = pl.BlockSpec(memory_space=pltpu.VMEM)
HBM = pl.BlockSpec(memory_space=pltpu.HBM)
PARAMS = pltpu.CompilerParams(vmem_limit_bytes=16 * 2**20)


def expert_call(near, far, gate, up, down):
    half = near.shape[0]
    _, width, hidden = gate.shape
    out = jax.ShapeDtypeStruct((half, width), BF16)
    return pl.pallas_call(
        expert_kernel,
        out_shape=(out, out),
        in_specs=[VMEM] * 5,
        out_specs=(VMEM, VMEM),
        scratch_shapes=[pltpu.VMEM((2 * half, width), BF16)],
        compiler_params=PARAMS,
        cost_estimate=pl.CostEstimate(
            flops=12 * half * width * hidden,
            bytes_accessed=6 * width * hidden,
            transcendentals=2 * half * hidden,
        ),
        name="experts",
    )(near, far, gate, up, down)


def hold_weights(token, *weights):
    outs = [jax.ShapeDtypeStruct(w.shape, w.dtype) for w in weights + (token,)]
    return pl.pallas_call(
        hold_kernel,
        out_shape=tuple(outs),
        in_specs=[VMEM] + [HBM] * 3,
        out_specs=(VMEM,) * 4,
        scratch_shapes=[pltpu.SemaphoreType.DMA((3,))],
        compiler_params=PARAMS,
        cost_estimate=pl.CostEstimate(
            flops=0, bytes_accessed=4 * sum(w.size for w in weights), transcendentals=0
        ),
        name="hold_weights",
    )(token, *weights)


def spread(array):
    return [array] + [swap(array, "section", j) for j in range(1, 4)]


def group_rows(normed):
    near = jnp.concatenate([normed] + [swap(normed, "expert", 2 * k) for k in range(1, 4)])
    return near, swap(near, "expert", 1)


def group_sum(near, far, count):
    other = swap(far, "expert", 1)
    both = (near.astype(F32) + other.astype(F32)).astype(BF16)
    parts = [both[k * count : (k + 1) * count] for k in range(4)]
    got = [parts[0]] + [swap(parts[k], "expert", 2 * k) for k in range(1, 4)]
    return sum(g.astype(F32) for g in got).astype(BF16)


def shards_group(embedded, norm_gain, gate_proj, up_proj, down_proj, expert_ids, route_gates):
    tokens, width = embedded.shape[1:]
    slots = expert_ids.shape[1] * CAP
    picked = slots + 2 * PACK

    def shape(dims, kind=BF16):
        return jax.ShapeDtypeStruct(dims, kind)

    def call(kernel, outs, ins, scratch=(), in_specs=None, out_specs=None):
        return pl.pallas_call(
            kernel,
            out_shape=outs,
            in_specs=in_specs or [VMEM] * len(ins),
            out_specs=out_specs or jax.tree.map(lambda _: VMEM, outs),
            scratch_shapes=scratch,
            compiler_params=PARAMS,
            name=kernel.__name__,
        )(*ins)

    gates = jnp.where(expert_ids[0] < 1, route_gates[0], 0.0).transpose(0, 2, 1)
    message, x, picks, hits, token = call(
        make_message,
        (
            shape((tokens, width + LANES)),
            shape((tokens, width)),
            shape((SECTIONS, picked, tokens)),
            shape((picked, tokens)),
            shape((8, LANES), F32),
        ),
        (gates, embedded),
        [pltpu.VMEM((LANES, tokens), F32), pltpu.SemaphoreType.DMA((2,))],
        in_specs=[VMEM, HBM],
    )
    messages = spread(message)
    *weights, token = hold_weights(token, gate_proj, up_proj, down_proj)
    y, normed, group, rank, linear = call(
        prepare_first,
        (
            shape((slots, width)),
            shape((PACK, width + LANES)),
            shape((SECTIONS, LANES), F32),
            shape((SECTIONS, LANES), F32),
            shape((tokens + picked, LANES)),
        ),
        (picks, hits, *messages, norm_gain, token),
        [pltpu.VMEM((2 * PACK, width), F32)],
    )

    def rest(normed):
        near, far = group_rows(normed)
        near_part, far_part = expert_call(near, far, *weights)
        return near, far, tuple(spread(group_sum(near_part, far_part, PACK)))

    near, far, updates = rest(normed)
    codes, line, rounds, turn = call(
        schedule,
        (
            shape((3, LANES, SECTIONS * PACK), F32),
            shape((1, LANES), F32),
            shape((1,), jnp.int32),
            shape((1, LANES), F32),
        ),
        (near, far, group, rank),
        out_specs=(VMEM, VMEM, pl.BlockSpec(memory_space=pltpu.SMEM), VMEM),
    )
    held = pltpu.VMEM((SECTIONS * PACK, width), F32)

    def body(state):
        count, turn, x, y, updates = state
        turn, x, y, normed = call(
            absorb,
            (shape((1, LANES), F32), shape((tokens, width)), shape((slots, width)), shape((PACK, width))),
            (turn, codes, line, linear, x, y, *updates, norm_gain),
            [held, pltpu.VMEM((2 * PACK, width), F32)],
        )
        return count + 1, turn, x, y, rest(normed)[2]

    _, turn, x, _, updates = lax.while_loop(
        lambda s: s[0][0] < rounds[0], body, (jnp.ones((1,), jnp.int32), turn, x, y, updates)
    )
    return call(
        finish, shape(embedded.shape), (turn, codes, linear, x, *updates), [held]
    )


def solution(mesh):
    placed = (
        P("section", "expert", None),
        P("section", None),
        P("section", None, "expert"),
        P("section", None, "expert"),
        P("section", "expert", None),
        P("section", None, "expert", None),
        P("section", None, "expert", None),
    )
    fits = mesh.shape["expert"] == 8 and mesh.shape["section"] == 4
    return jax.shard_map(
        shards_group if fits else shards_general, mesh=mesh, in_specs=placed, out_specs=P("section", "expert", None), check_vma=False
    )
```

```python
import jax
import jax.numpy as jnp
from jax import lax
from jax.experimental import pallas as pl
from jax.experimental.pallas import tpu as pltpu
from jax.sharding import PartitionSpec as P

CAP = 2

eps_norm = 1e-06


def slot_weights(chosen, gates, num_experts):
    expert_range = jnp.arange(num_experts, dtype=jnp.int32)
    matched = (chosen[..., None] == expert_range).astype(jnp.int32)
    hit_table = jnp.sum(matched, axis=-2, dtype=jnp.int32)
    tokens = chosen.shape[-2]
    before = jnp.arange(tokens)[:, None] > jnp.arange(tokens)[None, :]
    earlier = jnp.sum(
        jnp.where(before[:, :, None], hit_table[..., None, :, :], 0), axis=-2, dtype=jnp.int32
    )
    weight = jnp.sum(jnp.where(matched > 0, gates[..., None], 0.0), axis=-2)
    slots = jnp.arange(CAP, dtype=jnp.int32)
    table = jnp.where(earlier[..., None] == slots, weight[..., None], 0.0)
    return table.reshape(table.shape[:-2] + (num_experts * CAP,))


def swap(array, axis, by):
    devices = lax.axis_size(axis)
    return lax.ppermute(array, axis, [(i, i ^ by) for i in range(devices)])


def section_exchange(parts):
    return [parts[0]] + [swap(parts[k], "section", k) for k in range(1, len(parts))]


def dispatch(rows):
    experts, count, width = rows.shape
    n_dev = lax.axis_size("expert")
    send = jnp.repeat(rows, n_dev // experts, axis=0)
    return lax.all_to_all(send, "expert", split_axis=0, concat_axis=0, tiled=True)


def collect(partial, experts):
    n_dev, count, width = partial.shape
    back = lax.all_to_all(partial, "expert", split_axis=0, concat_axis=0, tiled=True)
    back = back.reshape(experts, n_dev // experts, count, width)
    return jnp.sum(back.astype(jnp.float32), axis=1)


def expert_block(rows_in, gate_mat, up_mat, down_mat):
    gate_val = jnp.dot(rows_in, gate_mat, preferred_element_type=jnp.float32)
    up_val = jnp.dot(rows_in, up_mat, preferred_element_type=jnp.float32)
    hidden = (jax.nn.silu(gate_val) * up_val).astype(jnp.bfloat16)
    return jnp.dot(hidden, down_mat, preferred_element_type=jnp.float32).astype(jnp.bfloat16)


def layer_round(sent, gain_row, gate_mat, up_mat, down_mat, num_experts):
    width = sent[0].shape[-1]
    here = jnp.stack(section_exchange(sent))
    rows_float = here.astype(jnp.float32)
    scale = lax.rsqrt(jnp.mean(rows_float * rows_float, axis=-1, keepdims=True) + eps_norm)
    normed = (rows_float * scale * gain_row).astype(jnp.bfloat16)
    micros = here.shape[0]
    normed = normed.reshape(micros, num_experts, CAP, width).transpose(1, 0, 2, 3)
    received = dispatch(normed.reshape(num_experts, micros * CAP, width))
    n_dev = received.shape[0]
    partial = expert_block(received.reshape(-1, width), gate_mat, up_mat, down_mat)
    total = collect(partial.reshape(n_dev, micros * CAP, width), num_experts)
    total = total.astype(jnp.bfloat16).reshape(num_experts, micros, CAP, width)
    total = total.transpose(1, 0, 2, 3).reshape(micros, num_experts * CAP, width)
    return section_exchange([total[k] for k in range(micros)])


def shards_general(embedded, norm_gain, gate_proj, up_proj, down_proj, expert_ids, route_gates):
    n_section = lax.axis_size("section")
    n_dev = lax.axis_size("expert")
    num_experts = n_dev // min(8, n_dev)
    me = lax.axis_index("section")
    base = embedded[0]
    own = slot_weights(expert_ids[0], route_gates[0], num_experts)

    def pick(stacked, index):
        return lax.dynamic_index_in_dim(stacked, index, 0, keepdims=False)

    tables = section_exchange([pick(own, me ^ k) for k in range(n_section)])
    tables = jnp.stack(tables)
    ordered = jnp.stack([pick(tables, me ^ l) for l in range(n_section)])
    chosen = ordered > 0
    picks = jnp.sum(jnp.any(chosen, axis=-1).astype(jnp.int32), axis=0)
    depth = lax.pmax(jnp.max(picks), ("section", "expert"))
    masks = chosen.astype(jnp.bfloat16)

    def take(mask, rows):
        return lax.dot_general(
            mask, rows, (((0,), (0,)), ((), ())), preferred_element_type=jnp.float32
        ).astype(jnp.bfloat16)

    def advance(rows, layer, update):
        routed = jnp.dot(
            ordered[layer],
            update.astype(jnp.float32),
            precision=lax.Precision.HIGHEST,
            preferred_element_type=jnp.float32,
        )
        return (rows.astype(jnp.float32) + routed).astype(jnp.bfloat16)

    def one_round(inputs):
        sent = [pick(inputs, me ^ k) for k in range(n_section)]
        got = jnp.stack(
            layer_round(sent, norm_gain[0], gate_proj[0], up_proj[0], down_proj[0], num_experts)
        )
        return jnp.stack([pick(got, me ^ l) for l in range(n_section)])

    def body(state):
        count, updates = state
        rows, inputs = base, []
        for layer in range(n_section):
            inputs.append(take(masks[layer], rows))
            if layer < n_section - 1:
                rows = advance(rows, layer, updates[layer])
        return count + 1, one_round(jnp.stack(inputs))

    first = jnp.stack([take(masks[layer], base) for layer in range(n_section)])
    updates = one_round(first)
    _, updates = lax.while_loop(lambda s: s[0] < depth, body, (jnp.int32(1), updates))
    rows = base
    for layer in range(n_section):
        rows = advance(rows, layer, updates[layer])
    return rows[None]


LANES = 128
SECTIONS = 4
STRIP = 1024
PACK = 4
BF16 = jnp.bfloat16
F32 = jnp.float32


def normalise(squares, kept, gain, normed_out):
    width = kept.shape[1]
    mean = jnp.sum(squares, axis=-1, keepdims=True) * (1.0 / width)
    scale = lax.rsqrt(mean + eps_norm)
    for start in range(0, width, STRIP):
        span = pl.ds(start, STRIP)
        value = kept[:, span] * scale * gain[:, span]
        normed_out[:, span] = value[:PACK].astype(BF16)


def before(values):
    total = values
    for by in (1, 2, 4):
        total = total + pltpu.roll(total, by, 1)
    return total - values


def slot_code(value):
    return (value & (SECTIONS * CAP - 1)) // CAP


def slot_tables(gates, parts_out, picks, picks_relayed, hits_out, table):
    me = lax.axis_index("section")
    micros, _, tokens = gates.shape
    slots = micros * CAP
    row = lax.broadcasted_iota(jnp.int32, (tokens, tokens), 0)
    column = lax.broadcasted_iota(jnp.int32, (tokens, tokens), 1)
    ahead = jnp.where(row < column, 1.0, 0.0).astype(BF16)
    table[...] = jnp.zeros(table.shape, F32)
    hits = jnp.zeros((tokens, tokens), F32)
    for m in range(micros):
        weight = jnp.sum(gates[m], axis=0, keepdims=True)
        hit = jnp.where(weight > 0, 1.0, 0.0)
        hit = jnp.broadcast_to(hit, (tokens, tokens))
        slot = jnp.dot(hit.astype(BF16), ahead, preferred_element_type=F32).astype(jnp.int32)
        spot = (hit > 0) & (row == m * CAP + slot) & (slot < CAP)
        hits = jnp.where(spot, 1.0, hits)
        for q in range(CAP):
            chosen = (hit[:1] > 0) & (slot[:1] == q)
            value = jnp.where(chosen, weight, 0.0)
            high = value.astype(BF16).astype(F32)
            middle = (value - high).astype(BF16).astype(F32)
            at = m * CAP + q
            table[pl.ds(at, 1)] = high
            table[pl.ds(at + slots, 1)] = middle
            table[pl.ds(at + 2 * slots, 1)] = value - high - middle
    contract = (((1,), (1,)), ((), ()))
    same = jnp.where(row == column, 1.0, 0.0).astype(BF16)
    parts_out[...] = lax.dot_general(
        same, table[...].astype(BF16), contract, preferred_element_type=F32
    ).astype(BF16)
    hits = hits.astype(BF16)
    hits_out[...] = hits
    sums = jnp.dot(
        jnp.where(column < row, 1.0, 0.0).astype(BF16), hits, preferred_element_type=F32
    )
    order = lax.dot_general(
        jnp.ones((tokens, tokens), BF16), sums.astype(BF16), contract, preferred_element_type=F32
    ).astype(jnp.int32)
    filled = lax.dot_general(
        jnp.ones((tokens, tokens), BF16), hits, contract, preferred_element_type=F32
    )
    wanted = (row == column) | ((row >= slots) & (row < slots + PACK) & (order == row - slots))
    wanted = wanted & (column < slots)
    for j in range(SECTIONS - 1):
        mine = wanted & (slot_code(column) == (me ^ j))
        picks[j] = jnp.dot(
            jnp.where(mine, 1.0, 0.0).astype(BF16), hits, preferred_element_type=F32
        ).astype(BF16)
    mine = wanted & (slot_code(column) == (me ^ (SECTIONS - 1)))
    picks_relayed[...] = jnp.where(mine, filled, 0.0)


def stage(after, gain, embedded, gain_out, x_out):
    gain_out[...] = gain[...]
    x_out[...] = embedded[0]


def relay(table, table_two, rows, gain, out):
    me = lax.axis_index("section")
    width = rows.shape[1]
    row = lax.broadcasted_iota(jnp.int32, (8, LANES), 0)
    lane = lax.broadcasted_iota(jnp.int32, (8, LANES), 1)
    wanted = (lane == (me ^ 2) * CAP + row) & (row < CAP)
    chosen = jnp.where(table[...].astype(F32) > 0, 1.0, 0.0).astype(BF16)
    pick = lax.dot_general(
        jnp.where(wanted, 1.0, 0.0).astype(BF16),
        chosen,
        (((1,), (1,)), ((), ())),
        preferred_element_type=F32,
    ).astype(BF16)
    for start in range(0, width, STRIP):
        span = pl.ds(start, STRIP)
        value = jnp.dot(pick, rows[:, span], preferred_element_type=F32)
        out[:, span] = value[:CAP].astype(BF16)
    extra = table_two[...].astype(F32)
    for t in range(extra.shape[0]):
        line = jnp.broadcast_to(extra[t : t + 1], (CAP, LANES))
        out[:, pl.ds(width + t * LANES, LANES)] = line.astype(BF16)


def prepare_first(
    picks, picks_relayed, own_hits, x0, x1, x2, relayed, t0, t1, t2, gain, rows_out,
    normed_out, group_out, rank_out, linear_out, kept, last,
):
    me = lax.axis_index("section")
    inputs = (x0, x1, x2)
    slots, width = rows_out.shape
    for t in range(last.shape[0]):
        last[pl.ds(t, 1)] = relayed[:, pl.ds(width + t * LANES, LANES)].astype(F32)[:1]
    tables = (t0, t1, t2, last)
    far_column = lax.broadcasted_iota(jnp.int32, picks_relayed.shape, 1)
    far = [
        jnp.sum(
            jnp.where((far_column & (CAP - 1)) == q, picks_relayed[...], 0.0), axis=1, keepdims=True
        )
        for q in range(CAP)
    ]
    total = 0.0
    for start in range(0, width, STRIP):
        span = pl.ds(start, STRIP)
        rows = sum(
            jnp.dot(picks[j], inputs[j][:, span], preferred_element_type=F32)
            for j in range(SECTIONS - 1)
        )
        extra = relayed[:, span].astype(F32)
        rows = rows + sum(far[q] * extra[q : q + 1] for q in range(CAP))
        rows_out[:, span] = rows[:slots].astype(BF16)
        packed = rows[slots:]
        kept[:, span] = packed
        total += packed * packed
    normalise(total, kept, gain, normed_out)

    lane = lax.broadcasted_iota(jnp.int32, (x0.shape[0], LANES), 1)
    hits = [
        jnp.where((lane < slots) & (t[...].astype(F32) > 0), 1.0, 0.0) for t in tables
    ]
    pairs = [
        h + jnp.where(lane % CAP == 0, pltpu.roll(h, LANES - 1, 1), pltpu.roll(h, 1, 1))
        for h in hits
    ]
    largest = [jnp.zeros((1, 1), F32) for _ in range(SECTIONS)]
    for j in range(SECTIONS):
        mine = me ^ j
        level = jnp.zeros_like(hits[0])
        for other in range(SECTIONS):
            if other != j:
                level += pairs[other] * jnp.where((me ^ other) < mine, 1.0, 0.0)
        filled = jnp.sum(hits[j], axis=0, keepdims=True)
        level = jnp.sum(hits[j] * level, axis=0, keepdims=True)
        order = before(filled)
        late = jnp.where((level == 0) & (order >= PACK), filled, 0.0)
        group = jnp.where(filled > 0, jnp.where(level > 0, level, late - 1.0), -2.0)
        rank = order
        for g in range(SECTIONS):
            member = jnp.where(group == g, 1.0, 0.0)
            rank = jnp.where(group == g, before(member), rank)
            size = jnp.sum(member, axis=1, keepdims=True)
            largest[g] = jnp.maximum(largest[g], size)
        group_out[pl.ds(j, 1)] = group
        rank_out[pl.ds(j, 1)] = rank
    sizes = jnp.zeros((PACK, LANES), F32)
    spot = lax.broadcasted_iota(jnp.int32, (PACK, LANES), 1)
    for g in range(SECTIONS):
        sizes = jnp.where(spot == g, largest[g], sizes)
    normed_out[:, width:] = sizes.astype(BF16)

    span = 3 * slots
    table = jnp.zeros(lane.shape, F32)
    sooner = jnp.zeros(own_hits.shape[:1] + (LANES,), F32)
    row = lax.broadcasted_iota(jnp.int32, sooner.shape, 0)
    column = lax.broadcasted_iota(jnp.int32, sooner.shape, 1)
    for j in range(SECTIONS):
        part = jnp.where(lane < span, tables[j][...].astype(F32), 0.0)
        table = table + (pltpu.roll(part, j * span, 1) if j else part)
        inside = (column >= j * span) & (column < (j + 1) * span)
        sooner = jnp.where(inside, jnp.where((me ^ j) < me, 1.0, 0.0), sooner)
    inner = jnp.dot(own_hits[...], table.astype(BF16), preferred_element_type=F32)
    inner = jnp.where(row // CAP == slot_code(column), inner * sooner, 0.0)
    tokens = lane.shape[0]
    linear_out[:tokens] = jnp.where(slot_code(lane) == me, table, 0.0).astype(BF16)
    linear_out[tokens:] = inner.astype(BF16)


def schedule(near, far, group, rank, codes_out, line_out, rounds_out, turn_out):
    width = near.shape[1] - LANES
    slots = SECTIONS * CAP
    sizes = jnp.maximum(
        jnp.max(near[:, width:].astype(F32), axis=0, keepdims=True),
        jnp.max(far[:, width:].astype(F32), axis=0, keepdims=True),
    )
    lane = lax.broadcasted_iota(jnp.int32, sizes.shape, 1)
    code = jnp.where(group[...] < -1, 0.0, rank[...] + 1)
    start = jnp.ones((1, 1), F32)
    for g in range(SECTIONS):
        code = jnp.where(group[...] == g, start * PACK + rank[...] + 1, code)
        size = jnp.sum(jnp.where(lane == g, sizes, 0.0), axis=1, keepdims=True)
        start = start + jnp.floor((size + (PACK - 1)) * (1.0 / PACK))
    rounds_out[0] = jnp.max(start).astype(jnp.int32)
    turn_out[...] = jnp.zeros(turn_out.shape, F32)
    span = 3 * slots
    line = jnp.zeros(sizes.shape, F32)
    for j in range(SECTIONS):
        own = jnp.where(lane < slots, code[j : j + 1], 0.0)
        for part in range(3):
            shift = j * span + part * slots
            line = line + (pltpu.roll(own, shift, 1) if shift else own)
    line_out[...] = line
    eye = lax.broadcasted_iota(jnp.int32, (LANES, LANES), 0) == lax.broadcasted_iota(
        jnp.int32, (LANES, LANES), 1
    )
    turned = lax.dot_general(
        jnp.where(eye, 1.0, 0.0).astype(BF16),
        jnp.broadcast_to(line, (SECTIONS * PACK, LANES)).astype(BF16),
        (((1,), (1,)), ((), ())),
        preferred_element_type=F32,
    )
    row = lax.broadcasted_iota(jnp.int32, turned.shape, 0)
    column = lax.broadcasted_iota(jnp.int32, turned.shape, 1)
    for part in range(3):
        kept = jnp.zeros(turned.shape, F32)
        for j in range(SECTIONS):
            low = j * span + part * slots
            block = (row >= low) & (row < low + slots) & (column // PACK == j)
            kept = jnp.where(block, turned, kept)
        codes_out[part] = kept


def arrived(turn, codes, linear, updates, held):
    for j, update in enumerate(updates):
        held[pl.ds(j * PACK, PACK)] = update[...].astype(F32)
    spot = lax.broadcasted_iota(jnp.int32, codes.shape[1:], 1)
    wanted = turn * PACK + (1 + (spot & (PACK - 1))).astype(F32)
    coefs = []
    for part in range(3):
        chosen = jnp.where(codes[part] == wanted, 1.0, 0.0).astype(BF16)
        coefs.append(jnp.dot(linear[...], chosen, preferred_element_type=F32))
    return jnp.concatenate(coefs, axis=0).astype(BF16)


def changes(coefs, held, span):
    result = jnp.dot(coefs, held[:, span].astype(BF16), preferred_element_type=F32)
    third = coefs.shape[0] // 3
    return result[:third] + result[third : 2 * third] + result[2 * third :]


def absorb(
    turn, codes, line, linear, x, y, u0, u1, u2, u3, gain, turn_out, x_out, y_out, normed_out,
    held, kept,
):
    turn_out[...] = turn[...] + 1
    coefs = arrived(turn[:, :1], codes, linear, (u0, u1, u2, u3), held)
    tokens, width = x.shape
    slots = y.shape[0]
    for start in range(0, width, STRIP):
        span = pl.ds(start, STRIP)
        change = changes(coefs, held, span)
        x_out[:, span] = (x[:, span].astype(F32) + change[:tokens]).astype(BF16)
        y_out[:, span] = (y[:, span].astype(F32) + change[tokens : tokens + slots]).astype(BF16)
    spot = lax.broadcasted_iota(jnp.int32, (2 * PACK, slots), 0)
    wanted = (turn[:, :1] + 1) * PACK + (1 + spot).astype(F32)
    pick = jnp.where((line[:, :slots] == wanted) & (spot < PACK), 1.0, 0.0).astype(BF16)
    total = 0.0
    for start in range(0, width, STRIP):
        span = pl.ds(start, STRIP)
        packed = jnp.dot(pick, y_out[:, span], preferred_element_type=F32)
        kept[:, span] = packed
        total += packed * packed
    normalise(total, kept, gain, normed_out)


def finish(turn, codes, linear, x, u0, u1, u2, u3, out, held):
    coefs = arrived(turn[:, :1], codes, linear, (u0, u1, u2, u3), held)
    tokens, width = x.shape
    for start in range(0, width, STRIP):
        span = pl.ds(start, STRIP)
        change = changes(coefs, held, span)
        out[0, :, span] = (x[:, span].astype(F32) + change[:tokens]).astype(BF16)


def expert_kernel(near, far, gate, up, down, near_out, far_out, rows):
    half, width = near_out.shape
    rows[:half] = near[:, :width]
    rows[half:] = far[:, :width]
    gate_val = jnp.dot(rows[...], gate[0], preferred_element_type=F32)
    up_val = jnp.dot(rows[...], up[0], preferred_element_type=F32)
    hidden = (gate_val * jax.nn.sigmoid(gate_val) * up_val).astype(BF16)
    for start in range(0, width, STRIP):
        span = pl.ds(start, STRIP)
        value = jnp.dot(hidden, down[0, :, span], preferred_element_type=F32).astype(BF16)
        near_out[:, span] = value[:half]
        far_out[:, span] = value[half:]


def hold_kernel(rows, gate, up, down, gate_out, up_out, down_out, rows_out, sems):
    rows_out[...] = rows[...]
    pairs = ((gate, gate_out), (up, up_out), (down, down_out))
    copies = [pltpu.make_async_copy(a, b, sems.at[i]) for i, (a, b) in enumerate(pairs)]
    for copy in copies:
        copy.start()
    for copy in copies:
        copy.wait()


VMEM = pl.BlockSpec(memory_space=pltpu.VMEM)
HBM = pl.BlockSpec(memory_space=pltpu.HBM)
PARAMS = pltpu.CompilerParams(vmem_limit_bytes=16 * 2**20)


def expert_call(near, far, gate, up, down):
    half = near.shape[0]
    _, width, hidden = gate.shape
    out = jax.ShapeDtypeStruct((half, width), BF16)
    return pl.pallas_call(
        expert_kernel,
        out_shape=(out, out),
        in_specs=[VMEM] * 5,
        out_specs=(VMEM, VMEM),
        scratch_shapes=[pltpu.VMEM((2 * half, width), BF16)],
        compiler_params=PARAMS,
        cost_estimate=pl.CostEstimate(
            flops=12 * half * width * hidden,
            bytes_accessed=6 * width * hidden,
            transcendentals=2 * half * hidden,
        ),
        name="experts",
    )(near, far, gate, up, down)


def hold_weights(rows, *weights):
    outs = [jax.ShapeDtypeStruct(w.shape, w.dtype) for w in weights + (rows,)]
    return pl.pallas_call(
        hold_kernel,
        out_shape=tuple(outs),
        in_specs=[VMEM] + [HBM] * 3,
        out_specs=(VMEM,) * 4,
        scratch_shapes=[pltpu.SemaphoreType.DMA((3,))],
        compiler_params=pltpu.CompilerParams(vmem_limit_bytes=52 * 2**20),
        cost_estimate=pl.CostEstimate(
            flops=0, bytes_accessed=4 * sum(w.size for w in weights), transcendentals=0
        ),
        name="hold_weights",
    )(rows, *weights)


def spread(array):
    return [array] + [swap(array, "section", j) for j in range(1, 4)]


def group_rows(normed, own, order):
    near = jnp.concatenate([own] + [swap(normed, "expert", 2 * k) for k in order])
    return near, swap(near, "expert", 1)


def group_sum(near, far, order, sums):
    other = swap(far, "expert", 1)
    both = (near.astype(F32) + other.astype(F32)).astype(BF16)
    parts = {k: both[i * PACK : (i + 1) * PACK] for i, k in enumerate((0, *order))}
    total = parts[0].astype(F32)
    for k in sums:
        total = total + swap(parts[k], "expert", 2 * k).astype(F32)
    return total.astype(BF16)


def shards_group(embedded, norm_gain, gate_proj, up_proj, down_proj, expert_ids, route_gates):
    tokens, width = embedded.shape[1:]
    slots = expert_ids.shape[1] * CAP
    picked = slots + 2 * PACK

    def shape(dims, kind=BF16):
        return jax.ShapeDtypeStruct(dims, kind)

    def call(kernel, outs, ins, scratch=(), in_specs=None, out_specs=None):
        return pl.pallas_call(
            kernel,
            out_shape=outs,
            in_specs=in_specs or [VMEM] * len(ins),
            out_specs=out_specs or jax.tree.map(lambda _: VMEM, outs),
            scratch_shapes=scratch,
            compiler_params=PARAMS,
            name=kernel.__name__,
        )(*ins)

    x_near = [swap(embedded[0], "section", j) for j in (1, 2)]
    gates = jnp.where(expert_ids[0] < 1, route_gates[0], 0.0).transpose(0, 2, 1)
    parts, picks, picks_relayed, hits = call(
        slot_tables,
        (
            shape((tokens, LANES)),
            shape((SECTIONS - 1, picked, tokens)),
            shape((picked, tokens), F32),
            shape((picked, tokens)),
        ),
        (gates,),
        [pltpu.VMEM((LANES, tokens), F32)],
    )
    tables = [parts] + [swap(parts, "section", j) for j in (1, 2)]
    gain, x = call(
        stage,
        (shape(norm_gain.shape, F32), shape((tokens, width))),
        (parts, norm_gain, embedded),
    )
    relayed = call(
        relay, shape((CAP, width + tokens * LANES)), (tables[1], tables[2], x_near[1], gain)
    )
    relayed = swap(relayed, "section", 1)
    y, normed, group, rank, linear = call(
        prepare_first,
        (
            shape((slots, width)),
            shape((PACK, width + LANES)),
            shape((SECTIONS, LANES), F32),
            shape((SECTIONS, LANES), F32),
            shape((tokens + picked, LANES)),
        ),
        (picks, picks_relayed, hits, x, *x_near, relayed, *tables, gain),
        [pltpu.VMEM((2 * PACK, width), F32), pltpu.VMEM((tokens, LANES), F32)],
    )
    *weights, own = hold_weights(normed, gate_proj, up_proj, down_proj)

    def rest(normed, own, order, sums):
        near, far = group_rows(normed, own, order)
        near_part, far_part = expert_call(near, far, *weights)
        return near, far, tuple(spread(group_sum(near_part, far_part, order, sums)))

    near, far, updates = rest(normed, own, (1, 2, 3), (3, 1, 2))
    codes, line, rounds, turn = call(
        schedule,
        (
            shape((3, LANES, SECTIONS * PACK), F32),
            shape((1, LANES), F32),
            shape((1,), jnp.int32),
            shape((1, LANES), F32),
        ),
        (near, far, group, rank),
        out_specs=(VMEM, VMEM, pl.BlockSpec(memory_space=pltpu.SMEM), VMEM),
    )
    held = pltpu.VMEM((SECTIONS * PACK, width), F32)

    def body(state):
        count, turn, x, y, updates = state
        turn, x, y, normed = call(
            absorb,
            (shape((1, LANES), F32), shape((tokens, width)), shape((slots, width)), shape((PACK, width))),
            (turn, codes, line, linear, x, y, *updates, gain),
            [held, pltpu.VMEM((2 * PACK, width), F32)],
        )
        return count + 1, turn, x, y, rest(normed, normed, (3, 2, 1), (1, 2, 3))[2]

    _, turn, x, _, updates = lax.while_loop(
        lambda s: s[0][0] < rounds[0], body, (jnp.ones((1,), jnp.int32), turn, x, y, updates)
    )
    return call(
        finish, shape(embedded.shape), (turn, codes, linear, x, *updates), [held]
    )


def solution(mesh):
    placed = (
        P("section", "expert", None),
        P("section", None),
        P("section", None, "expert"),
        P("section", None, "expert"),
        P("section", "expert", None),
        P("section", None, "expert", None),
        P("section", None, "expert", None),
    )
    fits = mesh.shape["expert"] == 8 and mesh.shape["section"] == 4
    return jax.shard_map(
        shards_group if fits else shards_general, mesh=mesh, in_specs=placed, out_specs=P("section", "expert", None), check_vma=False
    )
```

```python
import functools

import jax
import jax.numpy as jnp
from jax import lax
from jax.experimental import pallas as pl
from jax.experimental.pallas import tpu as pltpu
from jax.sharding import PartitionSpec as P

CAP = 2

eps_norm = 1e-06


def slot_weights(chosen, gates, num_experts):
    expert_range = jnp.arange(num_experts, dtype=jnp.int32)
    matched = (chosen[..., None] == expert_range).astype(jnp.int32)
    hit_table = jnp.sum(matched, axis=-2, dtype=jnp.int32)
    tokens = chosen.shape[-2]
    before = jnp.arange(tokens)[:, None] > jnp.arange(tokens)[None, :]
    earlier = jnp.sum(
        jnp.where(before[:, :, None], hit_table[..., None, :, :], 0), axis=-2, dtype=jnp.int32
    )
    weight = jnp.sum(jnp.where(matched > 0, gates[..., None], 0.0), axis=-2)
    slots = jnp.arange(CAP, dtype=jnp.int32)
    table = jnp.where(earlier[..., None] == slots, weight[..., None], 0.0)
    return table.reshape(table.shape[:-2] + (num_experts * CAP,))


def swap(array, axis, by):
    devices = lax.axis_size(axis)
    return lax.ppermute(array, axis, [(i, i ^ by) for i in range(devices)])


def section_exchange(parts):
    return [parts[0]] + [swap(parts[k], "section", k) for k in range(1, len(parts))]


def dispatch(rows):
    experts, count, width = rows.shape
    n_dev = lax.axis_size("expert")
    send = jnp.repeat(rows, n_dev // experts, axis=0)
    return lax.all_to_all(send, "expert", split_axis=0, concat_axis=0, tiled=True)


def collect(partial, experts):
    n_dev, count, width = partial.shape
    back = lax.all_to_all(partial, "expert", split_axis=0, concat_axis=0, tiled=True)
    back = back.reshape(experts, n_dev // experts, count, width)
    return jnp.sum(back.astype(jnp.float32), axis=1)


def expert_block(rows_in, gate_mat, up_mat, down_mat):
    gate_val = jnp.dot(rows_in, gate_mat, preferred_element_type=jnp.float32)
    up_val = jnp.dot(rows_in, up_mat, preferred_element_type=jnp.float32)
    hidden = (jax.nn.silu(gate_val) * up_val).astype(jnp.bfloat16)
    return jnp.dot(hidden, down_mat, preferred_element_type=jnp.float32).astype(jnp.bfloat16)


def layer_round(sent, gain_row, gate_mat, up_mat, down_mat, num_experts):
    width = sent[0].shape[-1]
    here = jnp.stack(section_exchange(sent))
    rows_float = here.astype(jnp.float32)
    scale = lax.rsqrt(jnp.mean(rows_float * rows_float, axis=-1, keepdims=True) + eps_norm)
    normed = (rows_float * scale * gain_row).astype(jnp.bfloat16)
    micros = here.shape[0]
    normed = normed.reshape(micros, num_experts, CAP, width).transpose(1, 0, 2, 3)
    received = dispatch(normed.reshape(num_experts, micros * CAP, width))
    n_dev = received.shape[0]
    partial = expert_block(received.reshape(-1, width), gate_mat, up_mat, down_mat)
    total = collect(partial.reshape(n_dev, micros * CAP, width), num_experts)
    total = total.astype(jnp.bfloat16).reshape(num_experts, micros, CAP, width)
    total = total.transpose(1, 0, 2, 3).reshape(micros, num_experts * CAP, width)
    return section_exchange([total[k] for k in range(micros)])


def shards_general(embedded, norm_gain, gate_proj, up_proj, down_proj, expert_ids, route_gates):
    n_section = lax.axis_size("section")
    n_dev = lax.axis_size("expert")
    num_experts = n_dev // min(8, n_dev)
    me = lax.axis_index("section")
    base = embedded[0]
    own = slot_weights(expert_ids[0], route_gates[0], num_experts)

    def pick(stacked, index):
        return lax.dynamic_index_in_dim(stacked, index, 0, keepdims=False)

    tables = section_exchange([pick(own, me ^ k) for k in range(n_section)])
    tables = jnp.stack(tables)
    ordered = jnp.stack([pick(tables, me ^ l) for l in range(n_section)])
    chosen = ordered > 0
    picks = jnp.sum(jnp.any(chosen, axis=-1).astype(jnp.int32), axis=0)
    depth = lax.pmax(jnp.max(picks), ("section", "expert"))
    masks = chosen.astype(jnp.bfloat16)

    def take(mask, rows):
        return lax.dot_general(
            mask, rows, (((0,), (0,)), ((), ())), preferred_element_type=jnp.float32
        ).astype(jnp.bfloat16)

    def advance(rows, layer, update):
        routed = jnp.dot(
            ordered[layer],
            update.astype(jnp.float32),
            precision=lax.Precision.HIGHEST,
            preferred_element_type=jnp.float32,
        )
        return (rows.astype(jnp.float32) + routed).astype(jnp.bfloat16)

    def one_round(inputs):
        sent = [pick(inputs, me ^ k) for k in range(n_section)]
        got = jnp.stack(
            layer_round(sent, norm_gain[0], gate_proj[0], up_proj[0], down_proj[0], num_experts)
        )
        return jnp.stack([pick(got, me ^ l) for l in range(n_section)])

    def body(state):
        count, updates = state
        rows, inputs = base, []
        for layer in range(n_section):
            inputs.append(take(masks[layer], rows))
            if layer < n_section - 1:
                rows = advance(rows, layer, updates[layer])
        return count + 1, one_round(jnp.stack(inputs))

    first = jnp.stack([take(masks[layer], base) for layer in range(n_section)])
    updates = one_round(first)
    _, updates = lax.while_loop(lambda s: s[0] < depth, body, (jnp.int32(1), updates))
    rows = base
    for layer in range(n_section):
        rows = advance(rows, layer, updates[layer])
    return rows[None]


LANES = 128
SECTIONS = 4
STRIP = 1024
PACK = 4
FEW = 2
BF16 = jnp.bfloat16
F32 = jnp.float32


def normalise(squares, kept, gain, normed_out):
    width = kept.shape[1]
    mean = jnp.sum(squares, axis=-1, keepdims=True) * (1.0 / width)
    scale = lax.rsqrt(mean + eps_norm)
    for start in range(0, width, STRIP):
        span = pl.ds(start, STRIP)
        value = kept[:, span] * scale * gain[:, span]
        normed_out[:, span] = value[: normed_out.shape[0]].astype(BF16)


def before(values):
    total = values
    for by in (1, 2, 4):
        total = total + pltpu.roll(total, by, 1)
    return total - values


def slot_code(value):
    return (value & (SECTIONS * CAP - 1)) // CAP


def slot_tables(gates, parts_out, picks, picks_relayed, hits_out, table):
    me = lax.axis_index("section")
    micros, _, tokens = gates.shape
    slots = micros * CAP
    row = lax.broadcasted_iota(jnp.int32, (tokens, tokens), 0)
    column = lax.broadcasted_iota(jnp.int32, (tokens, tokens), 1)
    ahead = jnp.where(row < column, 1.0, 0.0).astype(BF16)
    table[...] = jnp.zeros(table.shape, F32)
    hits = jnp.zeros((tokens, tokens), F32)
    for m in range(micros):
        weight = jnp.sum(gates[m], axis=0, keepdims=True)
        hit = jnp.where(weight > 0, 1.0, 0.0)
        hit = jnp.broadcast_to(hit, (tokens, tokens))
        slot = jnp.dot(hit.astype(BF16), ahead, preferred_element_type=F32).astype(jnp.int32)
        spot = (hit > 0) & (row == m * CAP + slot) & (slot < CAP)
        hits = jnp.where(spot, 1.0, hits)
        for q in range(CAP):
            chosen = (hit[:1] > 0) & (slot[:1] == q)
            value = jnp.where(chosen, weight, 0.0)
            high = value.astype(BF16).astype(F32)
            middle = (value - high).astype(BF16).astype(F32)
            at = m * CAP + q
            table[pl.ds(at, 1)] = high
            table[pl.ds(at + slots, 1)] = middle
            table[pl.ds(at + 2 * slots, 1)] = value - high - middle
    contract = (((1,), (1,)), ((), ()))
    same = jnp.where(row == column, 1.0, 0.0).astype(BF16)
    parts_out[...] = lax.dot_general(
        same, table[...].astype(BF16), contract, preferred_element_type=F32
    ).astype(BF16)
    hits = hits.astype(BF16)
    hits_out[...] = hits
    sums = jnp.dot(
        jnp.where(column < row, 1.0, 0.0).astype(BF16), hits, preferred_element_type=F32
    )
    order = lax.dot_general(
        jnp.ones((tokens, tokens), BF16), sums.astype(BF16), contract, preferred_element_type=F32
    ).astype(jnp.int32)
    filled = lax.dot_general(
        jnp.ones((tokens, tokens), BF16), hits, contract, preferred_element_type=F32
    )
    wanted = (row == column) | ((row >= slots) & (row < slots + PACK) & (order == row - slots))
    wanted = wanted & (column < slots)
    for j in range(SECTIONS - 1):
        mine = wanted & (slot_code(column) == (me ^ j))
        picks[j] = jnp.dot(
            jnp.where(mine, 1.0, 0.0).astype(BF16), hits, preferred_element_type=F32
        ).astype(BF16)
    mine = wanted & (slot_code(column) == (me ^ (SECTIONS - 1)))
    picks_relayed[...] = jnp.where(mine, filled, 0.0)


def stage(after, gain, embedded, gain_out, x_out):
    gain_out[...] = gain[...]
    x_out[...] = embedded[0]


def relay(table, table_two, rows, gain, out):
    me = lax.axis_index("section")
    width = rows.shape[1]
    row = lax.broadcasted_iota(jnp.int32, (8, LANES), 0)
    lane = lax.broadcasted_iota(jnp.int32, (8, LANES), 1)
    wanted = (lane == (me ^ 2) * CAP + row) & (row < CAP)
    chosen = jnp.where(table[...].astype(F32) > 0, 1.0, 0.0).astype(BF16)
    pick = lax.dot_general(
        jnp.where(wanted, 1.0, 0.0).astype(BF16),
        chosen,
        (((1,), (1,)), ((), ())),
        preferred_element_type=F32,
    ).astype(BF16)
    for start in range(0, width, STRIP):
        span = pl.ds(start, STRIP)
        value = jnp.dot(pick, rows[:, span], preferred_element_type=F32)
        out[:, span] = value[:CAP].astype(BF16)
    extra = table_two[...].astype(F32)
    for t in range(extra.shape[0]):
        line = jnp.broadcast_to(extra[t : t + 1], (CAP, LANES))
        out[:, pl.ds(width + t * LANES, LANES)] = line.astype(BF16)


def prepare_first(
    picks, picks_relayed, own_hits, x0, x1, x2, relayed, t0, t1, t2, gain, rows_out,
    normed_out, group_out, rank_out, linear_out, kept, last,
):
    me = lax.axis_index("section")
    inputs = (x0, x1, x2)
    slots, width = rows_out.shape
    for t in range(last.shape[0]):
        last[pl.ds(t, 1)] = relayed[:, pl.ds(width + t * LANES, LANES)].astype(F32)[:1]
    tables = (t0, t1, t2, last)
    far_column = lax.broadcasted_iota(jnp.int32, picks_relayed.shape, 1)
    far = [
        jnp.sum(
            jnp.where((far_column & (CAP - 1)) == q, picks_relayed[...], 0.0), axis=1, keepdims=True
        )
        for q in range(CAP)
    ]
    total = 0.0
    for start in range(0, width, STRIP):
        span = pl.ds(start, STRIP)
        rows = sum(
            jnp.dot(picks[j], inputs[j][:, span], preferred_element_type=F32)
            for j in range(SECTIONS - 1)
        )
        extra = relayed[:, span].astype(F32)
        rows = rows + sum(far[q] * extra[q : q + 1] for q in range(CAP))
        rows_out[:, span] = rows[:slots].astype(BF16)
        packed = rows[slots:]
        kept[:, span] = packed
        total += packed * packed
    normalise(total, kept, gain, normed_out)

    lane = lax.broadcasted_iota(jnp.int32, (x0.shape[0], LANES), 1)
    hits = [
        jnp.where((lane < slots) & (t[...].astype(F32) > 0), 1.0, 0.0) for t in tables
    ]
    pairs = [
        h + jnp.where(lane % CAP == 0, pltpu.roll(h, LANES - 1, 1), pltpu.roll(h, 1, 1))
        for h in hits
    ]
    largest = [jnp.zeros((1, 1), F32) for _ in range(SECTIONS)]
    for j in range(SECTIONS):
        mine = me ^ j
        level = jnp.zeros_like(hits[0])
        for other in range(SECTIONS):
            if other != j:
                level += pairs[other] * jnp.where((me ^ other) < mine, 1.0, 0.0)
        filled = jnp.sum(hits[j], axis=0, keepdims=True)
        level = jnp.sum(hits[j] * level, axis=0, keepdims=True)
        order = before(filled)
        late = jnp.where((level == 0) & (order >= PACK), filled, 0.0)
        group = jnp.where(filled > 0, jnp.where(level > 0, level, late - 1.0), -2.0)
        rank = order
        for g in range(SECTIONS):
            member = jnp.where(group == g, 1.0, 0.0)
            rank = jnp.where(group == g, before(member), rank)
            size = jnp.sum(member, axis=1, keepdims=True)
            largest[g] = jnp.maximum(largest[g], size)
        group_out[pl.ds(j, 1)] = group
        rank_out[pl.ds(j, 1)] = rank
    sizes = jnp.zeros((PACK, LANES), F32)
    spot = lax.broadcasted_iota(jnp.int32, (PACK, LANES), 1)
    for g in range(SECTIONS):
        sizes = jnp.where(spot == g, largest[g], sizes)
    normed_out[:, width:] = sizes.astype(BF16)

    span = 3 * slots
    table = jnp.zeros(lane.shape, F32)
    sooner = jnp.zeros(own_hits.shape[:1] + (LANES,), F32)
    row = lax.broadcasted_iota(jnp.int32, sooner.shape, 0)
    column = lax.broadcasted_iota(jnp.int32, sooner.shape, 1)
    for j in range(SECTIONS):
        part = jnp.where(lane < span, tables[j][...].astype(F32), 0.0)
        table = table + (pltpu.roll(part, j * span, 1) if j else part)
        inside = (column >= j * span) & (column < (j + 1) * span)
        sooner = jnp.where(inside, jnp.where((me ^ j) < me, 1.0, 0.0), sooner)
    inner = jnp.dot(own_hits[...], table.astype(BF16), preferred_element_type=F32)
    inner = jnp.where(row // CAP == slot_code(column), inner * sooner, 0.0)
    tokens = lane.shape[0]
    linear_out[:tokens] = jnp.where(slot_code(lane) == me, table, 0.0).astype(BF16)
    linear_out[tokens:] = inner.astype(BF16)


def schedule(near, far, group, rank, codes_out, line_out, rounds_out, few_out, base_out):
    width = near.shape[1] - LANES
    slots = SECTIONS * CAP
    sizes = jnp.maximum(
        jnp.max(near[:, width:].astype(F32), axis=0, keepdims=True),
        jnp.max(far[:, width:].astype(F32), axis=0, keepdims=True),
    )
    lane = lax.broadcasted_iota(jnp.int32, sizes.shape, 1)
    largest = jnp.max(jnp.where(lane < SECTIONS, sizes, 0.0), axis=1, keepdims=True)
    few = largest <= FEW
    count = jnp.where(few, float(FEW), float(PACK))
    code = jnp.where(group[...] < -1, 0.0, rank[...] + 1)
    start = jnp.ones((1, 1), F32)
    for g in range(SECTIONS):
        place = PACK + (start - 1) * count + rank[...] + 1
        code = jnp.where(group[...] == g, place, code)
        size = jnp.sum(jnp.where(lane == g, sizes, 0.0), axis=1, keepdims=True)
        start = start + jnp.floor((size + (count - 1)) / count)
    rounds_out[0] = jnp.max(jnp.where(few, 0.0, start)).astype(jnp.int32)
    few_out[0] = jnp.max(jnp.where(few, start, 0.0)).astype(jnp.int32)
    base_out[...] = jnp.zeros(base_out.shape, F32)
    span = 3 * slots
    line = jnp.zeros(sizes.shape, F32)
    for j in range(SECTIONS):
        own = jnp.where(lane < slots, code[j : j + 1], 0.0)
        for part in range(3):
            shift = j * span + part * slots
            line = line + (pltpu.roll(own, shift, 1) if shift else own)
    line_out[...] = line
    eye = lax.broadcasted_iota(jnp.int32, (LANES, LANES), 0) == lax.broadcasted_iota(
        jnp.int32, (LANES, LANES), 1
    )
    turned = lax.dot_general(
        jnp.where(eye, 1.0, 0.0).astype(BF16),
        jnp.broadcast_to(line, (SECTIONS * PACK, LANES)).astype(BF16),
        (((1,), (1,)), ((), ())),
        preferred_element_type=F32,
    )
    row = lax.broadcasted_iota(jnp.int32, turned.shape, 0)
    column = lax.broadcasted_iota(jnp.int32, turned.shape, 1)
    for part in range(3):
        kept = jnp.zeros(turned.shape, F32)
        for j in range(SECTIONS):
            low = j * span + part * slots
            block = (row >= low) & (row < low + slots) & (column // PACK == j)
            kept = jnp.where(block, turned, kept)
        codes_out[part] = kept


def arrived(base, codes, linear, updates, held):
    for j, update in enumerate(updates):
        held[pl.ds(j * PACK, PACK)] = update[...].astype(F32)
    spot = lax.broadcasted_iota(jnp.int32, codes.shape[1:], 1)
    wanted = base + (1 + (spot & (PACK - 1))).astype(F32)
    coefs = []
    for part in range(3):
        chosen = jnp.where(codes[part] == wanted, 1.0, 0.0).astype(BF16)
        coefs.append(jnp.dot(linear[...], chosen, preferred_element_type=F32))
    return jnp.concatenate(coefs, axis=0).astype(BF16)


def changes(coefs, held, span):
    result = jnp.dot(coefs, held[:, span].astype(BF16), preferred_element_type=F32)
    third = coefs.shape[0] // 3
    return result[:third] + result[third : 2 * third] + result[2 * third :]


def following(base, count):
    return jnp.where(base < PACK, float(PACK), base + count)


def next_rows(base, codes, line, linear, y, u0, u1, u2, u3, gain, normed_out, held, kept):
    coefs = arrived(base[:, :1], codes, linear, (u0, u1, u2, u3), held)
    slots, width = y.shape
    spot = lax.broadcasted_iota(jnp.int32, (2 * PACK, slots), 0)
    count = normed_out.shape[0]
    wanted = following(base[:, :1], count) + (1 + spot).astype(F32)
    pick = jnp.where((line[:, :slots] == wanted) & (spot < count), 1.0, 0.0).astype(BF16)
    third = coefs.shape[0] // 3
    first = third // 2
    mine = [coefs[i * third + first : i * third + first + slots] for i in range(3)]
    mine = jnp.concatenate(
        [jnp.dot(pick, part, preferred_element_type=F32) for part in mine], axis=0
    ).astype(BF16)
    total = 0.0
    for start in range(0, width, STRIP):
        span = pl.ds(start, STRIP)
        rows = jnp.dot(pick, y[:, span], preferred_element_type=F32) + changes(mine, held, span)
        rows = rows.astype(BF16).astype(F32)
        kept[:, span] = rows
        total += rows * rows
    normalise(total, kept, gain, normed_out)


def absorb(count, base, codes, linear, x, y, u0, u1, u2, u3, base_out, x_out, y_out, held):
    base_out[...] = following(base[...], count)
    coefs = arrived(base[:, :1], codes, linear, (u0, u1, u2, u3), held)
    tokens, width = x.shape
    slots = y.shape[0]
    for start in range(0, width, STRIP):
        span = pl.ds(start, STRIP)
        change = changes(coefs, held, span)
        x_out[:, span] = (x[:, span].astype(F32) + change[:tokens]).astype(BF16)
        y_out[:, span] = (y[:, span].astype(F32) + change[tokens : tokens + slots]).astype(BF16)


def finish(base, codes, linear, x, u0, u1, u2, u3, out, held):
    coefs = arrived(base[:, :1], codes, linear, (u0, u1, u2, u3), held)
    tokens, width = x.shape
    for start in range(0, width, STRIP):
        span = pl.ds(start, STRIP)
        change = changes(coefs, held, span)
        out[0, :, span] = (x[:, span].astype(F32) + change[:tokens]).astype(BF16)


def expert_kernel(near, far, gate, up, down, near_out, far_out, rows):
    half, width = near_out.shape
    if half % 16:
        for start in range(0, width, STRIP):
            span = pl.ds(start, STRIP)
            both = [near[:, span].astype(F32), far[:, span].astype(F32)]
            rows[:, span] = jnp.concatenate(both, axis=0).astype(BF16)
    else:
        rows[:half] = near[:, :width]
        rows[half:] = far[:, :width]
    gate_val = jnp.dot(rows[...], gate[0], preferred_element_type=F32)
    up_val = jnp.dot(rows[...], up[0], preferred_element_type=F32)
    hidden = (gate_val * jax.nn.sigmoid(gate_val) * up_val).astype(BF16)
    for start in range(0, width, STRIP):
        span = pl.ds(start, STRIP)
        value = jnp.dot(hidden, down[0, :, span], preferred_element_type=F32)
        near_out[:, span] = value[:half].astype(BF16)
        far_out[:, span] = value[half:].astype(BF16)


def hold_kernel(*refs):
    count = len(refs) // 2
    inputs, outputs, sems = refs[:count], refs[count : 2 * count], refs[-1]
    copies = [
        pltpu.make_async_copy(inputs[i], outputs[i], sems.at[i]) for i in range(count - 1)
    ]
    for copy in copies:
        copy.start()
    outputs[-1][...] = inputs[-1][...]
    for copy in copies:
        copy.wait()


VMEM = pl.BlockSpec(memory_space=pltpu.VMEM)
HBM = pl.BlockSpec(memory_space=pltpu.HBM)
PARAMS = pltpu.CompilerParams(vmem_limit_bytes=16 * 2**20)


def expert_call(near, far, gate, up, down):
    half = near.shape[0]
    _, width, hidden = gate.shape
    out = jax.ShapeDtypeStruct((half, width), BF16)
    return pl.pallas_call(
        expert_kernel,
        out_shape=(out, out),
        in_specs=[VMEM] * 5,
        out_specs=(VMEM, VMEM),
        scratch_shapes=[pltpu.VMEM((2 * half, width), BF16)],
        compiler_params=PARAMS,
        cost_estimate=pl.CostEstimate(
            flops=12 * half * width * hidden,
            bytes_accessed=6 * width * hidden,
            transcendentals=2 * half * hidden,
        ),
        name="experts",
    )(near, far, gate, up, down)


def hold_weights(rows, *weights, after=()):
    operands = weights + (rows,)
    return pl.pallas_call(
        lambda *refs: hold_kernel(*refs[: len(operands)], *refs[len(operands) + len(after) :]),
        out_shape=tuple(jax.ShapeDtypeStruct(w.shape, w.dtype) for w in operands),
        in_specs=[HBM] * len(weights) + [VMEM] * (1 + len(after)),
        out_specs=(VMEM,) * len(operands),
        scratch_shapes=[pltpu.SemaphoreType.DMA((len(weights),))],
        compiler_params=pltpu.CompilerParams(vmem_limit_bytes=52 * 2**20),
        cost_estimate=pl.CostEstimate(
            flops=0, bytes_accessed=4 * sum(w.size for w in weights), transcendentals=0
        ),
        name="hold_weights",
    )(*operands, *after)


def spread(array):
    return [array] + [swap(array, "section", j) for j in range(1, 4)]


def group_rows(normed, own, order):
    near = jnp.concatenate([own] + [swap(normed, "expert", 2 * k) for k in order])
    return near, swap(near, "expert", 1)


def group_sum(near, far, order, sums):
    other = swap(far, "expert", 1)
    both = (near.astype(F32) + other.astype(F32)).astype(BF16)
    count = both.shape[0] // 4
    parts = {k: both[i * count : (i + 1) * count] for i, k in enumerate((0, *order))}
    total = parts[0].astype(F32)
    for k in sums:
        total = total + swap(parts[k], "expert", 2 * k).astype(F32)
    return jnp.pad(total.astype(BF16), ((0, PACK - count), (0, 0)))


def shards_group(embedded, norm_gain, gate_proj, up_proj, down_proj, expert_ids, route_gates):
    tokens, width = embedded.shape[1:]
    slots = expert_ids.shape[1] * CAP
    picked = slots + 2 * PACK

    def shape(dims, kind=BF16):
        return jax.ShapeDtypeStruct(dims, kind)

    def call(kernel, outs, ins, scratch=(), in_specs=None, out_specs=None):
        return pl.pallas_call(
            kernel,
            out_shape=outs,
            in_specs=in_specs or [VMEM] * len(ins),
            out_specs=out_specs or jax.tree.map(lambda _: VMEM, outs),
            scratch_shapes=scratch,
            compiler_params=PARAMS,
            name=getattr(kernel, "func", kernel).__name__,
        )(*ins)

    x_near = [swap(embedded[0], "section", j) for j in (1, 2)]
    gates = jnp.where(expert_ids[0] < 1, route_gates[0], 0.0).transpose(0, 2, 1)
    parts, picks, picks_relayed, hits = call(
        slot_tables,
        (
            shape((tokens, LANES)),
            shape((SECTIONS - 1, picked, tokens)),
            shape((picked, tokens), F32),
            shape((picked, tokens)),
        ),
        (gates,),
        [pltpu.VMEM((LANES, tokens), F32)],
    )
    tables = [parts] + [swap(parts, "section", j) for j in (1, 2)]
    gain, x = call(
        stage,
        (shape(norm_gain.shape, F32), shape((tokens, width))),
        (parts, norm_gain, embedded),
    )
    relayed = call(
        relay, shape((CAP, width + tokens * LANES)), (tables[1], tables[2], x_near[1], gain)
    )
    down, gain = hold_weights(gain, down_proj, after=(relayed,))
    relayed = swap(relayed, "section", 1)
    y, normed, group, rank, linear = call(
        prepare_first,
        (
            shape((slots, width)),
            shape((PACK, width + LANES)),
            shape((SECTIONS, LANES), F32),
            shape((SECTIONS, LANES), F32),
            shape((tokens + picked, LANES)),
        ),
        (picks, picks_relayed, hits, x, *x_near, relayed, *tables, gain),
        [pltpu.VMEM((2 * PACK, width), F32), pltpu.VMEM((tokens, LANES), F32)],
    )
    gate, up, own = hold_weights(normed, gate_proj, up_proj)

    def rest(normed, own, order, sums):
        near, far = group_rows(normed, own, order)
        near_part, far_part = expert_call(near, far, gate, up, down)
        return near, far, tuple(spread(group_sum(near_part, far_part, order, sums)))

    near, far, updates = rest(normed, own, (1, 2, 3), (3, 1, 2))
    number = pl.BlockSpec(memory_space=pltpu.SMEM)
    codes, line, rounds, few_rounds, base = call(
        schedule,
        (
            shape((3, LANES, SECTIONS * PACK), F32),
            shape((1, LANES), F32),
            shape((1,), jnp.int32),
            shape((1,), jnp.int32),
            shape((1, LANES), F32),
        ),
        (near, far, group, rank),
        out_specs=(VMEM, VMEM, number, number, VMEM),
    )
    held = pltpu.VMEM((SECTIONS * PACK, width), F32)

    def body(count, state):
        done, base, x, y, updates = state
        normed = call(
            next_rows,
            shape((count, width)),
            (base, codes, line, linear, y, *updates, gain),
            [held, pltpu.VMEM((2 * PACK, width), F32)],
        )
        base, x, y = call(
            functools.partial(absorb, count),
            (shape((1, LANES), F32), shape((tokens, width)), shape((slots, width))),
            (base, codes, linear, x, y, *updates),
            [held],
        )
        return done + 1, base, x, y, rest(normed, normed, (3, 2, 1), (1, 2, 3))[2]

    state = (jnp.ones((1,), jnp.int32), base, x, y, updates)
    for count, limit in ((FEW, jnp.maximum(few_rounds, 1)), (PACK, jnp.maximum(rounds, 1))):
        state = lax.while_loop(
            functools.partial(lambda limit, s: s[0][0] < limit[0], limit),
            functools.partial(body, count),
            state,
        )
    _, base, x, _, updates = state
    return call(finish, shape(embedded.shape), (base, codes, linear, x, *updates), [held])


def solution(mesh):
    placed = (
        P("section", "expert", None),
        P("section", None),
        P("section", None, "expert"),
        P("section", None, "expert"),
        P("section", "expert", None),
        P("section", None, "expert", None),
        P("section", None, "expert", None),
    )
    fits = mesh.shape["expert"] == 8 and mesh.shape["section"] == 4
    return jax.shard_map(
        shards_group if fits else shards_general, mesh=mesh, in_specs=placed, out_specs=P("section", "expert", None), check_vma=False
    )
```

```python
import functools

import jax
import jax.numpy as jnp
from jax import lax
from jax.experimental import pallas as pl
from jax.experimental.pallas import tpu as pltpu
from jax.sharding import PartitionSpec as P

CAP = 2

eps_norm = 1e-06


def slot_weights(chosen, gates, num_experts):
    expert_range = jnp.arange(num_experts, dtype=jnp.int32)
    matched = (chosen[..., None] == expert_range).astype(jnp.int32)
    hit_table = jnp.sum(matched, axis=-2, dtype=jnp.int32)
    tokens = chosen.shape[-2]
    before = jnp.arange(tokens)[:, None] > jnp.arange(tokens)[None, :]
    earlier = jnp.sum(
        jnp.where(before[:, :, None], hit_table[..., None, :, :], 0), axis=-2, dtype=jnp.int32
    )
    weight = jnp.sum(jnp.where(matched > 0, gates[..., None], 0.0), axis=-2)
    slots = jnp.arange(CAP, dtype=jnp.int32)
    table = jnp.where(earlier[..., None] == slots, weight[..., None], 0.0)
    return table.reshape(table.shape[:-2] + (num_experts * CAP,))


def swap(array, axis, by):
    devices = lax.axis_size(axis)
    return lax.ppermute(array, axis, [(i, i ^ by) for i in range(devices)])


def section_exchange(parts):
    return [parts[0]] + [swap(parts[k], "section", k) for k in range(1, len(parts))]


def dispatch(rows):
    experts, count, width = rows.shape
    n_dev = lax.axis_size("expert")
    send = jnp.repeat(rows, n_dev // experts, axis=0)
    return lax.all_to_all(send, "expert", split_axis=0, concat_axis=0, tiled=True)


def collect(partial, experts):
    n_dev, count, width = partial.shape
    back = lax.all_to_all(partial, "expert", split_axis=0, concat_axis=0, tiled=True)
    back = back.reshape(experts, n_dev // experts, count, width)
    return jnp.sum(back.astype(jnp.float32), axis=1)


def expert_block(rows_in, gate_mat, up_mat, down_mat):
    gate_val = jnp.dot(rows_in, gate_mat, preferred_element_type=jnp.float32)
    up_val = jnp.dot(rows_in, up_mat, preferred_element_type=jnp.float32)
    hidden = (jax.nn.silu(gate_val) * up_val).astype(jnp.bfloat16)
    return jnp.dot(hidden, down_mat, preferred_element_type=jnp.float32).astype(jnp.bfloat16)


def layer_round(sent, gain_row, gate_mat, up_mat, down_mat, num_experts):
    width = sent[0].shape[-1]
    here = jnp.stack(section_exchange(sent))
    rows_float = here.astype(jnp.float32)
    scale = lax.rsqrt(jnp.mean(rows_float * rows_float, axis=-1, keepdims=True) + eps_norm)
    normed = (rows_float * scale * gain_row).astype(jnp.bfloat16)
    micros = here.shape[0]
    normed = normed.reshape(micros, num_experts, CAP, width).transpose(1, 0, 2, 3)
    received = dispatch(normed.reshape(num_experts, micros * CAP, width))
    n_dev = received.shape[0]
    partial = expert_block(received.reshape(-1, width), gate_mat, up_mat, down_mat)
    total = collect(partial.reshape(n_dev, micros * CAP, width), num_experts)
    total = total.astype(jnp.bfloat16).reshape(num_experts, micros, CAP, width)
    total = total.transpose(1, 0, 2, 3).reshape(micros, num_experts * CAP, width)
    return section_exchange([total[k] for k in range(micros)])


def shards_general(embedded, norm_gain, gate_proj, up_proj, down_proj, expert_ids, route_gates):
    n_section = lax.axis_size("section")
    n_dev = lax.axis_size("expert")
    num_experts = n_dev // min(8, n_dev)
    me = lax.axis_index("section")
    base = embedded[0]
    own = slot_weights(expert_ids[0], route_gates[0], num_experts)

    def pick(stacked, index):
        return lax.dynamic_index_in_dim(stacked, index, 0, keepdims=False)

    tables = section_exchange([pick(own, me ^ k) for k in range(n_section)])
    tables = jnp.stack(tables)
    ordered = jnp.stack([pick(tables, me ^ l) for l in range(n_section)])
    chosen = ordered > 0
    picks = jnp.sum(jnp.any(chosen, axis=-1).astype(jnp.int32), axis=0)
    depth = lax.pmax(jnp.max(picks), ("section", "expert"))
    masks = chosen.astype(jnp.bfloat16)

    def take(mask, rows):
        return lax.dot_general(
            mask, rows, (((0,), (0,)), ((), ())), preferred_element_type=jnp.float32
        ).astype(jnp.bfloat16)

    def advance(rows, layer, update):
        routed = jnp.dot(
            ordered[layer],
            update.astype(jnp.float32),
            precision=lax.Precision.HIGHEST,
            preferred_element_type=jnp.float32,
        )
        return (rows.astype(jnp.float32) + routed).astype(jnp.bfloat16)

    def one_round(inputs):
        sent = [pick(inputs, me ^ k) for k in range(n_section)]
        got = jnp.stack(
            layer_round(sent, norm_gain[0], gate_proj[0], up_proj[0], down_proj[0], num_experts)
        )
        return jnp.stack([pick(got, me ^ l) for l in range(n_section)])

    def body(state):
        count, updates = state
        rows, inputs = base, []
        for layer in range(n_section):
            inputs.append(take(masks[layer], rows))
            if layer < n_section - 1:
                rows = advance(rows, layer, updates[layer])
        return count + 1, one_round(jnp.stack(inputs))

    first = jnp.stack([take(masks[layer], base) for layer in range(n_section)])
    updates = one_round(first)
    _, updates = lax.while_loop(lambda s: s[0] < depth, body, (jnp.int32(1), updates))
    rows = base
    for layer in range(n_section):
        rows = advance(rows, layer, updates[layer])
    return rows[None]


LANES = 128
SECTIONS = 4
STRIP = 1024
PACK = 4
FEW = 2
BF16 = jnp.bfloat16
F32 = jnp.float32


def normalise(squares, kept, gain, normed_out):
    width = kept.shape[1]
    mean = jnp.sum(squares, axis=-1, keepdims=True) * (1.0 / width)
    scale = lax.rsqrt(mean + eps_norm)
    for start in range(0, width, STRIP):
        span = pl.ds(start, STRIP)
        value = kept[:, span] * scale * gain[:, span]
        normed_out[:, span] = value[: normed_out.shape[0]].astype(BF16)


def before(values):
    total = values
    for by in (1, 2, 4):
        total = total + pltpu.roll(total, by, 1)
    return total - values


def slot_code(value):
    return (value & (SECTIONS * CAP - 1)) // CAP


def slot_tables(gates, parts_out, picks, picks_relayed, hits_out, table):
    me = lax.axis_index("section")
    micros, _, tokens = gates.shape
    slots = micros * CAP
    row = lax.broadcasted_iota(jnp.int32, (tokens, tokens), 0)
    column = lax.broadcasted_iota(jnp.int32, (tokens, tokens), 1)
    ahead = jnp.where(row < column, 1.0, 0.0).astype(BF16)
    table[...] = jnp.zeros(table.shape, F32)
    hits = jnp.zeros((tokens, tokens), F32)
    for m in range(micros):
        weight = jnp.sum(gates[m], axis=0, keepdims=True)
        hit = jnp.where(weight > 0, 1.0, 0.0)
        hit = jnp.broadcast_to(hit, (tokens, tokens))
        slot = jnp.dot(hit.astype(BF16), ahead, preferred_element_type=F32).astype(jnp.int32)
        spot = (hit > 0) & (row == m * CAP + slot) & (slot < CAP)
        hits = jnp.where(spot, 1.0, hits)
        for q in range(CAP):
            chosen = (hit[:1] > 0) & (slot[:1] == q)
            value = jnp.where(chosen, weight, 0.0)
            high = value.astype(BF16).astype(F32)
            middle = (value - high).astype(BF16).astype(F32)
            at = m * CAP + q
            table[pl.ds(at, 1)] = high
            table[pl.ds(at + slots, 1)] = middle
            table[pl.ds(at + 2 * slots, 1)] = value - high - middle
    contract = (((1,), (1,)), ((), ()))
    same = jnp.where(row == column, 1.0, 0.0).astype(BF16)
    parts_out[...] = lax.dot_general(
        same, table[...].astype(BF16), contract, preferred_element_type=F32
    ).astype(BF16)
    hits = hits.astype(BF16)
    hits_out[...] = hits
    sums = jnp.dot(
        jnp.where(column < row, 1.0, 0.0).astype(BF16), hits, preferred_element_type=F32
    )
    order = lax.dot_general(
        jnp.ones((tokens, tokens), BF16), sums.astype(BF16), contract, preferred_element_type=F32
    ).astype(jnp.int32)
    filled = lax.dot_general(
        jnp.ones((tokens, tokens), BF16), hits, contract, preferred_element_type=F32
    )
    wanted = (row == column) | ((row >= slots) & (row < slots + PACK) & (order == row - slots))
    wanted = wanted & (column < slots)
    for j in range(SECTIONS - 1):
        mine = wanted & (slot_code(column) == (me ^ j))
        picks[j] = jnp.dot(
            jnp.where(mine, 1.0, 0.0).astype(BF16), hits, preferred_element_type=F32
        ).astype(BF16)
    mine = wanted & (slot_code(column) == (me ^ (SECTIONS - 1)))
    picks_relayed[...] = jnp.where(mine, filled, 0.0)


def stage(after, gain, embedded, gain_out, x_out):
    gain_out[...] = gain[...]
    x_out[...] = embedded[0]


def relay(table, table_two, rows, gain, out):
    me = lax.axis_index("section")
    width = rows.shape[1]
    row = lax.broadcasted_iota(jnp.int32, (8, LANES), 0)
    lane = lax.broadcasted_iota(jnp.int32, (8, LANES), 1)
    wanted = (lane == (me ^ 2) * CAP + row) & (row < CAP)
    chosen = jnp.where(table[...].astype(F32) > 0, 1.0, 0.0).astype(BF16)
    pick = lax.dot_general(
        jnp.where(wanted, 1.0, 0.0).astype(BF16),
        chosen,
        (((1,), (1,)), ((), ())),
        preferred_element_type=F32,
    ).astype(BF16)
    for start in range(0, width, STRIP):
        span = pl.ds(start, STRIP)
        value = jnp.dot(pick, rows[:, span], preferred_element_type=F32)
        out[:, span] = value[:CAP].astype(BF16)
    extra = table_two[...].astype(F32)
    for t in range(extra.shape[0]):
        line = jnp.broadcast_to(extra[t : t + 1], (CAP, LANES))
        out[:, pl.ds(width + t * LANES, LANES)] = line.astype(BF16)


def prepare_first(
    picks, picks_relayed, own_hits, x0, x1, x2, relayed, t0, t1, t2, gain, rows_out,
    normed_out, group_out, rank_out, linear_out, kept, last,
):
    me = lax.axis_index("section")
    inputs = (x0, x1, x2)
    slots, width = rows_out.shape
    for t in range(last.shape[0]):
        last[pl.ds(t, 1)] = relayed[:, pl.ds(width + t * LANES, LANES)].astype(F32)[:1]
    tables = (t0, t1, t2, last)
    far_column = lax.broadcasted_iota(jnp.int32, picks_relayed.shape, 1)
    far = [
        jnp.sum(
            jnp.where((far_column & (CAP - 1)) == q, picks_relayed[...], 0.0), axis=1, keepdims=True
        )
        for q in range(CAP)
    ]
    total = 0.0
    for start in range(0, width, STRIP):
        span = pl.ds(start, STRIP)
        rows = sum(
            jnp.dot(picks[j], inputs[j][:, span], preferred_element_type=F32)
            for j in range(SECTIONS - 1)
        )
        extra = relayed[:, span].astype(F32)
        rows = rows + sum(far[q] * extra[q : q + 1] for q in range(CAP))
        rows_out[:, span] = rows[:slots].astype(BF16)
        packed = rows[slots:]
        kept[:, span] = packed
        total += packed * packed
    normalise(total, kept, gain, normed_out)

    lane = lax.broadcasted_iota(jnp.int32, (x0.shape[0], LANES), 1)
    hits = [
        jnp.where((lane < slots) & (t[...].astype(F32) > 0), 1.0, 0.0) for t in tables
    ]
    pairs = [
        h + jnp.where(lane % CAP == 0, pltpu.roll(h, LANES - 1, 1), pltpu.roll(h, 1, 1))
        for h in hits
    ]
    largest = [jnp.zeros((1, 1), F32) for _ in range(SECTIONS)]
    for j in range(SECTIONS):
        mine = me ^ j
        level = jnp.zeros_like(hits[0])
        for other in range(SECTIONS):
            if other != j:
                level += pairs[other] * jnp.where((me ^ other) < mine, 1.0, 0.0)
        filled = jnp.sum(hits[j], axis=0, keepdims=True)
        level = jnp.sum(hits[j] * level, axis=0, keepdims=True)
        order = before(filled)
        late = jnp.where((level == 0) & (order >= PACK), filled, 0.0)
        group = jnp.where(filled > 0, jnp.where(level > 0, level, late - 1.0), -2.0)
        rank = order
        for g in range(SECTIONS):
            member = jnp.where(group == g, 1.0, 0.0)
            rank = jnp.where(group == g, before(member), rank)
            size = jnp.sum(member, axis=1, keepdims=True)
            largest[g] = jnp.maximum(largest[g], size)
        group_out[pl.ds(j, 1)] = group
        rank_out[pl.ds(j, 1)] = rank
    sizes = jnp.zeros((PACK, LANES), F32)
    spot = lax.broadcasted_iota(jnp.int32, (PACK, LANES), 1)
    for g in range(SECTIONS):
        sizes = jnp.where(spot == g, largest[g], sizes)
    normed_out[:, width:] = sizes.astype(BF16)

    span = 3 * slots
    table = jnp.zeros(lane.shape, F32)
    sooner = jnp.zeros(own_hits.shape[:1] + (LANES,), F32)
    row = lax.broadcasted_iota(jnp.int32, sooner.shape, 0)
    column = lax.broadcasted_iota(jnp.int32, sooner.shape, 1)
    for j in range(SECTIONS):
        part = jnp.where(lane < span, tables[j][...].astype(F32), 0.0)
        table = table + (pltpu.roll(part, j * span, 1) if j else part)
        inside = (column >= j * span) & (column < (j + 1) * span)
        sooner = jnp.where(inside, jnp.where((me ^ j) < me, 1.0, 0.0), sooner)
    inner = jnp.dot(own_hits[...], table.astype(BF16), preferred_element_type=F32)
    inner = jnp.where(row // CAP == slot_code(column), inner * sooner, 0.0)
    tokens = lane.shape[0]
    linear_out[:tokens] = jnp.where(slot_code(lane) == me, table, 0.0).astype(BF16)
    linear_out[tokens:] = inner.astype(BF16)


def schedule(
    near, far, group, rank, linear, codes_out, line_out, rounds_out, few_out, base_out, coefs_out,
    mine_out, pick_out,
):
    width = near.shape[1] - LANES
    slots = SECTIONS * CAP
    sizes = jnp.maximum(
        jnp.max(near[:, width:].astype(F32), axis=0, keepdims=True),
        jnp.max(far[:, width:].astype(F32), axis=0, keepdims=True),
    )
    lane = lax.broadcasted_iota(jnp.int32, sizes.shape, 1)
    largest = jnp.max(jnp.where(lane < SECTIONS, sizes, 0.0), axis=1, keepdims=True)
    few = largest <= FEW
    count = jnp.where(few, float(FEW), float(PACK))
    code = jnp.where(group[...] < -1, 0.0, rank[...] + 1)
    start = jnp.ones((1, 1), F32)
    for g in range(SECTIONS):
        place = PACK + (start - 1) * count + rank[...] + 1
        code = jnp.where(group[...] == g, place, code)
        size = jnp.sum(jnp.where(lane == g, sizes, 0.0), axis=1, keepdims=True)
        start = start + jnp.floor((size + (count - 1)) / count)
    rounds_out[0] = jnp.max(jnp.where(few, 0.0, start)).astype(jnp.int32)
    few_out[0] = jnp.max(jnp.where(few, start, 0.0)).astype(jnp.int32)
    base_out[...] = jnp.zeros(base_out.shape, F32)
    span = 3 * slots
    line = jnp.zeros(sizes.shape, F32)
    for j in range(SECTIONS):
        own = jnp.where(lane < slots, code[j : j + 1], 0.0)
        for part in range(3):
            shift = j * span + part * slots
            line = line + (pltpu.roll(own, shift, 1) if shift else own)
    line_out[...] = line
    eye = lax.broadcasted_iota(jnp.int32, (LANES, LANES), 0) == lax.broadcasted_iota(
        jnp.int32, (LANES, LANES), 1
    )
    turned = lax.dot_general(
        jnp.where(eye, 1.0, 0.0).astype(BF16),
        jnp.broadcast_to(line, (SECTIONS * PACK, LANES)).astype(BF16),
        (((1,), (1,)), ((), ())),
        preferred_element_type=F32,
    )
    row = lax.broadcasted_iota(jnp.int32, turned.shape, 0)
    column = lax.broadcasted_iota(jnp.int32, turned.shape, 1)
    codes = []
    for part in range(3):
        kept = jnp.zeros(turned.shape, F32)
        for j in range(SECTIONS):
            low = j * span + part * slots
            block = (row >= low) & (row < low + slots) & (column // PACK == j)
            kept = jnp.where(block, turned, kept)
        codes_out[part] = kept
        codes.append(kept)
    coefs_out[...], mine_out[...], pick_out[...] = plan(
        jnp.zeros((1, 1), F32), count, codes, line, linear, slots
    )


def following(base, count):
    return jnp.where(base < PACK, float(PACK), base + count)


def plan(base, count, codes, line, linear, slots):
    spot = lax.broadcasted_iota(jnp.int32, codes[0].shape, 1)
    wanted = base + (1 + (spot & (PACK - 1))).astype(F32)
    coefs = []
    for part in range(3):
        chosen = jnp.where(codes[part] == wanted, 1.0, 0.0).astype(BF16)
        coefs.append(jnp.dot(linear[...], chosen, preferred_element_type=F32))
    spot = lax.broadcasted_iota(jnp.int32, (2 * PACK, slots), 0)
    wanted = following(base, count) + (1 + spot).astype(F32)
    pick = jnp.where((line[:, :slots] == wanted) & (spot < count), 1.0, 0.0)
    first = linear.shape[0] // 2
    mine = [
        jnp.dot(
            pick.astype(BF16),
            part[first : first + slots].astype(BF16),
            preferred_element_type=F32,
        )
        for part in coefs
    ]
    return jnp.concatenate(coefs, axis=0).astype(BF16), jnp.concatenate(mine, axis=0), pick


def gather(updates, held):
    for j, update in enumerate(updates):
        held[pl.ds(j * PACK, PACK)] = update[...].astype(F32)


def changes(coefs, held, span):
    result = jnp.dot(coefs, held[:, span].astype(BF16), preferred_element_type=F32)
    third = coefs.shape[0] // 3
    return result[:third] + result[third : 2 * third] + result[2 * third :]


def next_rows(mine, pick, y, u0, u1, u2, u3, gain, normed_out, held, kept):
    gather((u0, u1, u2, u3), held)
    chosen = pick[...].astype(BF16)
    coefs = mine[...].astype(BF16)
    total = 0.0
    for start in range(0, y.shape[1], STRIP):
        span = pl.ds(start, STRIP)
        rows = jnp.dot(chosen, y[:, span], preferred_element_type=F32)
        rows = (rows + changes(coefs, held, span)).astype(BF16).astype(F32)
        kept[:, span] = rows
        total += rows * rows
    normalise(total, kept, gain, normed_out)


def absorb(
    count, base, coefs, codes, line, linear, x, y, u0, u1, u2, u3, base_out, coefs_out, mine_out,
    pick_out, x_out, y_out, held,
):
    gather((u0, u1, u2, u3), held)
    tokens, width = x.shape
    slots = y.shape[0]
    known = coefs[...]
    for start in range(0, width, STRIP):
        span = pl.ds(start, STRIP)
        change = changes(known, held, span)
        x_out[:, span] = (x[:, span].astype(F32) + change[:tokens]).astype(BF16)
        y_out[:, span] = (y[:, span].astype(F32) + change[tokens : tokens + slots]).astype(BF16)
    after = following(base[...], count)
    base_out[...] = after
    parts = [codes[part] for part in range(3)]
    coefs_out[...], mine_out[...], pick_out[...] = plan(
        after[:, :1], count, parts, line, linear, slots
    )


def finish(coefs, x, u0, u1, u2, u3, out, held):
    gather((u0, u1, u2, u3), held)
    tokens, width = x.shape
    third = coefs.shape[0] // 3
    known = jnp.concatenate([coefs[pl.ds(i * third, tokens)] for i in range(3)], axis=0)
    for start in range(0, width, STRIP):
        span = pl.ds(start, STRIP)
        out[0, :, span] = (x[:, span].astype(F32) + changes(known, held, span)).astype(BF16)


def expert_kernel(near, far, gate, up, down, near_out, far_out, rows):
    half, width = near_out.shape
    if half % 16:
        for start in range(0, width, STRIP):
            span = pl.ds(start, STRIP)
            both = [near[:, span].astype(F32), far[:, span].astype(F32)]
            rows[:, span] = jnp.concatenate(both, axis=0).astype(BF16)
    else:
        rows[:half] = near[:, :width]
        rows[half:] = far[:, :width]
    gate_val = jnp.dot(rows[...], gate[0], preferred_element_type=F32)
    up_val = jnp.dot(rows[...], up[0], preferred_element_type=F32)
    hidden = (gate_val * jax.nn.sigmoid(gate_val) * up_val).astype(BF16)
    for start in range(0, width, STRIP):
        span = pl.ds(start, STRIP)
        value = jnp.dot(hidden, down[0, :, span], preferred_element_type=F32)
        near_out[:, span] = value[:half].astype(BF16)
        far_out[:, span] = value[half:].astype(BF16)


def hold_kernel(*refs):
    count = len(refs) // 2
    inputs, outputs, sems = refs[:count], refs[count : 2 * count], refs[-1]
    copies = [
        pltpu.make_async_copy(inputs[i], outputs[i], sems.at[i]) for i in range(count - 1)
    ]
    for copy in copies:
        copy.start()
    outputs[-1][...] = inputs[-1][...]
    for copy in copies:
        copy.wait()


VMEM = pl.BlockSpec(memory_space=pltpu.VMEM)
HBM = pl.BlockSpec(memory_space=pltpu.HBM)
PARAMS = pltpu.CompilerParams(vmem_limit_bytes=16 * 2**20)


def expert_call(near, far, gate, up, down):
    half = near.shape[0]
    _, width, hidden = gate.shape
    out = jax.ShapeDtypeStruct((half, width), BF16)
    return pl.pallas_call(
        expert_kernel,
        out_shape=(out, out),
        in_specs=[VMEM] * 5,
        out_specs=(VMEM, VMEM),
        scratch_shapes=[pltpu.VMEM((2 * half, width), BF16)],
        compiler_params=PARAMS,
        cost_estimate=pl.CostEstimate(
            flops=12 * half * width * hidden,
            bytes_accessed=6 * width * hidden,
            transcendentals=2 * half * hidden,
        ),
        name="experts",
    )(near, far, gate, up, down)


def hold_weights(rows, *weights, after=()):
    operands = weights + (rows,)
    return pl.pallas_call(
        lambda *refs: hold_kernel(*refs[: len(operands)], *refs[len(operands) + len(after) :]),
        out_shape=tuple(jax.ShapeDtypeStruct(w.shape, w.dtype) for w in operands),
        in_specs=[HBM] * len(weights) + [VMEM] * (1 + len(after)),
        out_specs=(VMEM,) * len(operands),
        scratch_shapes=[pltpu.SemaphoreType.DMA((len(weights),))],
        compiler_params=pltpu.CompilerParams(vmem_limit_bytes=52 * 2**20),
        cost_estimate=pl.CostEstimate(
            flops=0, bytes_accessed=4 * sum(w.size for w in weights), transcendentals=0
        ),
        name="hold_weights",
    )(*operands, *after)


def spread(array):
    return [array] + [swap(array, "section", j) for j in range(1, 4)]


def group_rows(normed, own, order):
    near = jnp.concatenate([own] + [swap(normed, "expert", 2 * k) for k in order])
    return near, swap(near, "expert", 1)


def group_sum(near, far, order, sums):
    other = swap(far, "expert", 1)
    both = (near.astype(F32) + other.astype(F32)).astype(BF16)
    count = both.shape[0] // 4
    parts = {k: both[i * count : (i + 1) * count] for i, k in enumerate((0, *order))}
    total = parts[0].astype(F32)
    for k in sums:
        total = total + swap(parts[k], "expert", 2 * k).astype(F32)
    return total.astype(BF16)


def shards_group(embedded, norm_gain, gate_proj, up_proj, down_proj, expert_ids, route_gates):
    tokens, width = embedded.shape[1:]
    slots = expert_ids.shape[1] * CAP
    picked = slots + 2 * PACK

    def shape(dims, kind=BF16):
        return jax.ShapeDtypeStruct(dims, kind)

    def call(kernel, outs, ins, scratch=(), in_specs=None, out_specs=None):
        return pl.pallas_call(
            kernel,
            out_shape=outs,
            in_specs=in_specs or [VMEM] * len(ins),
            out_specs=out_specs or jax.tree.map(lambda _: VMEM, outs),
            scratch_shapes=scratch,
            compiler_params=PARAMS,
            name=getattr(kernel, "func", kernel).__name__,
        )(*ins)

    x_near = [swap(embedded[0], "section", j) for j in (1, 2)]
    gates = jnp.where(expert_ids[0] < 1, route_gates[0], 0.0).transpose(0, 2, 1)
    parts, picks, picks_relayed, hits = call(
        slot_tables,
        (
            shape((tokens, LANES)),
            shape((SECTIONS - 1, picked, tokens)),
            shape((picked, tokens), F32),
            shape((picked, tokens)),
        ),
        (gates,),
        [pltpu.VMEM((LANES, tokens), F32)],
    )
    tables = [parts] + [swap(parts, "section", j) for j in (1, 2)]
    gain, x = call(
        stage,
        (shape(norm_gain.shape, F32), shape((tokens, width))),
        (parts, norm_gain, embedded),
    )
    relayed = call(
        relay, shape((CAP, width + tokens * LANES)), (tables[1], tables[2], x_near[1], gain)
    )
    down, gain = hold_weights(gain, down_proj, after=(relayed,))
    relayed = swap(relayed, "section", 1)
    y, normed, group, rank, linear = call(
        prepare_first,
        (
            shape((slots, width)),
            shape((PACK, width + LANES)),
            shape((SECTIONS, LANES), F32),
            shape((SECTIONS, LANES), F32),
            shape((tokens + picked, LANES)),
        ),
        (picks, picks_relayed, hits, x, *x_near, relayed, *tables, gain),
        [pltpu.VMEM((2 * PACK, width), F32), pltpu.VMEM((tokens, LANES), F32)],
    )
    gate, up, own = hold_weights(normed, gate_proj, up_proj)

    def rest(normed, own, order, sums):
        near, far = group_rows(normed, own, order)
        near_part, far_part = expert_call(near, far, gate, up, down)
        updates = spread(group_sum(near_part, far_part, order, sums))
        return near, far, tuple(jnp.pad(u, ((0, PACK - u.shape[0]), (0, 0))) for u in updates)

    near, far, updates = rest(normed, own, (1, 2, 3), (3, 1, 2))
    number = pl.BlockSpec(memory_space=pltpu.SMEM)
    planned = (
        shape((6 * tokens, SECTIONS * PACK)),
        shape((6 * PACK, SECTIONS * PACK), F32),
        shape((2 * PACK, slots), F32),
    )
    codes, line, rounds, few_rounds, base, *now = call(
        schedule,
        (
            shape((3, LANES, SECTIONS * PACK), F32),
            shape((1, LANES), F32),
            shape((1,), jnp.int32),
            shape((1,), jnp.int32),
            shape((1, LANES), F32),
            *planned,
        ),
        (near, far, group, rank, linear),
        out_specs=(VMEM, VMEM, number, number) + (VMEM,) * 4,
    )
    held = pltpu.VMEM((SECTIONS * PACK, width), F32)

    def body(count, state):
        done, base, now, x, y, updates = state
        coefs, mine, pick = now
        normed = call(
            next_rows,
            shape((count, width)),
            (mine, pick, y, *updates, gain),
            [held, pltpu.VMEM((2 * PACK, width), F32)],
        )
        base, *now, x, y = call(
            functools.partial(absorb, count),
            (shape(base.shape, F32), *planned, shape((tokens, width)), shape((slots, width))),
            (base, coefs, codes, line, linear, x, y, *updates),
            [held],
        )
        updates = rest(normed, normed, (3, 2, 1), (1, 2, 3))[2]
        return done + 1, base, tuple(now), x, y, updates

    state = (jnp.ones((1,), jnp.int32), base, tuple(now), x, y, updates)
    for count, limit in ((FEW, jnp.maximum(few_rounds, 1)), (PACK, jnp.maximum(rounds, 1))):
        state = lax.while_loop(
            functools.partial(lambda limit, s: s[0][0] < limit[0], limit),
            functools.partial(body, count),
            state,
        )
    _, _, now, x, _, updates = state
    return call(finish, shape(embedded.shape), (now[0], x, *updates), [held])


def solution(mesh):
    placed = (
        P("section", "expert", None),
        P("section", None),
        P("section", None, "expert"),
        P("section", None, "expert"),
        P("section", "expert", None),
        P("section", None, "expert", None),
        P("section", None, "expert", None),
    )
    fits = mesh.shape["expert"] == 8 and mesh.shape["section"] == 4
    return jax.shard_map(
        shards_group if fits else shards_general, mesh=mesh, in_specs=placed, out_specs=P("section", "expert", None), check_vma=False
    )
```

```python
import functools

import jax
import jax.numpy as jnp
from jax import lax
from jax.experimental import pallas as pl
from jax.experimental.pallas import tpu as pltpu
from jax.sharding import PartitionSpec as P

CAP = 2

eps_norm = 1e-06


def slot_weights(chosen, gates, num_experts):
    expert_range = jnp.arange(num_experts, dtype=jnp.int32)
    matched = (chosen[..., None] == expert_range).astype(jnp.int32)
    hit_table = jnp.sum(matched, axis=-2, dtype=jnp.int32)
    tokens = chosen.shape[-2]
    before = jnp.arange(tokens)[:, None] > jnp.arange(tokens)[None, :]
    earlier = jnp.sum(
        jnp.where(before[:, :, None], hit_table[..., None, :, :], 0), axis=-2, dtype=jnp.int32
    )
    weight = jnp.sum(jnp.where(matched > 0, gates[..., None], 0.0), axis=-2)
    slots = jnp.arange(CAP, dtype=jnp.int32)
    table = jnp.where(earlier[..., None] == slots, weight[..., None], 0.0)
    return table.reshape(table.shape[:-2] + (num_experts * CAP,))


def swap(array, axis, by):
    devices = lax.axis_size(axis)
    return lax.ppermute(array, axis, [(i, i ^ by) for i in range(devices)])


def section_exchange(parts):
    return [parts[0]] + [swap(parts[k], "section", k) for k in range(1, len(parts))]


def dispatch(rows):
    experts, count, width = rows.shape
    n_dev = lax.axis_size("expert")
    send = jnp.repeat(rows, n_dev // experts, axis=0)
    return lax.all_to_all(send, "expert", split_axis=0, concat_axis=0, tiled=True)


def collect(partial, experts):
    n_dev, count, width = partial.shape
    back = lax.all_to_all(partial, "expert", split_axis=0, concat_axis=0, tiled=True)
    back = back.reshape(experts, n_dev // experts, count, width)
    return jnp.sum(back.astype(jnp.float32), axis=1)


def expert_block(rows_in, gate_mat, up_mat, down_mat):
    gate_val = jnp.dot(rows_in, gate_mat, preferred_element_type=jnp.float32)
    up_val = jnp.dot(rows_in, up_mat, preferred_element_type=jnp.float32)
    hidden = (jax.nn.silu(gate_val) * up_val).astype(jnp.bfloat16)
    return jnp.dot(hidden, down_mat, preferred_element_type=jnp.float32).astype(jnp.bfloat16)


def layer_round(sent, gain_row, gate_mat, up_mat, down_mat, num_experts):
    width = sent[0].shape[-1]
    here = jnp.stack(section_exchange(sent))
    rows_float = here.astype(jnp.float32)
    scale = lax.rsqrt(jnp.mean(rows_float * rows_float, axis=-1, keepdims=True) + eps_norm)
    normed = (rows_float * scale * gain_row).astype(jnp.bfloat16)
    micros = here.shape[0]
    normed = normed.reshape(micros, num_experts, CAP, width).transpose(1, 0, 2, 3)
    received = dispatch(normed.reshape(num_experts, micros * CAP, width))
    n_dev = received.shape[0]
    partial = expert_block(received.reshape(-1, width), gate_mat, up_mat, down_mat)
    total = collect(partial.reshape(n_dev, micros * CAP, width), num_experts)
    total = total.astype(jnp.bfloat16).reshape(num_experts, micros, CAP, width)
    total = total.transpose(1, 0, 2, 3).reshape(micros, num_experts * CAP, width)
    return section_exchange([total[k] for k in range(micros)])


def shards_general(embedded, norm_gain, gate_proj, up_proj, down_proj, expert_ids, route_gates):
    n_section = lax.axis_size("section")
    n_dev = lax.axis_size("expert")
    num_experts = n_dev // min(8, n_dev)
    me = lax.axis_index("section")
    base = embedded[0]
    own = slot_weights(expert_ids[0], route_gates[0], num_experts)

    def pick(stacked, index):
        return lax.dynamic_index_in_dim(stacked, index, 0, keepdims=False)

    tables = section_exchange([pick(own, me ^ k) for k in range(n_section)])
    tables = jnp.stack(tables)
    ordered = jnp.stack([pick(tables, me ^ l) for l in range(n_section)])
    chosen = ordered > 0
    picks = jnp.sum(jnp.any(chosen, axis=-1).astype(jnp.int32), axis=0)
    depth = lax.pmax(jnp.max(picks), ("section", "expert"))
    masks = chosen.astype(jnp.bfloat16)

    def take(mask, rows):
        return lax.dot_general(
            mask, rows, (((0,), (0,)), ((), ())), preferred_element_type=jnp.float32
        ).astype(jnp.bfloat16)

    def advance(rows, layer, update):
        routed = jnp.dot(
            ordered[layer],
            update.astype(jnp.float32),
            precision=lax.Precision.HIGHEST,
            preferred_element_type=jnp.float32,
        )
        return (rows.astype(jnp.float32) + routed).astype(jnp.bfloat16)

    def one_round(inputs):
        sent = [pick(inputs, me ^ k) for k in range(n_section)]
        got = jnp.stack(
            layer_round(sent, norm_gain[0], gate_proj[0], up_proj[0], down_proj[0], num_experts)
        )
        return jnp.stack([pick(got, me ^ l) for l in range(n_section)])

    def body(state):
        count, updates = state
        rows, inputs = base, []
        for layer in range(n_section):
            inputs.append(take(masks[layer], rows))
            if layer < n_section - 1:
                rows = advance(rows, layer, updates[layer])
        return count + 1, one_round(jnp.stack(inputs))

    first = jnp.stack([take(masks[layer], base) for layer in range(n_section)])
    updates = one_round(first)
    _, updates = lax.while_loop(lambda s: s[0] < depth, body, (jnp.int32(1), updates))
    rows = base
    for layer in range(n_section):
        rows = advance(rows, layer, updates[layer])
    return rows[None]


LANES = 128
SECTIONS = 4
STRIP = 1024
PACK = 4
FEW = 2
BF16 = jnp.bfloat16
F32 = jnp.float32


def normalise(squares, kept, gain, normed_out):
    width = kept.shape[1]
    mean = jnp.sum(squares, axis=-1, keepdims=True) * (1.0 / width)
    scale = lax.rsqrt(mean + eps_norm)
    for start in range(0, width, STRIP):
        span = pl.ds(start, STRIP)
        value = kept[:, span] * scale * gain[:, span]
        normed_out[:, span] = value[: normed_out.shape[0]].astype(BF16)


def before(values):
    total = values
    for by in (1, 2, 4):
        total = total + pltpu.roll(total, by, 1)
    return total - values


def slot_code(value):
    return (value & (SECTIONS * CAP - 1)) // CAP


def slot_tables(gates, parts_out, picks, picks_relayed, hits_out, table):
    me = lax.axis_index("section")
    micros, _, tokens = gates.shape
    slots = micros * CAP
    row = lax.broadcasted_iota(jnp.int32, (tokens, tokens), 0)
    column = lax.broadcasted_iota(jnp.int32, (tokens, tokens), 1)
    ahead = jnp.where(row < column, 1.0, 0.0).astype(BF16)
    table[...] = jnp.zeros(table.shape, F32)
    hits = jnp.zeros((tokens, tokens), F32)
    for m in range(micros):
        weight = jnp.sum(gates[m], axis=0, keepdims=True)
        hit = jnp.where(weight > 0, 1.0, 0.0)
        hit = jnp.broadcast_to(hit, (tokens, tokens))
        slot = jnp.dot(hit.astype(BF16), ahead, preferred_element_type=F32).astype(jnp.int32)
        spot = (hit > 0) & (row == m * CAP + slot) & (slot < CAP)
        hits = jnp.where(spot, 1.0, hits)
        for q in range(CAP):
            chosen = (hit[:1] > 0) & (slot[:1] == q)
            value = jnp.where(chosen, weight, 0.0)
            high = value.astype(BF16).astype(F32)
            middle = (value - high).astype(BF16).astype(F32)
            at = m * CAP + q
            table[pl.ds(at, 1)] = high
            table[pl.ds(at + slots, 1)] = middle
            table[pl.ds(at + 2 * slots, 1)] = value - high - middle
    contract = (((1,), (1,)), ((), ()))
    same = jnp.where(row == column, 1.0, 0.0).astype(BF16)
    parts_out[...] = lax.dot_general(
        same, table[...].astype(BF16), contract, preferred_element_type=F32
    ).astype(BF16)
    hits = hits.astype(BF16)
    hits_out[...] = hits
    sums = jnp.dot(
        jnp.where(column < row, 1.0, 0.0).astype(BF16), hits, preferred_element_type=F32
    )
    order = lax.dot_general(
        jnp.ones((tokens, tokens), BF16), sums.astype(BF16), contract, preferred_element_type=F32
    ).astype(jnp.int32)
    filled = lax.dot_general(
        jnp.ones((tokens, tokens), BF16), hits, contract, preferred_element_type=F32
    )
    wanted = (row == column) | ((row >= slots) & (row < slots + PACK) & (order == row - slots))
    wanted = wanted & (column < slots)
    for j in range(SECTIONS - 1):
        mine = wanted & (slot_code(column) == (me ^ j))
        picks[j] = jnp.dot(
            jnp.where(mine, 1.0, 0.0).astype(BF16), hits, preferred_element_type=F32
        ).astype(BF16)
    mine = wanted & (slot_code(column) == (me ^ (SECTIONS - 1)))
    picks_relayed[...] = jnp.where(mine, filled, 0.0)


def stage(after, gain, embedded, gain_out, x_out):
    gain_out[...] = gain[...]
    x_out[...] = embedded[0]


def relay(table, table_two, rows, gain, out):
    me = lax.axis_index("section")
    width = rows.shape[1]
    row = lax.broadcasted_iota(jnp.int32, (8, LANES), 0)
    lane = lax.broadcasted_iota(jnp.int32, (8, LANES), 1)
    wanted = (lane == (me ^ 2) * CAP + row) & (row < CAP)
    chosen = jnp.where(table[...].astype(F32) > 0, 1.0, 0.0).astype(BF16)
    pick = lax.dot_general(
        jnp.where(wanted, 1.0, 0.0).astype(BF16),
        chosen,
        (((1,), (1,)), ((), ())),
        preferred_element_type=F32,
    ).astype(BF16)
    for start in range(0, width, STRIP):
        span = pl.ds(start, STRIP)
        value = jnp.dot(pick, rows[:, span], preferred_element_type=F32)
        out[:, span] = value[:CAP].astype(BF16)
    extra = table_two[...].astype(F32)
    for t in range(extra.shape[0]):
        line = jnp.broadcast_to(extra[t : t + 1], (CAP, LANES))
        out[:, pl.ds(width + t * LANES, LANES)] = line.astype(BF16)


def prepare_first(
    picks, picks_relayed, own_hits, x0, x1, x2, relayed, t0, t1, t2, gain, rows_out,
    normed_out, group_out, rank_out, linear_out, kept, last,
):
    me = lax.axis_index("section")
    inputs = (x0, x1, x2)
    slots, width = rows_out.shape
    for t in range(last.shape[0]):
        last[pl.ds(t, 1)] = relayed[:, pl.ds(width + t * LANES, LANES)].astype(F32)[:1]
    tables = (t0, t1, t2, last)
    far_column = lax.broadcasted_iota(jnp.int32, picks_relayed.shape, 1)
    far = [
        jnp.sum(
            jnp.where((far_column & (CAP - 1)) == q, picks_relayed[...], 0.0), axis=1, keepdims=True
        )
        for q in range(CAP)
    ]
    total = 0.0
    for start in range(0, width, STRIP):
        span = pl.ds(start, STRIP)
        rows = sum(
            jnp.dot(picks[j], inputs[j][:, span], preferred_element_type=F32)
            for j in range(SECTIONS - 1)
        )
        extra = relayed[:, span].astype(F32)
        rows = rows + sum(far[q] * extra[q : q + 1] for q in range(CAP))
        rows_out[:, span] = rows[:slots].astype(BF16)
        packed = rows[slots:]
        kept[:, span] = packed
        total += packed * packed
    normalise(total, kept, gain, normed_out)

    lane = lax.broadcasted_iota(jnp.int32, (x0.shape[0], LANES), 1)
    hits = [
        jnp.where((lane < slots) & (t[...].astype(F32) > 0), 1.0, 0.0) for t in tables
    ]
    pairs = [
        h + jnp.where(lane % CAP == 0, pltpu.roll(h, LANES - 1, 1), pltpu.roll(h, 1, 1))
        for h in hits
    ]
    largest = [jnp.zeros((1, 1), F32) for _ in range(SECTIONS)]
    for j in range(SECTIONS):
        mine = me ^ j
        level = jnp.zeros_like(hits[0])
        for other in range(SECTIONS):
            if other != j:
                level += pairs[other] * jnp.where((me ^ other) < mine, 1.0, 0.0)
        filled = jnp.sum(hits[j], axis=0, keepdims=True)
        level = jnp.sum(hits[j] * level, axis=0, keepdims=True)
        order = before(filled)
        late = jnp.where((level == 0) & (order >= PACK), filled, 0.0)
        group = jnp.where(filled > 0, jnp.where(level > 0, level, late - 1.0), -2.0)
        rank = order
        for g in range(SECTIONS):
            member = jnp.where(group == g, 1.0, 0.0)
            rank = jnp.where(group == g, before(member), rank)
            size = jnp.sum(member, axis=1, keepdims=True)
            largest[g] = jnp.maximum(largest[g], size)
        group_out[pl.ds(j, 1)] = group
        rank_out[pl.ds(j, 1)] = rank
    sizes = jnp.zeros((PACK, LANES), F32)
    spot = lax.broadcasted_iota(jnp.int32, (PACK, LANES), 1)
    for g in range(SECTIONS):
        sizes = jnp.where(spot == g, largest[g], sizes)
    normed_out[:, width:] = sizes.astype(BF16)

    span = 3 * slots
    table = jnp.zeros(lane.shape, F32)
    sooner = jnp.zeros(own_hits.shape[:1] + (LANES,), F32)
    row = lax.broadcasted_iota(jnp.int32, sooner.shape, 0)
    column = lax.broadcasted_iota(jnp.int32, sooner.shape, 1)
    for j in range(SECTIONS):
        part = jnp.where(lane < span, tables[j][...].astype(F32), 0.0)
        table = table + (pltpu.roll(part, j * span, 1) if j else part)
        inside = (column >= j * span) & (column < (j + 1) * span)
        sooner = jnp.where(inside, jnp.where((me ^ j) < me, 1.0, 0.0), sooner)
    inner = jnp.dot(own_hits[...], table.astype(BF16), preferred_element_type=F32)
    inner = jnp.where(row // CAP == slot_code(column), inner * sooner, 0.0)
    tokens = lane.shape[0]
    linear_out[:tokens] = jnp.where(slot_code(lane) == me, table, 0.0).astype(BF16)
    linear_out[tokens:] = inner.astype(BF16)


def schedule(
    near, far, group, rank, linear, codes_out, line_out, rounds_out, few_out, base_out, coefs_out,
    mine_out, pick_out,
):
    width = near.shape[1] - LANES
    slots = SECTIONS * CAP
    sizes = jnp.maximum(
        jnp.max(near[:, width:].astype(F32), axis=0, keepdims=True),
        jnp.max(far[:, width:].astype(F32), axis=0, keepdims=True),
    )
    lane = lax.broadcasted_iota(jnp.int32, sizes.shape, 1)
    largest = jnp.max(jnp.where(lane < SECTIONS, sizes, 0.0), axis=1, keepdims=True)
    few = largest <= FEW
    count = jnp.where(few, float(FEW), float(PACK))
    code = jnp.where(group[...] < -1, 0.0, rank[...] + 1)
    start = jnp.ones((1, 1), F32)
    for g in range(SECTIONS):
        place = PACK + (start - 1) * count + rank[...] + 1
        code = jnp.where(group[...] == g, place, code)
        size = jnp.sum(jnp.where(lane == g, sizes, 0.0), axis=1, keepdims=True)
        start = start + jnp.floor((size + (count - 1)) / count)
    rounds_out[0] = jnp.max(jnp.where(few, 0.0, start)).astype(jnp.int32)
    few_out[0] = jnp.max(jnp.where(few, start, 0.0)).astype(jnp.int32)
    base_out[...] = jnp.zeros(base_out.shape, F32)
    span = 3 * slots
    line = jnp.zeros(sizes.shape, F32)
    for j in range(SECTIONS):
        own = jnp.where(lane < slots, code[j : j + 1], 0.0)
        for part in range(3):
            shift = j * span + part * slots
            line = line + (pltpu.roll(own, shift, 1) if shift else own)
    line_out[...] = line
    eye = lax.broadcasted_iota(jnp.int32, (LANES, LANES), 0) == lax.broadcasted_iota(
        jnp.int32, (LANES, LANES), 1
    )
    turned = lax.dot_general(
        jnp.where(eye, 1.0, 0.0).astype(BF16),
        jnp.broadcast_to(line, (SECTIONS * PACK, LANES)).astype(BF16),
        (((1,), (1,)), ((), ())),
        preferred_element_type=F32,
    )
    row = lax.broadcasted_iota(jnp.int32, turned.shape, 0)
    column = lax.broadcasted_iota(jnp.int32, turned.shape, 1)
    codes = []
    for part in range(3):
        kept = jnp.zeros(turned.shape, F32)
        for j in range(SECTIONS):
            low = j * span + part * slots
            block = (row >= low) & (row < low + slots) & (column // PACK == j)
            kept = jnp.where(block, turned, kept)
        codes_out[part] = kept
        codes.append(kept)
    coefs_out[...], mine_out[...], pick_out[...] = plan(
        jnp.zeros((1, 1), F32), count, codes, line, linear, slots
    )


def following(base, count):
    return jnp.where(base < PACK, float(PACK), base + count)


def plan(base, count, codes, line, linear, slots):
    spot = lax.broadcasted_iota(jnp.int32, codes[0].shape, 1)
    wanted = base + (1 + (spot & (PACK - 1))).astype(F32)
    coefs = []
    for part in range(3):
        chosen = jnp.where(codes[part] == wanted, 1.0, 0.0).astype(BF16)
        coefs.append(jnp.dot(linear[...], chosen, preferred_element_type=F32))
    spot = lax.broadcasted_iota(jnp.int32, (2 * PACK, slots), 0)
    wanted = following(base, count) + (1 + spot).astype(F32)
    pick = jnp.where((line[:, :slots] == wanted) & (spot < count), 1.0, 0.0)
    first = linear.shape[0] // 2
    mine = [
        jnp.dot(
            pick.astype(BF16),
            part[first : first + slots].astype(BF16),
            preferred_element_type=F32,
        )
        for part in coefs
    ]
    return jnp.concatenate(coefs, axis=0).astype(BF16), jnp.concatenate(mine, axis=0), pick


def gather(updates, held):
    for j, update in enumerate(updates):
        held[pl.ds(j * PACK, PACK)] = update[...].astype(F32)


def changes(coefs, held, span):
    result = jnp.dot(coefs, held[:, span].astype(BF16), preferred_element_type=F32)
    third = coefs.shape[0] // 3
    return result[:third] + result[third : 2 * third] + result[2 * third :]


def next_rows(mine, pick, y, u0, u1, u2, u3, gain, normed_out, held, kept):
    gather((u0, u1, u2, u3), held)
    chosen = pick[...].astype(BF16)
    coefs = mine[...].astype(BF16)
    total = 0.0
    for start in range(0, y.shape[1], STRIP):
        span = pl.ds(start, STRIP)
        rows = jnp.dot(chosen, y[:, span], preferred_element_type=F32)
        rows = (rows + changes(coefs, held, span)).astype(BF16).astype(F32)
        kept[:, span] = rows
        total += rows * rows
    normalise(total, kept, gain, normed_out)


def absorb(
    count, base, coefs, codes, line, linear, x, y, u0, u1, u2, u3, base_out, coefs_out, mine_out,
    pick_out, x_out, y_out, held,
):
    gather((u0, u1, u2, u3), held)
    tokens, width = x.shape
    slots = y.shape[0]
    known = coefs[...]
    for start in range(0, width, STRIP):
        span = pl.ds(start, STRIP)
        change = changes(known, held, span)
        x_out[:, span] = (x[:, span].astype(F32) + change[:tokens]).astype(BF16)
        y_out[:, span] = (y[:, span].astype(F32) + change[tokens : tokens + slots]).astype(BF16)
    after = following(base[...], count)
    base_out[...] = after
    parts = [codes[part] for part in range(3)]
    coefs_out[...], mine_out[...], pick_out[...] = plan(
        after[:, :1], count, parts, line, linear, slots
    )


def finish(coefs, x, u0, u1, u2, u3, out, held):
    gather((u0, u1, u2, u3), held)
    tokens, width = x.shape
    third = coefs.shape[0] // 3
    known = jnp.concatenate([coefs[pl.ds(i * third, tokens)] for i in range(3)], axis=0)
    for start in range(0, width, STRIP):
        span = pl.ds(start, STRIP)
        out[0, :, span] = (x[:, span].astype(F32) + changes(known, held, span)).astype(BF16)


def expert_kernel(near, far, gate, up, down, near_out, far_out, rows):
    half, width = near_out.shape
    if half % 16:
        for start in range(0, width, STRIP):
            span = pl.ds(start, STRIP)
            both = [near[:, span].astype(F32), far[:, span].astype(F32)]
            rows[:, span] = jnp.concatenate(both, axis=0).astype(BF16)
    else:
        rows[:half] = near[:, :width]
        rows[half:] = far[:, :width]
    gate_val = jnp.dot(rows[...], gate[0], preferred_element_type=F32)
    up_val = jnp.dot(rows[...], up[0], preferred_element_type=F32)
    hidden = (gate_val * jax.nn.sigmoid(gate_val) * up_val).astype(BF16)
    for start in range(0, width, STRIP):
        span = pl.ds(start, STRIP)
        value = jnp.dot(hidden, down[0, :, span], preferred_element_type=F32)
        near_out[:, span] = value[:half].astype(BF16)
        far_out[:, span] = value[half:].astype(BF16)


def hold_kernel(*refs):
    count = len(refs) // 2
    inputs, outputs, sems = refs[:count], refs[count : 2 * count], refs[-1]
    copies = [
        pltpu.make_async_copy(inputs[i], outputs[i], sems.at[i]) for i in range(count - 1)
    ]
    for copy in copies:
        copy.start()
    outputs[-1][...] = inputs[-1][...]
    for copy in copies:
        copy.wait()


VMEM = pl.BlockSpec(memory_space=pltpu.VMEM)
HBM = pl.BlockSpec(memory_space=pltpu.HBM)
PARAMS = pltpu.CompilerParams(vmem_limit_bytes=16 * 2**20)


def expert_call(near, far, gate, up, down):
    half = near.shape[0]
    _, width, hidden = gate.shape
    out = jax.ShapeDtypeStruct((half, width), BF16)
    return pl.pallas_call(
        expert_kernel,
        out_shape=(out, out),
        in_specs=[VMEM] * 5,
        out_specs=(VMEM, VMEM),
        scratch_shapes=[pltpu.VMEM((2 * half, width), BF16)],
        compiler_params=PARAMS,
        cost_estimate=pl.CostEstimate(
            flops=12 * half * width * hidden,
            bytes_accessed=6 * width * hidden,
            transcendentals=2 * half * hidden,
        ),
        name="experts",
    )(near, far, gate, up, down)


def hold_weights(rows, *weights, after=()):
    operands = weights + (rows,)
    return pl.pallas_call(
        lambda *refs: hold_kernel(*refs[: len(operands)], *refs[len(operands) + len(after) :]),
        out_shape=tuple(jax.ShapeDtypeStruct(w.shape, w.dtype) for w in operands),
        in_specs=[HBM] * len(weights) + [VMEM] * (1 + len(after)),
        out_specs=(VMEM,) * len(operands),
        scratch_shapes=[pltpu.SemaphoreType.DMA((len(weights),))],
        compiler_params=pltpu.CompilerParams(vmem_limit_bytes=52 * 2**20),
        cost_estimate=pl.CostEstimate(
            flops=0, bytes_accessed=4 * sum(w.size for w in weights), transcendentals=0
        ),
        name="hold_weights",
    )(*operands, *after)


def spread(array):
    return [array] + [swap(array, "section", j) for j in range(1, 4)]


def group_rows(normed, own, order):
    near = jnp.concatenate([own] + [swap(normed, "expert", 2 * k) for k in order])
    return near, swap(near, "expert", 1)


def group_sum(near, far, order, sums):
    other = swap(far, "expert", 1)
    both = (near.astype(F32) + other.astype(F32)).astype(BF16)
    count = both.shape[0] // 4
    parts = {k: both[i * count : (i + 1) * count] for i, k in enumerate((0, *order))}
    total = parts[0].astype(F32)
    for k in sums:
        total = total + swap(parts[k], "expert", 2 * k).astype(F32)
    return total.astype(BF16)


def shards_group(embedded, norm_gain, gate_proj, up_proj, down_proj, expert_ids, route_gates):
    tokens, width = embedded.shape[1:]
    slots = expert_ids.shape[1] * CAP
    picked = slots + 2 * PACK

    def shape(dims, kind=BF16):
        return jax.ShapeDtypeStruct(dims, kind)

    def call(kernel, outs, ins, scratch=(), in_specs=None, out_specs=None):
        return pl.pallas_call(
            kernel,
            out_shape=outs,
            in_specs=in_specs or [VMEM] * len(ins),
            out_specs=out_specs or jax.tree.map(lambda _: VMEM, outs),
            scratch_shapes=scratch,
            compiler_params=PARAMS,
            name=getattr(kernel, "func", kernel).__name__,
        )(*ins)

    x_near = [swap(embedded[0], "section", j) for j in (1, 2)]
    gates = jnp.where(expert_ids[0] < 1, route_gates[0], 0.0).transpose(0, 2, 1)
    parts, picks, picks_relayed, hits = call(
        slot_tables,
        (
            shape((tokens, LANES)),
            shape((SECTIONS - 1, picked, tokens)),
            shape((picked, tokens), F32),
            shape((picked, tokens)),
        ),
        (gates,),
        [pltpu.VMEM((LANES, tokens), F32)],
    )
    tables = [parts] + [swap(parts, "section", j) for j in (1, 2)]
    gain, x = call(
        stage,
        (shape(norm_gain.shape, F32), shape((tokens, width))),
        (parts, norm_gain, embedded),
    )
    relayed = call(
        relay, shape((CAP, width + tokens * LANES)), (tables[1], tables[2], x_near[1], gain)
    )
    down, gain = hold_weights(gain, down_proj, after=(relayed,))
    relayed = swap(relayed, "section", 1)
    y, normed, group, rank, linear = call(
        prepare_first,
        (
            shape((slots, width)),
            shape((PACK, width + LANES)),
            shape((SECTIONS, LANES), F32),
            shape((SECTIONS, LANES), F32),
            shape((tokens + picked, LANES)),
        ),
        (picks, picks_relayed, hits, x, *x_near, relayed, *tables, gain),
        [pltpu.VMEM((2 * PACK, width), F32), pltpu.VMEM((tokens, LANES), F32)],
    )
    gate, up, own = hold_weights(normed, gate_proj, up_proj)

    def rest(normed, own, order, sums):
        near, far = group_rows(normed, own, order)
        near_part, far_part = expert_call(near, far, gate, up, down)
        updates = spread(group_sum(near_part, far_part, order, sums))
        return near, far, tuple(jnp.pad(u, ((0, PACK - u.shape[0]), (0, 0))) for u in updates)

    near, far, updates = rest(normed, own, (1, 3, 2), (3, 1, 2))
    number = pl.BlockSpec(memory_space=pltpu.SMEM)
    planned = (
        shape((6 * tokens, SECTIONS * PACK)),
        shape((6 * PACK, SECTIONS * PACK), F32),
        shape((2 * PACK, slots), F32),
    )
    codes, line, rounds, few_rounds, base, *now = call(
        schedule,
        (
            shape((3, LANES, SECTIONS * PACK), F32),
            shape((1, LANES), F32),
            shape((1,), jnp.int32),
            shape((1,), jnp.int32),
            shape((1, LANES), F32),
            *planned,
        ),
        (near, far, group, rank, linear),
        out_specs=(VMEM, VMEM, number, number) + (VMEM,) * 4,
    )
    held = pltpu.VMEM((SECTIONS * PACK, width), F32)

    def body(count, state):
        done, base, now, x, y, updates = state
        coefs, mine, pick = now
        normed = call(
            next_rows,
            shape((count, width)),
            (mine, pick, y, *updates, gain),
            [held, pltpu.VMEM((2 * PACK, width), F32)],
        )
        base, *now, x, y = call(
            functools.partial(absorb, count),
            (shape(base.shape, F32), *planned, shape((tokens, width)), shape((slots, width))),
            (base, coefs, codes, line, linear, x, y, *updates),
            [held],
        )
        updates = rest(normed, normed, (2, 3, 1), (1, 2, 3))[2]
        return done + 1, base, tuple(now), x, y, updates

    state = (jnp.ones((1,), jnp.int32), base, tuple(now), x, y, updates)
    for count, limit in ((FEW, jnp.maximum(few_rounds, 1)), (PACK, jnp.maximum(rounds, 1))):
        state = lax.while_loop(
            functools.partial(lambda limit, s: s[0][0] < limit[0], limit),
            functools.partial(body, count),
            state,
        )
    _, _, now, x, _, updates = state
    return call(finish, shape(embedded.shape), (now[0], x, *updates), [held])


def solution(mesh):
    placed = (
        P("section", "expert", None),
        P("section", None),
        P("section", None, "expert"),
        P("section", None, "expert"),
        P("section", "expert", None),
        P("section", None, "expert", None),
        P("section", None, "expert", None),
    )
    fits = mesh.shape["expert"] == 8 and mesh.shape["section"] == 4
    return jax.shard_map(
        shards_group if fits else shards_general, mesh=mesh, in_specs=placed, out_specs=P("section", "expert", None), check_vma=False
    )
```

```python
import functools

import jax
import jax.numpy as jnp
from jax import lax
from jax.experimental import pallas as pl
from jax.experimental.pallas import tpu as pltpu
from jax.sharding import PartitionSpec as P

CAP = 2

eps_norm = 1e-06


def slot_weights(chosen, gates, num_experts):
    expert_range = jnp.arange(num_experts, dtype=jnp.int32)
    matched = (chosen[..., None] == expert_range).astype(jnp.int32)
    hit_table = jnp.sum(matched, axis=-2, dtype=jnp.int32)
    tokens = chosen.shape[-2]
    before = jnp.arange(tokens)[:, None] > jnp.arange(tokens)[None, :]
    earlier = jnp.sum(
        jnp.where(before[:, :, None], hit_table[..., None, :, :], 0), axis=-2, dtype=jnp.int32
    )
    weight = jnp.sum(jnp.where(matched > 0, gates[..., None], 0.0), axis=-2)
    slots = jnp.arange(CAP, dtype=jnp.int32)
    table = jnp.where(earlier[..., None] == slots, weight[..., None], 0.0)
    return table.reshape(table.shape[:-2] + (num_experts * CAP,))


def swap(array, axis, by):
    devices = lax.axis_size(axis)
    return lax.ppermute(array, axis, [(i, i ^ by) for i in range(devices)])


def section_exchange(parts):
    return [parts[0]] + [swap(parts[k], "section", k) for k in range(1, len(parts))]


def dispatch(rows):
    experts, count, width = rows.shape
    n_dev = lax.axis_size("expert")
    send = jnp.repeat(rows, n_dev // experts, axis=0)
    return lax.all_to_all(send, "expert", split_axis=0, concat_axis=0, tiled=True)


def collect(partial, experts):
    n_dev, count, width = partial.shape
    back = lax.all_to_all(partial, "expert", split_axis=0, concat_axis=0, tiled=True)
    back = back.reshape(experts, n_dev // experts, count, width)
    return jnp.sum(back.astype(jnp.float32), axis=1)


def expert_block(rows_in, gate_mat, up_mat, down_mat):
    gate_val = jnp.dot(rows_in, gate_mat, preferred_element_type=jnp.float32)
    up_val = jnp.dot(rows_in, up_mat, preferred_element_type=jnp.float32)
    hidden = (jax.nn.silu(gate_val) * up_val).astype(jnp.bfloat16)
    return jnp.dot(hidden, down_mat, preferred_element_type=jnp.float32).astype(jnp.bfloat16)


def layer_round(sent, gain_row, gate_mat, up_mat, down_mat, num_experts):
    width = sent[0].shape[-1]
    here = jnp.stack(section_exchange(sent))
    rows_float = here.astype(jnp.float32)
    scale = lax.rsqrt(jnp.mean(rows_float * rows_float, axis=-1, keepdims=True) + eps_norm)
    normed = (rows_float * scale * gain_row).astype(jnp.bfloat16)
    micros = here.shape[0]
    normed = normed.reshape(micros, num_experts, CAP, width).transpose(1, 0, 2, 3)
    received = dispatch(normed.reshape(num_experts, micros * CAP, width))
    n_dev = received.shape[0]
    partial = expert_block(received.reshape(-1, width), gate_mat, up_mat, down_mat)
    total = collect(partial.reshape(n_dev, micros * CAP, width), num_experts)
    total = total.astype(jnp.bfloat16).reshape(num_experts, micros, CAP, width)
    total = total.transpose(1, 0, 2, 3).reshape(micros, num_experts * CAP, width)
    return section_exchange([total[k] for k in range(micros)])


def shards_general(embedded, norm_gain, gate_proj, up_proj, down_proj, expert_ids, route_gates):
    n_section = lax.axis_size("section")
    n_dev = lax.axis_size("expert")
    num_experts = n_dev // min(8, n_dev)
    me = lax.axis_index("section")
    base = embedded[0]
    own = slot_weights(expert_ids[0], route_gates[0], num_experts)

    def pick(stacked, index):
        return lax.dynamic_index_in_dim(stacked, index, 0, keepdims=False)

    tables = section_exchange([pick(own, me ^ k) for k in range(n_section)])
    tables = jnp.stack(tables)
    ordered = jnp.stack([pick(tables, me ^ l) for l in range(n_section)])
    chosen = ordered > 0
    picks = jnp.sum(jnp.any(chosen, axis=-1).astype(jnp.int32), axis=0)
    depth = lax.pmax(jnp.max(picks), ("section", "expert"))
    masks = chosen.astype(jnp.bfloat16)

    def take(mask, rows):
        return lax.dot_general(
            mask, rows, (((0,), (0,)), ((), ())), preferred_element_type=jnp.float32
        ).astype(jnp.bfloat16)

    def advance(rows, layer, update):
        routed = jnp.dot(
            ordered[layer],
            update.astype(jnp.float32),
            precision=lax.Precision.HIGHEST,
            preferred_element_type=jnp.float32,
        )
        return (rows.astype(jnp.float32) + routed).astype(jnp.bfloat16)

    def one_round(inputs):
        sent = [pick(inputs, me ^ k) for k in range(n_section)]
        got = jnp.stack(
            layer_round(sent, norm_gain[0], gate_proj[0], up_proj[0], down_proj[0], num_experts)
        )
        return jnp.stack([pick(got, me ^ l) for l in range(n_section)])

    def body(state):
        count, updates = state
        rows, inputs = base, []
        for layer in range(n_section):
            inputs.append(take(masks[layer], rows))
            if layer < n_section - 1:
                rows = advance(rows, layer, updates[layer])
        return count + 1, one_round(jnp.stack(inputs))

    first = jnp.stack([take(masks[layer], base) for layer in range(n_section)])
    updates = one_round(first)
    _, updates = lax.while_loop(lambda s: s[0] < depth, body, (jnp.int32(1), updates))
    rows = base
    for layer in range(n_section):
        rows = advance(rows, layer, updates[layer])
    return rows[None]


LANES = 128
SECTIONS = 4
STRIP = 1024
PACK = 4
FEW = 2
BF16 = jnp.bfloat16
F32 = jnp.float32


def normalise(squares, kept, gain, normed_out):
    width = kept.shape[1]
    mean = jnp.sum(squares, axis=-1, keepdims=True) * (1.0 / width)
    scale = lax.rsqrt(mean + eps_norm)
    for start in range(0, width, STRIP):
        span = pl.ds(start, STRIP)
        value = kept[:, span] * scale * gain[:, span]
        normed_out[:, span] = value[: normed_out.shape[0]].astype(BF16)


def before(values):
    total = values
    for by in (1, 2, 4):
        total = total + pltpu.roll(total, by, 1)
    return total - values


def slot_code(value):
    return (value & (SECTIONS * CAP - 1)) // CAP


def slot_tables(gates, parts_out, picks, picks_relayed, hits_out, table):
    me = lax.axis_index("section")
    micros, _, tokens = gates.shape
    slots = micros * CAP
    row = lax.broadcasted_iota(jnp.int32, (tokens, tokens), 0)
    column = lax.broadcasted_iota(jnp.int32, (tokens, tokens), 1)
    ahead = jnp.where(row < column, 1.0, 0.0).astype(BF16)
    table[...] = jnp.zeros(table.shape, F32)
    hits = jnp.zeros((tokens, tokens), F32)
    for m in range(micros):
        weight = jnp.sum(gates[m], axis=0, keepdims=True)
        hit = jnp.where(weight > 0, 1.0, 0.0)
        hit = jnp.broadcast_to(hit, (tokens, tokens))
        slot = jnp.dot(hit.astype(BF16), ahead, preferred_element_type=F32).astype(jnp.int32)
        spot = (hit > 0) & (row == m * CAP + slot) & (slot < CAP)
        hits = jnp.where(spot, 1.0, hits)
        for q in range(CAP):
            chosen = (hit[:1] > 0) & (slot[:1] == q)
            value = jnp.where(chosen, weight, 0.0)
            high = value.astype(BF16).astype(F32)
            middle = (value - high).astype(BF16).astype(F32)
            at = m * CAP + q
            table[pl.ds(at, 1)] = high
            table[pl.ds(at + slots, 1)] = middle
            table[pl.ds(at + 2 * slots, 1)] = value - high - middle
    contract = (((1,), (1,)), ((), ()))
    same = jnp.where(row == column, 1.0, 0.0).astype(BF16)
    parts_out[...] = lax.dot_general(
        same, table[...].astype(BF16), contract, preferred_element_type=F32
    ).astype(BF16)
    hits = hits.astype(BF16)
    hits_out[...] = hits
    sums = jnp.dot(
        jnp.where(column < row, 1.0, 0.0).astype(BF16), hits, preferred_element_type=F32
    )
    order = lax.dot_general(
        jnp.ones((tokens, tokens), BF16), sums.astype(BF16), contract, preferred_element_type=F32
    ).astype(jnp.int32)
    filled = lax.dot_general(
        jnp.ones((tokens, tokens), BF16), hits, contract, preferred_element_type=F32
    )
    wanted = (row == column) | ((row >= slots) & (row < slots + PACK) & (order == row - slots))
    wanted = wanted & (column < slots)
    for j in range(SECTIONS - 1):
        mine = wanted & (slot_code(column) == (me ^ j))
        picks[j] = jnp.dot(
            jnp.where(mine, 1.0, 0.0).astype(BF16), hits, preferred_element_type=F32
        ).astype(BF16)
    mine = wanted & (slot_code(column) == (me ^ (SECTIONS - 1)))
    picks_relayed[...] = jnp.where(mine, filled, 0.0)


def stage(after, gain, embedded, gain_out, x_out):
    gain_out[...] = gain[...]
    x_out[...] = embedded[0]


def relay(table, table_two, rows, gain, out):
    me = lax.axis_index("section")
    width = rows.shape[1]
    row = lax.broadcasted_iota(jnp.int32, (8, LANES), 0)
    lane = lax.broadcasted_iota(jnp.int32, (8, LANES), 1)
    wanted = (lane == (me ^ 2) * CAP + row) & (row < CAP)
    chosen = jnp.where(table[...].astype(F32) > 0, 1.0, 0.0).astype(BF16)
    pick = lax.dot_general(
        jnp.where(wanted, 1.0, 0.0).astype(BF16),
        chosen,
        (((1,), (1,)), ((), ())),
        preferred_element_type=F32,
    ).astype(BF16)
    for start in range(0, width, STRIP):
        span = pl.ds(start, STRIP)
        value = jnp.dot(pick, rows[:, span], preferred_element_type=F32)
        out[:, span] = value[:CAP].astype(BF16)
    extra = table_two[...].astype(F32)
    for t in range(extra.shape[0]):
        line = jnp.broadcast_to(extra[t : t + 1], (CAP, LANES))
        out[:, pl.ds(width + t * LANES, LANES)] = line.astype(BF16)


def prepare_first(
    picks, picks_relayed, own_hits, x0, x1, x2, relayed, t0, t1, t2, gain, rows_out,
    normed_out, group_out, rank_out, linear_out, kept, last,
):
    me = lax.axis_index("section")
    inputs = (x0, x1, x2)
    slots, width = rows_out.shape
    for t in range(last.shape[0]):
        last[pl.ds(t, 1)] = relayed[:, pl.ds(width + t * LANES, LANES)].astype(F32)[:1]
    tables = (t0, t1, t2, last)
    far_column = lax.broadcasted_iota(jnp.int32, picks_relayed.shape, 1)
    far = [
        jnp.sum(
            jnp.where((far_column & (CAP - 1)) == q, picks_relayed[...], 0.0), axis=1, keepdims=True
        )
        for q in range(CAP)
    ]
    total = 0.0
    for start in range(0, width, STRIP):
        span = pl.ds(start, STRIP)
        rows = sum(
            jnp.dot(picks[j], inputs[j][:, span], preferred_element_type=F32)
            for j in range(SECTIONS - 1)
        )
        extra = relayed[:, span].astype(F32)
        rows = rows + sum(far[q] * extra[q : q + 1] for q in range(CAP))
        rows_out[:, span] = rows[:slots].astype(BF16)
        packed = rows[slots:]
        kept[:, span] = packed
        total += packed * packed
    normalise(total, kept, gain, normed_out)

    lane = lax.broadcasted_iota(jnp.int32, (x0.shape[0], LANES), 1)
    hits = [
        jnp.where((lane < slots) & (t[...].astype(F32) > 0), 1.0, 0.0) for t in tables
    ]
    pairs = [
        h + jnp.where(lane % CAP == 0, pltpu.roll(h, LANES - 1, 1), pltpu.roll(h, 1, 1))
        for h in hits
    ]
    largest = [jnp.zeros((1, 1), F32) for _ in range(SECTIONS)]
    for j in range(SECTIONS):
        mine = me ^ j
        level = jnp.zeros_like(hits[0])
        for other in range(SECTIONS):
            if other != j:
                level += pairs[other] * jnp.where((me ^ other) < mine, 1.0, 0.0)
        filled = jnp.sum(hits[j], axis=0, keepdims=True)
        level = jnp.sum(hits[j] * level, axis=0, keepdims=True)
        order = before(filled)
        late = jnp.where((level == 0) & (order >= PACK), filled, 0.0)
        group = jnp.where(filled > 0, jnp.where(level > 0, level, late - 1.0), -2.0)
        rank = order
        for g in range(SECTIONS):
            member = jnp.where(group == g, 1.0, 0.0)
            rank = jnp.where(group == g, before(member), rank)
            size = jnp.sum(member, axis=1, keepdims=True)
            largest[g] = jnp.maximum(largest[g], size)
        group_out[pl.ds(j, 1)] = group
        rank_out[pl.ds(j, 1)] = rank
    sizes = jnp.zeros((PACK, LANES), F32)
    spot = lax.broadcasted_iota(jnp.int32, (PACK, LANES), 1)
    for g in range(SECTIONS):
        sizes = jnp.where(spot == g, largest[g], sizes)
    normed_out[:, width:] = sizes.astype(BF16)

    span = 3 * slots
    table = jnp.zeros(lane.shape, F32)
    sooner = jnp.zeros(own_hits.shape[:1] + (LANES,), F32)
    row = lax.broadcasted_iota(jnp.int32, sooner.shape, 0)
    column = lax.broadcasted_iota(jnp.int32, sooner.shape, 1)
    for j in range(SECTIONS):
        part = jnp.where(lane < span, tables[j][...].astype(F32), 0.0)
        table = table + (pltpu.roll(part, j * span, 1) if j else part)
        inside = (column >= j * span) & (column < (j + 1) * span)
        sooner = jnp.where(inside, jnp.where((me ^ j) < me, 1.0, 0.0), sooner)
    inner = jnp.dot(own_hits[...], table.astype(BF16), preferred_element_type=F32)
    inner = jnp.where(row // CAP == slot_code(column), inner * sooner, 0.0)
    tokens = lane.shape[0]
    linear_out[:tokens] = jnp.where(slot_code(lane) == me, table, 0.0).astype(BF16)
    linear_out[tokens:] = inner.astype(BF16)


def schedule(
    near, far, group, rank, linear, codes_out, line_out, rounds_out, few_out, base_out, coefs_out,
    mine_out, pick_out,
):
    width = near.shape[1] - LANES
    slots = SECTIONS * CAP
    sizes = jnp.maximum(
        jnp.max(near[:, width:].astype(F32), axis=0, keepdims=True),
        jnp.max(far[:, width:].astype(F32), axis=0, keepdims=True),
    )
    lane = lax.broadcasted_iota(jnp.int32, sizes.shape, 1)
    largest = jnp.max(jnp.where(lane < SECTIONS, sizes, 0.0), axis=1, keepdims=True)
    few = largest <= FEW
    count = jnp.where(few, float(FEW), float(PACK))
    code = jnp.where(group[...] < -1, 0.0, rank[...] + 1)
    start = jnp.ones((1, 1), F32)
    for g in range(SECTIONS):
        place = PACK + (start - 1) * count + rank[...] + 1
        code = jnp.where(group[...] == g, place, code)
        size = jnp.sum(jnp.where(lane == g, sizes, 0.0), axis=1, keepdims=True)
        start = start + jnp.floor((size + (count - 1)) / count)
    rounds_out[0] = jnp.max(jnp.where(few, 0.0, start)).astype(jnp.int32)
    few_out[0] = jnp.max(jnp.where(few, start, 0.0)).astype(jnp.int32)
    base_out[...] = jnp.zeros(base_out.shape, F32)
    span = 3 * slots
    line = jnp.zeros(sizes.shape, F32)
    for j in range(SECTIONS):
        own = jnp.where(lane < slots, code[j : j + 1], 0.0)
        for part in range(3):
            shift = j * span + part * slots
            line = line + (pltpu.roll(own, shift, 1) if shift else own)
    line_out[...] = line
    eye = lax.broadcasted_iota(jnp.int32, (LANES, LANES), 0) == lax.broadcasted_iota(
        jnp.int32, (LANES, LANES), 1
    )
    turned = lax.dot_general(
        jnp.where(eye, 1.0, 0.0).astype(BF16),
        jnp.broadcast_to(line, (SECTIONS * PACK, LANES)).astype(BF16),
        (((1,), (1,)), ((), ())),
        preferred_element_type=F32,
    )
    row = lax.broadcasted_iota(jnp.int32, turned.shape, 0)
    column = lax.broadcasted_iota(jnp.int32, turned.shape, 1)
    codes = []
    for part in range(3):
        kept = jnp.zeros(turned.shape, F32)
        for j in range(SECTIONS):
            low = j * span + part * slots
            block = (row >= low) & (row < low + slots) & (column // PACK == j)
            kept = jnp.where(block, turned, kept)
        codes_out[part] = kept
        codes.append(kept)
    coefs_out[...], mine_out[...], pick_out[...] = plan(
        jnp.zeros((1, 1), F32), count, codes, line, linear, slots
    )


def following(base, count):
    return jnp.where(base < PACK, float(PACK), base + count)


def plan(base, count, codes, line, linear, slots):
    spot = lax.broadcasted_iota(jnp.int32, codes[0].shape, 1)
    wanted = base + (1 + (spot & (PACK - 1))).astype(F32)
    coefs = []
    for part in range(3):
        chosen = jnp.where(codes[part] == wanted, 1.0, 0.0).astype(BF16)
        coefs.append(jnp.dot(linear[...], chosen, preferred_element_type=F32))
    spot = lax.broadcasted_iota(jnp.int32, (2 * PACK, slots), 0)
    wanted = following(base, count) + (1 + spot).astype(F32)
    pick = jnp.where((line[:, :slots] == wanted) & (spot < count), 1.0, 0.0)
    first = linear.shape[0] // 2
    mine = [
        jnp.dot(
            pick.astype(BF16),
            part[first : first + slots].astype(BF16),
            preferred_element_type=F32,
        )
        for part in coefs
    ]
    return jnp.concatenate(coefs, axis=0).astype(BF16), jnp.concatenate(mine, axis=0), pick


def gather(updates, held):
    for j, update in enumerate(updates):
        held[pl.ds(j * PACK, PACK)] = update[...].astype(F32)


def changes(coefs, held, span):
    result = jnp.dot(coefs, held[:, span].astype(BF16), preferred_element_type=F32)
    third = coefs.shape[0] // 3
    return result[:third] + result[third : 2 * third] + result[2 * third :]


def next_rows(mine, pick, y, u0, u1, u2, u3, gain, normed_out, held, kept):
    gather((u0, u1, u2, u3), held)
    chosen = pick[...].astype(BF16)
    coefs = mine[...].astype(BF16)
    total = 0.0
    for start in range(0, y.shape[1], STRIP):
        span = pl.ds(start, STRIP)
        rows = jnp.dot(chosen, y[:, span], preferred_element_type=F32)
        rows = (rows + changes(coefs, held, span)).astype(BF16).astype(F32)
        kept[:, span] = rows
        total += rows * rows
    normalise(total, kept, gain, normed_out)


def absorb(
    count, base, coefs, codes, line, linear, x, y, u0, u1, u2, u3, base_out, coefs_out, mine_out,
    pick_out, x_out, y_out, held,
):
    gather((u0, u1, u2, u3), held)
    tokens, width = x.shape
    slots = y.shape[0]
    known = coefs[...]
    for start in range(0, width, STRIP):
        span = pl.ds(start, STRIP)
        change = changes(known, held, span)
        x_out[:, span] = (x[:, span].astype(F32) + change[:tokens]).astype(BF16)
        y_out[:, span] = (y[:, span].astype(F32) + change[tokens : tokens + slots]).astype(BF16)
    after = following(base[...], count)
    base_out[...] = after
    parts = [codes[part] for part in range(3)]
    coefs_out[...], mine_out[...], pick_out[...] = plan(
        after[:, :1], count, parts, line, linear, slots
    )


def finish(coefs, x, u0, u1, u2, u3, out, held):
    gather((u0, u1, u2, u3), held)
    tokens, width = x.shape
    third = coefs.shape[0] // 3
    known = jnp.concatenate([coefs[pl.ds(i * third, tokens)] for i in range(3)], axis=0)
    for start in range(0, width, STRIP):
        span = pl.ds(start, STRIP)
        out[0, :, span] = (x[:, span].astype(F32) + changes(known, held, span)).astype(BF16)


def expert_kernel(near, far, gate, up, down, near_out, far_out):
    half, width = near_out.shape
    gate_val = up_val = 0.0
    for start in range(0, width, STRIP):
        span = pl.ds(start, STRIP)
        both = [near[:, span], far[:, span]]
        if half % 16:
            rows = jnp.concatenate([r.astype(F32) for r in both], axis=0).astype(BF16)
        else:
            rows = jnp.concatenate(both, axis=0)
        gate_val += jnp.dot(rows, gate[0, span], preferred_element_type=F32)
        up_val += jnp.dot(rows, up[0, span], preferred_element_type=F32)
    hidden = (gate_val * jax.nn.sigmoid(gate_val) * up_val).astype(BF16)
    for start in range(0, width, STRIP):
        span = pl.ds(start, STRIP)
        value = jnp.dot(hidden, down[0, :, span], preferred_element_type=F32)
        near_out[:, span] = value[:half].astype(BF16)
        far_out[:, span] = value[half:].astype(BF16)


def hold_kernel(*refs):
    count = len(refs) // 2
    inputs, outputs, sems = refs[:count], refs[count : 2 * count], refs[-1]
    copies = [
        pltpu.make_async_copy(inputs[i], outputs[i], sems.at[i]) for i in range(count - 1)
    ]
    for copy in copies:
        copy.start()
    outputs[-1][...] = inputs[-1][...]
    for copy in copies:
        copy.wait()


VMEM = pl.BlockSpec(memory_space=pltpu.VMEM)
HBM = pl.BlockSpec(memory_space=pltpu.HBM)
PARAMS = pltpu.CompilerParams(vmem_limit_bytes=16 * 2**20)


def expert_call(near, far, gate, up, down):
    half = near.shape[0]
    _, width, hidden = gate.shape
    out = jax.ShapeDtypeStruct((half, width), BF16)
    return pl.pallas_call(
        expert_kernel,
        out_shape=(out, out),
        in_specs=[VMEM] * 5,
        out_specs=(VMEM, VMEM),
        compiler_params=PARAMS,
        cost_estimate=pl.CostEstimate(
            flops=12 * half * width * hidden,
            bytes_accessed=6 * width * hidden,
            transcendentals=2 * half * hidden,
        ),
        name="experts",
    )(near, far, gate, up, down)


def hold_weights(rows, *weights, after=()):
    operands = weights + (rows,)
    return pl.pallas_call(
        lambda *refs: hold_kernel(*refs[: len(operands)], *refs[len(operands) + len(after) :]),
        out_shape=tuple(jax.ShapeDtypeStruct(w.shape, w.dtype) for w in operands),
        in_specs=[HBM] * len(weights) + [VMEM] * (1 + len(after)),
        out_specs=(VMEM,) * len(operands),
        scratch_shapes=[pltpu.SemaphoreType.DMA((len(weights),))],
        compiler_params=pltpu.CompilerParams(vmem_limit_bytes=52 * 2**20),
        cost_estimate=pl.CostEstimate(
            flops=0, bytes_accessed=4 * sum(w.size for w in weights), transcendentals=0
        ),
        name="hold_weights",
    )(*operands, *after)


def spread(array):
    return [array] + [swap(array, "section", j) for j in range(1, 4)]


def group_rows(normed, own, order):
    near = jnp.concatenate([own] + [swap(normed, "expert", 2 * k) for k in order])
    return near, swap(near, "expert", 1)


def group_sum(near, far, order, sums):
    other = swap(far, "expert", 1)
    both = (near.astype(F32) + other.astype(F32)).astype(BF16)
    count = both.shape[0] // 4
    parts = {k: both[i * count : (i + 1) * count] for i, k in enumerate((0, *order))}
    total = parts[0].astype(F32)
    for k in sums:
        total = total + swap(parts[k], "expert", 2 * k).astype(F32)
    return total.astype(BF16)


def shards_group(embedded, norm_gain, gate_proj, up_proj, down_proj, expert_ids, route_gates):
    tokens, width = embedded.shape[1:]
    slots = expert_ids.shape[1] * CAP
    picked = slots + 2 * PACK

    def shape(dims, kind=BF16):
        return jax.ShapeDtypeStruct(dims, kind)

    def call(kernel, outs, ins, scratch=(), in_specs=None, out_specs=None):
        return pl.pallas_call(
            kernel,
            out_shape=outs,
            in_specs=in_specs or [VMEM] * len(ins),
            out_specs=out_specs or jax.tree.map(lambda _: VMEM, outs),
            scratch_shapes=scratch,
            compiler_params=PARAMS,
            name=getattr(kernel, "func", kernel).__name__,
        )(*ins)

    x_near = [swap(embedded[0], "section", j) for j in (1, 2)]
    gates = jnp.where(expert_ids[0] < 1, route_gates[0], 0.0).transpose(0, 2, 1)
    parts, picks, picks_relayed, hits = call(
        slot_tables,
        (
            shape((tokens, LANES)),
            shape((SECTIONS - 1, picked, tokens)),
            shape((picked, tokens), F32),
            shape((picked, tokens)),
        ),
        (gates,),
        [pltpu.VMEM((LANES, tokens), F32)],
    )
    tables = [parts] + [swap(parts, "section", j) for j in (1, 2)]
    gain, x = call(
        stage,
        (shape(norm_gain.shape, F32), shape((tokens, width))),
        (parts, norm_gain, embedded),
    )
    relayed = call(
        relay, shape((CAP, width + tokens * LANES)), (tables[1], tables[2], x_near[1], gain)
    )
    down, gain = hold_weights(gain, down_proj, after=(relayed,))
    relayed = swap(relayed, "section", 1)
    y, normed, group, rank, linear = call(
        prepare_first,
        (
            shape((slots, width)),
            shape((PACK, width + LANES)),
            shape((SECTIONS, LANES), F32),
            shape((SECTIONS, LANES), F32),
            shape((tokens + picked, LANES)),
        ),
        (picks, picks_relayed, hits, x, *x_near, relayed, *tables, gain),
        [pltpu.VMEM((2 * PACK, width), F32), pltpu.VMEM((tokens, LANES), F32)],
    )
    gate, up, own = hold_weights(normed, gate_proj, up_proj)

    def rest(normed, own, order, sums):
        near, far = group_rows(normed, own, order)
        near_part, far_part = expert_call(near, far, gate, up, down)
        updates = spread(group_sum(near_part, far_part, order, sums))
        return near, far, tuple(jnp.pad(u, ((0, PACK - u.shape[0]), (0, 0))) for u in updates)

    near, far, updates = rest(normed, own, (1, 3, 2), (3, 1, 2))
    number = pl.BlockSpec(memory_space=pltpu.SMEM)
    planned = (
        shape((6 * tokens, SECTIONS * PACK)),
        shape((6 * PACK, SECTIONS * PACK), F32),
        shape((2 * PACK, slots), F32),
    )
    codes, line, rounds, few_rounds, base, *now = call(
        schedule,
        (
            shape((3, LANES, SECTIONS * PACK), F32),
            shape((1, LANES), F32),
            shape((1,), jnp.int32),
            shape((1,), jnp.int32),
            shape((1, LANES), F32),
            *planned,
        ),
        (near, far, group, rank, linear),
        out_specs=(VMEM, VMEM, number, number) + (VMEM,) * 4,
    )
    held = pltpu.VMEM((SECTIONS * PACK, width), F32)

    def body(count, state):
        done, base, now, x, y, updates = state
        coefs, mine, pick = now
        normed = call(
            next_rows,
            shape((count, width)),
            (mine, pick, y, *updates, gain),
            [held, pltpu.VMEM((2 * PACK, width), F32)],
        )
        base, *now, x, y = call(
            functools.partial(absorb, count),
            (shape(base.shape, F32), *planned, shape((tokens, width)), shape((slots, width))),
            (base, coefs, codes, line, linear, x, y, *updates),
            [held],
        )
        updates = rest(normed, normed, (2, 3, 1), (1, 2, 3))[2]
        return done + 1, base, tuple(now), x, y, updates

    state = (jnp.ones((1,), jnp.int32), base, tuple(now), x, y, updates)
    for count, limit in ((FEW, jnp.maximum(few_rounds, 1)), (PACK, jnp.maximum(rounds, 1))):
        state = lax.while_loop(
            functools.partial(lambda limit, s: s[0][0] < limit[0], limit),
            functools.partial(body, count),
            state,
        )
    _, _, now, x, _, updates = state
    return call(finish, shape(embedded.shape), (now[0], x, *updates), [held])


def solution(mesh):
    placed = (
        P("section", "expert", None),
        P("section", None),
        P("section", None, "expert"),
        P("section", None, "expert"),
        P("section", "expert", None),
        P("section", None, "expert", None),
        P("section", None, "expert", None),
    )
    fits = mesh.shape["expert"] == 8 and mesh.shape["section"] == 4
    return jax.shard_map(
        shards_group if fits else shards_general, mesh=mesh, in_specs=placed, out_specs=P("section", "expert", None), check_vma=False
    )
```
